32 devices in a mesh: sec: 4 (over x, core), tile: 8 (over z, y).
Axes of the slice: x: 2, y: 2, z: 4, core: 2. Of those that a mesh axis runs over, the one named last changes fastest.
Arguments:
- velocity: float32 [3, 96, 16, 128], P(None, 'sec', 'tile'), may hold values from -5 to 8
- prev_tendency: float32 [3, 96, 16, 128], P(None, 'sec', 'tile'), may hold values from -12 to 12
- disk_cells: int32 [4, 8, 256], P('sec', 'tile'), may hold values from 0 to 6144, as said below
- disk_kind: int32 [4, 8, 256], P('sec', 'tile'), may hold values from 0 to 15
- rotor_weights: float32 [16], replicated, may hold values from 0.5 to 2
Outputs:
- velocity_next: float32 [3, 96, 16, 128], P(None, 'sec', 'tile')
- tendency: float32 [3, 96, 16, 128], P(None, 'sec', 'tile')
The draws below stay inside these ranges and needn't reach their ends.
Inputs may be any that keep to these rules, and one draw needn't show every extreme that they name: `disk_cells`: an entry equal to 6144 marks an empty slot; any other entry is a flat index (i * 2 + j) * 128 + k into the device's own block, repeats allowed. Every slot of a device in the first half of the sec indices is empty; some other device has all 256 slots live in every draw.
All inputs are finite; a program needn't handle non-finite values.
Results may differ from the reference program's by a relative error of at most 0.0003.
Values sent between devices are 32-bit elements; how exact they have to be, the bound alone decides.
A program may use at most 64 MiB of HBM per device.

```python
import math
import jax
import jax.numpy as jnp
from jax import lax

XB = 24
YT = 2
NZ = 128
STEPS = 2
DSLOT = 256
KINDS = 16
NX = 96
NY = 16
N_SEC = 4
N_TILE = 8


def draw_velocity(key, part):
    whole_shape = (3, NX, NY, NZ)
    height = (jnp.arange(NZ).astype(jnp.float32) + 0.5) / NZ
    fluctuation = jnp.clip(jax.random.normal(key, whole_shape, jnp.float32), -5.0, 5.0)
    mean_flow = 1.5 * height[None, None, :] + jnp.zeros((NX, 1, 1), jnp.float32)
    return fluctuation.at[0].add(mean_flow)


def draw_disk_cells(key, part):
    cell_count = XB * YT * NZ
    key_cells, key_live, key_tile, key_sec = jax.random.split(key, 4)
    picked = jax.random.randint(key_cells, (N_SEC, N_TILE, DSLOT), 0, cell_count)
    live_count = jax.random.randint(key_live, (N_SEC, N_TILE), DSLOT // 2, DSLOT + 1)
    full_tile = jax.random.randint(key_tile, (), 0, N_TILE)
    full_sec = jax.random.randint(key_sec, (), N_SEC // 2, N_SEC)
    sec_ids = jnp.arange(N_SEC)[:, None]
    tile_ids = jnp.arange(N_TILE)[None, :]
    live_count = jnp.where((sec_ids == full_sec) & (tile_ids == full_tile), DSLOT, live_count)
    live_count = jnp.where(sec_ids < N_SEC // 2, 0, live_count)
    slot_ids = jnp.arange(DSLOT)[None, None, :]
    return jnp.where(slot_ids < live_count[:, :, None], picked, cell_count).astype(jnp.int32)


def set_ends(entries, rng, low, top_value):
    longest = entries.shape.index(max(entries.shape))
    spots = []
    for shift in (0, 1):
        where = [jax.random.randint(jax.random.fold_in(rng, axis), (), 0, length) for axis, length in enumerate(entries.shape)]
        where[longest] = (where[longest] + shift) % entries.shape[longest]
        spots.append(tuple(where))
    return entries.at[spots[0]].set(low).at[spots[1]].set(top_value)


def block_scale(stream_key, shape, cuts, low, top_value):
    level = 1.0
    for axis_at, parts in cuts:
        steps = jax.random.uniform(jax.random.fold_in(jax.random.fold_in(stream_key, 6), axis_at), (parts,), jnp.float32, low / len(cuts), top_value / len(cuts))
        level = level * jnp.repeat(jnp.exp(steps), shape[axis_at] // parts).reshape((-1,) + (1,) * (len(shape) - 1 - axis_at))
    return level


def noise(stream_key, shape, deviation, reach, cuts=(), held_as=jnp.bfloat16):
    values = jax.random.normal(stream_key, shape, jnp.float32) * deviation
    if len(cuts) > 0:
        values = block_scale(stream_key, shape, cuts, -0.22, 0.18) * values
    return jnp.clip(values, min=-reach, max=reach).astype(held_as)


def setup_inputs(seed: int = 0) -> dict:
    streams_of = jax.random.split(jax.random.key(seed), 6)
    velocity = draw_velocity(jax.random.fold_in(streams_of[5], 71), 0)
    prev_tendency = noise(streams_of[1], (3, NX, NY, NZ), 2.0, 12.0, ((1, 4), (2, 8)), jnp.float32)
    disk_cells = draw_disk_cells(jax.random.fold_in(streams_of[5], 71), 0)
    disk_kind = set_ends(jax.random.randint(streams_of[3], (N_SEC, N_TILE, DSLOT), 0, KINDS), jax.random.fold_in(streams_of[3], 1), 0, KINDS - 1).astype(jnp.int32)
    rotor_weights = jnp.clip(jnp.exp(jax.random.uniform(streams_of[4], (KINDS,), jnp.float32, math.log(0.5), math.log(2.0))), 0.5, 2.0)
    return {"velocity": velocity, "prev_tendency": prev_tendency, "disk_cells": disk_cells, "disk_kind": disk_kind, "rotor_weights": rotor_weights}


precise = lax.Precision.HIGHEST
time_step = 0.1
fringe_rate = 2.0
smag_coef = 0.04

def gradients(padded, z_sign):
    centre = padded[:, 1:-1, 1:-1, :]
    grad_x = 0.5 * (padded[:, 2:, 1:-1, :] - padded[:, :-2, 1:-1, :])
    grad_y = 0.5 * (padded[:, 1:-1, 2:, :] - padded[:, 1:-1, :-2, :])
    extended = jnp.concatenate([z_sign * centre[..., :1], centre, z_sign * centre[..., -1:]], axis=-1)
    grad_z = 0.5 * (extended[..., 2:] - extended[..., :-2])
    return (grad_x, grad_y, grad_z)

def strain_stress(slopes):

    def strain(first, second):
        return 0.5 * (slopes[second][first] + slopes[first][second])
    strain_xx = strain(0, 0)
    strain_yy = strain(1, 1)
    strain_zz = strain(2, 2)
    strain_xy = strain(0, 1)
    strain_xz = strain(0, 2)
    strain_yz = strain(1, 2)
    squared = strain_xx * strain_xx + strain_yy * strain_yy + strain_zz * strain_zz
    squared = squared + 2.0 * (strain_xy * strain_xy + strain_xz * strain_xz + strain_yz * strain_yz)
    double = 2.0 * (smag_coef * jnp.sqrt(2.0 * squared + 0.01))
    return jnp.stack([double * strain_xx, double * strain_yy, double * strain_zz, double * strain_xy, double * strain_xz, double * strain_yz])

def advection(slopes, centre):
    return centre[0:1] * slopes[0] + centre[1:2] * slopes[1] + centre[2:3] * slopes[2]

def stress_force(padded):
    grad_x, grad_y, grad_z = gradients(padded, 0.0)
    return jnp.stack([grad_x[0] + grad_y[3] + grad_z[4], grad_x[3] + grad_y[1] + grad_z[5], grad_x[4] + grad_y[5] + grad_z[2]])

def wrap_pad(source):
    return jnp.pad(source, ((0, 0), (1, 1), (1, 1), (0, 0)), mode='wrap')

def hartley(source, axis):
    spectrum = jnp.fft.fft(source, axis=axis)
    return spectrum.real - spectrum.imag

def cosine_table():
    modes = jnp.arange(NZ).astype(jnp.float32)[:, None]
    points = jnp.arange(NZ).astype(jnp.float32)[None, :] + 0.5
    return jnp.cos(math.pi * modes * points / NZ)

def spectral_inverse():
    mode_x = jnp.arange(NX)
    mode_y = jnp.arange(NY)
    mode_z = jnp.arange(NZ)
    sin_x = jnp.sin(2.0 * math.pi * mode_x.astype(jnp.float32) / NX)
    sin_y = jnp.sin(2.0 * math.pi * mode_y.astype(jnp.float32) / NY)
    sin_z = jnp.sin(math.pi * mode_z.astype(jnp.float32) / NZ)
    eigen = -((sin_x * sin_x)[:, None, None] + (sin_y * sin_y)[None, :, None] + (sin_z * sin_z)[None, None, :])
    zero_mode = (mode_x % (NX // 2) == 0)[:, None, None] & (mode_y % (NY // 2) == 0)[None, :, None] & (mode_z == 0)[None, None, :]
    return jnp.where(zero_mode, 0.0, 1.0 / jnp.where(zero_mode, 1.0, eigen))

def solve_pressure(rhs, cos_tab, weights, recip):
    coeffs = jnp.einsum('xyz,mz->xym', rhs, cos_tab, precision=precise)
    coeffs = hartley(hartley(coeffs, 0), 1)
    coeffs = coeffs * recip
    coeffs = hartley(hartley(coeffs, 1), 0) / (NX * NY)
    return jnp.einsum('xym,mz->xyz', coeffs * weights[None, None, :], cos_tab, precision=precise)

def turbine_push(axial, disk_cells, disk_kind, rotor_weights):
    cell_count = XB * YT * NZ
    blocks = axial.reshape(N_SEC, XB, N_TILE, YT, NZ).transpose(0, 2, 1, 3, 4).reshape(N_SEC * N_TILE, cell_count)
    picked = disk_cells.reshape(N_SEC * N_TILE, DSLOT)
    kinds = disk_kind.reshape(N_SEC * N_TILE, DSLOT)
    live = picked < cell_count
    safe = jnp.minimum(picked, cell_count - 1).astype(jnp.int32)
    sampled = jnp.take_along_axis(blocks, safe, axis=1)
    weight = rotor_weights[kinds]
    push = jnp.where(live, -(weight * sampled * jnp.abs(sampled)), 0.0)
    row_ids = jnp.arange(N_SEC * N_TILE).astype(jnp.int32)[:, None]
    summed = jnp.zeros_like(blocks).at[row_ids, safe].add(push)
    return summed.reshape(N_SEC, N_TILE, XB, YT, NZ).transpose(0, 2, 1, 3, 4).reshape(NX, NY, NZ)

def reference(velocity, prev_tendency, disk_cells, disk_kind, rotor_weights):
    cos_tab = cosine_table()
    weights = jnp.where(jnp.arange(NZ) == 0, 1.0 / NZ, 2.0 / NZ).astype(jnp.float32)
    recip = spectral_inverse()
    root_slab = N_SEC // 2 - 1
    slab_pos = jnp.sin(math.pi * (jnp.arange(XB).astype(jnp.float32) + 0.5) / XB)
    lam_x = fringe_rate * (slab_pos * slab_pos)
    sec_ids = jnp.arange(N_SEC)
    flags = ((sec_ids == 0) | (sec_ids == N_SEC // 2) | (sec_ids == 3 * N_SEC // 4) | (sec_ids == N_SEC - 1)).astype(jnp.float32)
    current = velocity
    tendency_old = prev_tendency
    tendency = prev_tendency
    for step_no in range(STEPS):
        slopes = gradients(wrap_pad(current), -1.0)
        stress = strain_stress(slopes)
        advect = advection(slopes, current)
        push_field = stress_force(wrap_pad(stress))
        blocks = current.reshape(3, N_SEC, XB, NY, NZ)
        target = blocks[:, root_slab]
        fringe = flags[None, :, None, None, None] * lam_x[None, None, :, None, None] * (target[:, None] - blocks)
        fringe = fringe.reshape(current.shape)
        turbine = turbine_push(current[0], disk_cells, disk_kind, rotor_weights)
        empty = jnp.zeros_like(turbine)
        tendency = push_field - advect + jnp.stack([turbine, empty, empty]) + fringe
        interim = current + time_step * (1.5 * tendency - 0.5 * tendency_old)
        grad_x, grad_y, grad_z = gradients(wrap_pad(interim), -1.0)
        rhs = grad_x[0] + grad_y[1] + grad_z[2]
        pressure = solve_pressure(rhs, cos_tab, weights, recip)
        press_x, press_y, press_z = gradients(wrap_pad(pressure[None]), 1.0)
        current = interim - jnp.concatenate([press_x, press_y, press_z], axis=0)
        tendency_old = tendency
    return (current, tendency)
```

```python
import functools
import math

import jax
import jax.numpy as jnp
import numpy as np
from jax import lax
from jax.experimental import pallas as pl
from jax.experimental.pallas import tpu as pltpu
from jax.sharding import PartitionSpec as P

STEPS = 2
KINDS = 16
ROWS = 8
LANES = 128
MESH = pl.DeviceIdType.MESH

precise = lax.Precision.HIGHEST
time_step = 0.1
fringe_rate = 2.0
smag_coef = 0.04


def extended_2(block, sides, width):
    for axis, dim in sides:
        count = lax.axis_size(axis)
        forward = [(i, i + 1) for i in range(count - 1)]
        forward.append((count - 1, 0))
        backward = [(target, source) for source, target in forward]
        low = lax.ppermute(
            lax.slice_in_dim(block, block.shape[dim] - width, None, axis=dim), axis, forward
        )
        high = lax.ppermute(lax.slice_in_dim(block, 0, width, axis=dim), axis, backward)
        block = jnp.concatenate([low, block, high], axis=dim)
    return block


def from_root(block, axis, owner):
    block = jnp.where(lax.axis_index(axis) == owner, block, jnp.zeros_like(block))
    return lax.psum(block, axis)


def gradients(padded, z_sign):
    centre = padded[:, 1:-1, 1:-1, :]
    grad_x = 0.5 * (padded[:, 2:, 1:-1, :] - padded[:, :-2, 1:-1, :])
    grad_y = 0.5 * (padded[:, 1:-1, 2:, :] - padded[:, 1:-1, :-2, :])
    extended = jnp.concatenate(
        [z_sign * centre[..., :1], centre, z_sign * centre[..., -1:]], axis=-1
    )
    grad_z = 0.5 * (extended[..., 2:] - extended[..., :-2])
    return (grad_x, grad_y, grad_z)


def strain_stress(slopes):

    def strain(first, second):
        return 0.5 * (slopes[second][first] + slopes[first][second])

    strain_xx = strain(0, 0)
    strain_yy = strain(1, 1)
    strain_zz = strain(2, 2)
    strain_xy = strain(0, 1)
    strain_xz = strain(0, 2)
    strain_yz = strain(1, 2)
    squared = strain_xx * strain_xx + strain_yy * strain_yy + strain_zz * strain_zz
    squared = squared + 2.0 * (
        strain_xy * strain_xy + strain_xz * strain_xz + strain_yz * strain_yz
    )
    double = 2.0 * (smag_coef * jnp.sqrt(2.0 * squared + 0.01))
    return jnp.stack(
        [
            double * strain_xx,
            double * strain_yy,
            double * strain_zz,
            double * strain_xy,
            double * strain_xz,
            double * strain_yz,
        ]
    )


def advection(slopes, centre):
    return centre[0:1] * slopes[0] + centre[1:2] * slopes[1] + centre[2:3] * slopes[2]


def stress_force(padded):
    grad_x, grad_y, grad_z = gradients(padded, 0.0)
    return jnp.stack(
        [
            grad_x[0] + grad_y[3] + grad_z[4],
            grad_x[3] + grad_y[1] + grad_z[5],
            grad_x[4] + grad_y[5] + grad_z[2],
        ]
    )


def faces(source):
    return extended_2(source, (("sec", 1), ("tile", 2)), 1)


def sec_turn(blocks):
    return lax.all_to_all(blocks, "sec", split_axis=0, concat_axis=0, tiled=True)


def tile_turn(blocks):
    return lax.all_to_all(blocks, "tile", split_axis=0, concat_axis=0, tiled=True)


def hartley_table(length):
    index_row = jnp.arange(length)
    product = index_row[:, None] * index_row[None, :] % length
    angle = 2.0 * math.pi / length * product.astype(jnp.float32)
    return jnp.cos(angle) + jnp.sin(angle)


def local(velocity, prev_tendency, disk_cells, disk_kind, rotor_weights):
    sec_count = lax.axis_size("sec")
    tile_count = lax.axis_size("tile")
    sec_at = lax.axis_index("sec")
    tile_at = lax.axis_index("tile")
    slab_x = velocity.shape[1]
    tile_y = velocity.shape[2]
    depth_z = velocity.shape[3]
    full_x = slab_x * sec_count
    full_y = tile_y * tile_count
    part_z = depth_z // sec_count
    modes_each = slab_x * depth_z // tile_count
    cell_count = slab_x * tile_y * depth_z
    modes = jnp.arange(depth_z).astype(jnp.float32)[:, None]
    points = jnp.arange(depth_z).astype(jnp.float32)[None, :] + 0.5
    cos_blocks = jnp.cos(math.pi * modes * points / depth_z).reshape(sec_count, part_z, depth_z)
    weight_blocks = jnp.where(jnp.arange(depth_z) == 0, 1.0 / depth_z, 2.0 / depth_z).astype(
        jnp.float32
    )
    weight_blocks = weight_blocks.reshape(sec_count, part_z)
    x_table = hartley_table(full_x)
    y_table = hartley_table(full_y).reshape(full_y, tile_count, tile_y)
    flat_ids = tile_at * modes_each + jnp.arange(modes_each)
    mode_x = flat_ids // part_z
    mode_z = sec_at * part_z + flat_ids % part_z
    mode_y = jnp.arange(full_y)
    sin_x = jnp.sin(2.0 * math.pi * mode_x.astype(jnp.float32) / full_x)
    sin_y = jnp.sin(2.0 * math.pi * mode_y.astype(jnp.float32) / full_y)
    sin_z = jnp.sin(math.pi * mode_z.astype(jnp.float32) / depth_z)
    eigen = -((sin_x * sin_x)[:, None] + (sin_y * sin_y)[None, :] + (sin_z * sin_z)[:, None])
    zero_mode = (
        (mode_x % (full_x // 2) == 0)[:, None]
        & (mode_y % (full_y // 2) == 0)[None, :]
        & (mode_z == 0)[:, None]
    )
    recip = jnp.where(zero_mode, 0.0, 1.0 / jnp.where(zero_mode, 1.0, eigen))
    slab_pos = jnp.sin(math.pi * (jnp.arange(slab_x).astype(jnp.float32) + 0.5) / slab_x)
    lam_x = fringe_rate * (slab_pos * slab_pos)
    flag = (
        (sec_at == 0)
        | (sec_at == sec_count // 2)
        | (sec_at == 3 * sec_count // 4)
        | (sec_at == sec_count - 1)
    ).astype(jnp.float32)
    picked = disk_cells.reshape(-1)
    kinds = disk_kind.reshape(-1)
    live = picked < cell_count
    safe = jnp.minimum(picked, cell_count - 1)
    weight = jnp.sum(
        jnp.where(kinds[:, None] == jnp.arange(KINDS)[None, :], rotor_weights[None, :], 0.0), axis=1
    )
    current = velocity
    tendency_old = prev_tendency
    tendency = prev_tendency
    for step_no in range(STEPS):
        wide = extended_2(current, (("sec", 1), ("tile", 2)), 2)
        wide_slopes = gradients(wide, -1.0)
        push_field = stress_force(strain_stress(wide_slopes))
        slopes = tuple((piece[:, 1:-1, 1:-1, :] for piece in wide_slopes))
        advect = advection(slopes, current)
        target = from_root(current, "sec", sec_count // 2 - 1)
        fringe = flag * lam_x[None, :, None, None] * (target - current)
        sampled = current[0].reshape(-1)[safe]
        push = jnp.where(live, -(weight * sampled * jnp.abs(sampled)), 0.0)
        turbine = (
            jnp.zeros((cell_count,), jnp.float32)
            .at[safe]
            .add(push)
            .reshape(slab_x, tile_y, depth_z)
        )
        empty = jnp.zeros_like(turbine)
        tendency = push_field - advect + jnp.stack([turbine, empty, empty]) + fringe
        interim = current + time_step * (1.5 * tendency - 0.5 * tendency_old)
        grad_x, grad_y, grad_z = gradients(faces(interim), -1.0)
        rhs = grad_x[0] + grad_y[1] + grad_z[2]
        coeffs = jnp.einsum("xyz,bcz->bxyc", rhs, cos_blocks, precision=precise)
        gathered = sec_turn(coeffs).reshape(full_x, tile_y, part_z)
        along_x = jnp.einsum("xyc,kx->kcy", gathered, x_table, precision=precise)
        spread = tile_turn(along_x.reshape(tile_count, modes_each, tile_y))
        along_y = jnp.einsum("sqt,lst->ql", spread, y_table, precision=precise)
        scaled = along_y * recip
        back_y = jnp.einsum("ql,lst->sqt", scaled, y_table, precision=precise) / (full_x * full_y)
        returned = tile_turn(back_y).reshape(full_x, part_z, tile_y)
        back_x = jnp.einsum("kcy,kx->xyc", returned, x_table, precision=precise)
        home = sec_turn(back_x.reshape(sec_count, slab_x, tile_y, part_z))
        pressure = jnp.einsum(
            "bxyc,bcz->xyz", home * weight_blocks[:, None, None, :], cos_blocks, precision=precise
        )
        press_x, press_y, press_z = gradients(faces(pressure[None]), 1.0)
        current = interim - jnp.concatenate([press_x, press_y, press_z], axis=0)
        tendency_old = tendency
    return (current, tendency)


def cas_table(first, second, length):
    angle = 2.0 * np.pi / length * (np.outer(first, second) % length)
    return np.cos(angle) + np.sin(angle)


def halves(table):
    high = table.astype(np.float32).astype(jnp.bfloat16)
    low = (table - high.astype(np.float64)).astype(np.float32).astype(jnp.bfloat16)
    return np.stack([high, low])


def tables(sec_count, tile_count, slab_x, tile_y, depth_z):
    full_x, full_y = slab_x * sec_count, tile_y * tile_count
    wide_x = -(-full_x // LANES) * LANES
    planes = tile_y + 2
    z_at = np.arange(depth_z)
    cos_z = np.cos(np.pi / depth_z * np.outer(z_at, z_at + 0.5))
    x_cas = np.zeros((sec_count, LANES, planes * wide_x))
    for sec in range(sec_count):
        start = sec * slab_x
        for plane in range(planes):
            x_cas[sec, plane * slab_x : (plane + 1) * slab_x, plane * wide_x : plane * wide_x + full_x] = (
                cas_table(start + np.arange(slab_x), np.arange(full_x), full_x)
            )
        for row in range(tile_y):
            for side, x_at in ((0, start - 1), (1, start + slab_x)):
                x_cas[
                    sec,
                    planes * slab_x + side * tile_y + row,
                    (row + 1) * wide_x : (row + 1) * wide_x + full_x,
                ] = cas_table(np.array([x_at % full_x]), np.arange(full_x), full_x)[0]
    y_blocks = []
    for plane in range(planes):
        y_at = (np.arange(tile_count) * tile_y + plane - 1) % full_y
        y_blocks.append(np.kron(cas_table(np.arange(full_y), y_at, full_y), np.eye(ROWS)))
    y_cas = np.concatenate(y_blocks, axis=1)
    k_x, k_y = np.arange(full_x), np.arange(full_y)
    sin_x = np.where(k_x % (full_x // 2) == 0, 0.0, np.sin(2.0 * np.pi * k_x / full_x) ** 2)
    sin_y = np.where(k_y % (full_y // 2) == 0, 0.0, np.sin(2.0 * np.pi * k_y / full_y) ** 2)
    sin_xy = np.ones((full_y * ROWS, wide_x), np.float32)
    sin_xy[:, :full_x] = np.repeat(sin_y, ROWS)[:, None] + sin_x[None, :]
    sin_z = np.sin(np.pi * z_at / depth_z) ** 2
    weight_z = -np.where(z_at == 0, 1.0, 2.0) / (depth_z * full_x * full_y)
    mode_z = np.stack([sin_z, weight_z]).astype(np.float32)
    mode_z = np.ascontiguousarray(np.broadcast_to(mode_z[:, :, None], (2, depth_z, wide_x)))
    lam = fringe_rate * np.sin(np.pi * (np.arange(slab_x) + 0.5) / slab_x) ** 2
    lam = np.ascontiguousarray(np.broadcast_to(lam.astype(np.float32)[:, None], (slab_x, depth_z)))
    return halves(cos_z), halves(x_cas), halves(y_cas), halves(y_cas.T), sin_xy, mode_z, lam


def split(value):
    high = value.astype(jnp.bfloat16)
    return high, (value - high.astype(jnp.float32)).astype(jnp.bfloat16)


def dot3(first, second, dims):
    def dot(one, two):
        return lax.dot_general(one, two, (dims, ((), ())), preferred_element_type=jnp.float32)

    return dot(first[0], second[0]) + (dot(first[0], second[1]) + dot(first[1], second[0]))


NN = ((1,), (0,))
NT = ((1,), (1,))


def slope_z(value, z_sign):
    depth = value.shape[1]
    lane = lax.broadcasted_iota(jnp.int32, value.shape, 1)
    edge = value * z_sign
    above = jnp.where(lane == depth - 1, edge, pltpu.roll(value, depth - 1, 1))
    below = jnp.where(lane == 0, edge, pltpu.roll(value, 1, 1))
    return 0.5 * (above - below)


def slope_x(value, low=None, high=None):
    count = value.shape[0]
    after = pltpu.roll(value, count - 1, 0)
    before = pltpu.roll(value, 1, 0)
    if low is not None:
        row = lax.broadcasted_iota(jnp.int32, value.shape, 0)
        after = jnp.where(row == count - 1, high, after)
        before = jnp.where(row == 0, low, before)
    return 0.5 * (after - before)


def step_kernel(
    sec_count,
    tile_count,
    slab_x,
    tile_y,
    depth_z,
    vel_ref,
    old_ref,
    cells_ref,
    kinds_ref,
    weights_ref,
    cos_ref,
    x_ref,
    y_ref,
    yt_ref,
    sin_xy_ref,
    mode_z_ref,
    lam_ref,
    vel_out,
    tend_out,
    wide,
    target,
    share,
    coeffs,
    plane_in,
    plane_out,
    returned,
    press,
    thrust,
    recip,
    halo_send,
    halo_recv,
    target_send,
    target_recv,
    mode_send,
    mode_recv,
    back_send,
    back_recv,
):
    sec = lax.axis_index("sec")
    tile = lax.axis_index("tile")
    devices = sec_count * tile_count
    me = tile * sec_count + sec
    owners = depth_z // ROWS
    spacing = devices // owners
    planes = tile_y + 2
    deep = tile_y + 4
    wide_x = sin_xy_ref.shape[1]
    group = tile_count * ROWS
    root = sec_count // 2 - 1
    fringes = sorted({0, sec_count // 2, 3 * sec_count // 4, sec_count - 1} - {root})
    is_owner = lax.rem(me, spacing) == 0
    owner_at = lax.div(me, spacing)
    in_fringe = functools.reduce(jnp.logical_or, [sec == which for which in fringes])
    low_sec, high_sec = lax.rem(sec + sec_count - 1, sec_count), lax.rem(sec + 1, sec_count)
    low_tile, high_tile = lax.rem(tile + tile_count - 1, tile_count), lax.rem(tile + 1, tile_count)
    end_x = ROWS + slab_x
    own_x, own_y = slice(ROWS, end_x), slice(2, 2 + tile_y)

    barrier = pltpu.get_barrier_semaphore()

    def greet(ahead, carry):
        other = lax.rem(me + ahead, devices)
        pl.semaphore_signal(
            barrier,
            inc=1,
            device_id=(lax.rem(other, sec_count), lax.div(other, sec_count)),
            device_id_type=MESH,
        )
        return carry

    lax.fori_loop(1, devices, greet, 0)

    for part in range(3):
        for row in range(tile_y):
            wide[0, part, 2 + row, own_x, :] = vel_ref[part, pl.ds(row, slab_x, stride=tile_y), :]
    share[...] = jnp.zeros_like(share)

    pl.semaphore_wait(barrier, devices - 1)

    def start_halo(step):
        xs = {
            -1: (low_sec, slice(ROWS, 2 * ROWS), slice(end_x, end_x + ROWS)),
            0: (sec, own_x, own_x),
            1: (high_sec, slice(end_x - ROWS, end_x), slice(0, ROWS)),
        }
        ys = {
            -1: (low_tile, slice(2, 4), slice(2 + tile_y, deep)),
            0: (tile, own_y, own_y),
            1: (high_tile, slice(tile_y, 2 + tile_y), slice(0, 2)),
        }
        copies = []
        for x_way in (-1, 0, 1):
            for y_way in (-1, 0, 1):
                if x_way == 0 and y_way == 0:
                    continue
                slot = len(copies)
                to_sec, x_from, x_to = xs[x_way]
                to_tile, y_from, y_to = ys[y_way]
                copy = pltpu.make_async_remote_copy(
                    src_ref=wide.at[step, :, y_from, x_from, :],
                    dst_ref=wide.at[step, :, y_to, x_to, :],
                    send_sem=halo_send.at[step, slot],
                    recv_sem=halo_recv.at[step, slot],
                    device_id=(to_sec, to_tile),
                    device_id_type=MESH,
                )
                copies.append(copy)
        sends = [
            pltpu.make_async_remote_copy(
                src_ref=wide.at[step, :, own_y, own_x, :],
                dst_ref=target.at[step],
                send_sem=target_send.at[step, place],
                recv_sem=target_recv.at[step],
                device_id=(which, tile),
                device_id_type=MESH,
            )
            for place, which in enumerate(fringes)
        ]

        @pl.when(sec == root)
        def _():
            for send in sends:
                send.start()

        for copy in copies:
            copy.start()
        return copies, sends

    halo = start_halo(0)
    pending = [halo]

    cells = cells_ref[...]
    kinds = kinds_ref[...]
    weight = jnp.zeros(cells.shape, jnp.float32)
    for kind in range(KINDS):
        weight = jnp.where(kinds == kind, weights_ref[kind], weight)
    weight = jnp.where(cells < slab_x * tile_y * depth_z, weight, 0.0)
    column = lax.div(cells, depth_z)
    row_of = lax.rem(column, tile_y) * slab_x + lax.div(column, tile_y)
    slots = cells.shape[1]
    hit_row = lax.broadcasted_iota(jnp.int32, (tile_y * slab_x, slots), 0) == row_of
    hit_z = lax.broadcasted_iota(jnp.int32, (depth_z, slots), 0) == lax.rem(cells, depth_z)
    hit_z = hit_z.astype(jnp.float32).astype(jnp.bfloat16)
    rest = jnp.where(hit_row, weight, 0.0)
    summed = jnp.zeros((tile_y * slab_x, depth_z), jnp.float32)
    for _ in range(3):
        piece, rest_next = rest.astype(jnp.bfloat16), None
        rest_next = rest - piece.astype(jnp.float32)
        summed = summed + lax.dot_general(
            piece, hit_z, (NT, ((), ())), preferred_element_type=jnp.float32
        )
        rest = rest_next
    thrust[...] = summed

    @pl.when(is_owner)
    def _():
        rows = pl.ds(pl.multiple_of(owner_at * ROWS, ROWS), ROWS)
        full_y = tile_y * tile_count
        sum_sin = sin_xy_ref[...] + jnp.concatenate([mode_z_ref[0, rows, :]] * full_y, axis=0)
        scale = jnp.concatenate([mode_z_ref[1, rows, :]] * full_y, axis=0)
        zero_mode = sum_sin == 0.0
        recip[...] = jnp.where(zero_mode, 0.0, scale / jnp.where(zero_mode, 1.0, sum_sin))

    cos_z = (cos_ref[0], cos_ref[1])
    old = [
        [old_ref[part, pl.ds(row, slab_x, stride=tile_y), :] for row in range(tile_y)]
        for part in range(3)
    ]

    for step in range(STEPS):
        copies, sends = halo

        @pl.when(in_fringe)
        def _(step=step):
            pltpu.make_async_copy(target.at[step], target.at[step], target_recv.at[step]).wait()

        @pl.when(jnp.logical_not(in_fringe))
        def _(step=step):
            target[step] = wide[step, :, own_y, own_x, :]

        for copy in copies:
            copy.wait_recv()

        centre, stress, advect = {}, {}, {}
        for plane in range(1, deep - 1):
            here = [wide[step, part, plane] for part in range(3)]
            d_x = [slope_x(value) for value in here]
            d_y = [
                0.5 * (wide[step, part, plane + 1] - wide[step, part, plane - 1])
                for part in range(3)
            ]
            d_z = [slope_z(value, -1.0) for value in here]
            s_xx, s_yy, s_zz = d_x[0], d_y[1], d_z[2]
            s_xy = 0.5 * (d_x[1] + d_y[0])
            s_xz = 0.5 * (d_x[2] + d_z[0])
            s_yz = 0.5 * (d_y[2] + d_z[1])
            squared = s_xx * s_xx + s_yy * s_yy + s_zz * s_zz
            squared = squared + 2.0 * (s_xy * s_xy + s_xz * s_xz + s_yz * s_yz)
            double = (2.0 * smag_coef) * jnp.sqrt(2.0 * squared + 0.01)
            stress[plane] = [double * s for s in (s_xx, s_yy, s_zz, s_xy, s_xz, s_yz)]
            centre[plane] = here
            advect[plane] = [
                here[0] * d_x[part] + here[1] * d_y[part] + here[2] * d_z[part]
                for part in range(3)
            ]
        interim, tendency = [], []
        for row in range(tile_y):
            plane = 2 + row
            xx, yy, zz, xy, xz, yz = stress[plane]
            before, after = stress[plane - 1], stress[plane + 1]
            push = [
                slope_x(xx) + 0.5 * (after[3] - before[3]) + slope_z(xz, 0.0),
                slope_x(xy) + 0.5 * (after[1] - before[1]) + slope_z(yz, 0.0),
                slope_x(xz) + 0.5 * (after[5] - before[5]) + slope_z(zz, 0.0),
            ]
            lam = lam_ref[...]
            tend, mid = [], []
            for part in range(3):
                here = centre[plane][part][own_x]
                total = (push[part] - advect[plane][part])[own_x]
                if part == 0:
                    force = thrust[row * slab_x : (row + 1) * slab_x, :]
                    total = total - force * here * jnp.abs(here)
                total = total + lam * (target[step, part, row] - here)
                tend.append(total)
                mid.append(here + time_step * (1.5 * total - 0.5 * old[part][row]))
                if step == STEPS - 1:
                    tend_out[part, pl.ds(row, slab_x, stride=tile_y), :] = total
            tendency.append(tend)
            interim.append(mid)
        old = [[tendency[row][part] for row in range(tile_y)] for part in range(3)]

        share[0:slab_x, :] = 0.5 * interim[0][1]
        share[(planes - 1) * slab_x : planes * slab_x, :] = -0.5 * interim[tile_y - 1][1]
        for row in range(tile_y):
            along_x, _, along_z = interim[row]
            total = slope_x(along_x, 0.0, 0.0) + slope_z(along_z, -1.0)
            if row + 1 < tile_y:
                total = total + 0.5 * interim[row + 1][1]
            if row > 0:
                total = total - 0.5 * interim[row - 1][1]
            share[(row + 1) * slab_x : (row + 2) * slab_x, :] = total
            edge = planes * slab_x + row
            share[edge : edge + 1, :] = 0.5 * along_x[0:1]
            share[edge + tile_y : edge + tile_y + 1, :] = -0.5 * along_x[slab_x - 1 : slab_x]
        coeffs[step] = dot3(cos_z, split(share[...]), NT)

        my_rows = pl.ds(pl.multiple_of(tile * ROWS, ROWS), ROWS)

        def send_modes(ahead, carry, step=step):
            owner = lax.rem(owner_at + ahead, owners)
            flat = owner * spacing
            rows = pl.ds(pl.multiple_of(owner * ROWS, ROWS), ROWS)

            @pl.when(flat == me)
            def _():
                pltpu.make_async_copy(
                    coeffs.at[step, rows, :], plane_in.at[step, sec, my_rows, :], mode_recv.at[step]
                ).start()

            @pl.when(flat != me)
            def _():
                pltpu.make_async_remote_copy(
                    src_ref=coeffs.at[step, rows, :],
                    dst_ref=plane_in.at[step, sec, my_rows, :],
                    send_sem=mode_send.at[step],
                    recv_sem=mode_recv.at[step],
                    device_id=(lax.rem(flat, sec_count), lax.div(flat, sec_count)),
                    device_id_type=MESH,
                ).start()

            return carry

        lax.fori_loop(0, owners, send_modes, 0)

        @pl.when(is_owner)
        def _(step=step):
            pltpu.make_async_copy(
                plane_in.at[step], plane_in.at[step], mode_recv.at[step]
            ).wait()
            along_x = jnp.zeros((group, planes * wide_x), jnp.float32)
            for part in range(sec_count):
                along_x = along_x + dot3(
                    split(plane_in[step, part]), (x_ref[0, part], x_ref[1, part]), NN
                )
            stacked = jnp.concatenate(
                [along_x[:, i * wide_x : (i + 1) * wide_x] for i in range(planes)], axis=0
            )
            modes = dot3((y_ref[0], y_ref[1]), split(stacked), NN) * recip[...]
            back_y = dot3((yt_ref[0], yt_ref[1]), split(modes), NN)
            flat_y = split(
                jnp.concatenate([back_y[i * group : (i + 1) * group] for i in range(planes)], axis=1)
            )
            for part in range(sec_count):
                plane_out[step, part] = dot3(flat_y, (x_ref[0, part], x_ref[1, part]), NT)
            rows = pl.ds(pl.multiple_of(owner_at * ROWS, ROWS), ROWS)

            pltpu.make_async_copy(
                plane_out.at[step, sec, my_rows, :], returned.at[step, rows, :], back_recv.at[step]
            ).start()

            def send_back(ahead, carry):
                other = lax.rem(me + ahead, devices)
                to_sec, to_tile = lax.rem(other, sec_count), lax.div(other, sec_count)
                pltpu.make_async_remote_copy(
                    src_ref=plane_out.at[
                        step, to_sec, pl.ds(pl.multiple_of(to_tile * ROWS, ROWS), ROWS), :
                    ],
                    dst_ref=returned.at[step, rows, :],
                    send_sem=back_send.at[step],
                    recv_sem=back_recv.at[step],
                    device_id=(to_sec, to_tile),
                    device_id_type=MESH,
                ).start()
                return carry

            lax.fori_loop(1, devices, send_back, 0)

        pltpu.make_async_copy(returned.at[step], returned.at[step], back_recv.at[step]).wait()
        press[...] = dot3(split(returned[step].T), cos_z, NN)
        for row in range(tile_y):
            here = press[(row + 1) * slab_x : (row + 2) * slab_x, :]
            edge = planes * slab_x + row
            slopes = [
                slope_x(here, press[edge : edge + 1, :], press[edge + tile_y : edge + tile_y + 1, :]),
                0.5
                * (
                    press[(row + 2) * slab_x : (row + 3) * slab_x, :]
                    - press[row * slab_x : (row + 1) * slab_x, :]
                ),
                slope_z(here, 1.0),
            ]
            for part in range(3):
                value = interim[row][part] - slopes[part]
                if step == STEPS - 1:
                    vel_out[part, pl.ds(row, slab_x, stride=tile_y), :] = value
                else:
                    wide[step + 1, part, 2 + row, own_x, :] = value
        if step < STEPS - 1:
            halo = start_halo(step + 1)
            pending.append(halo)

    for step, (copies, sends) in enumerate(pending):
        for copy in copies:
            copy.wait_send()

        @pl.when(sec == root)
        def _(sends=sends):
            for send in sends:
                send.wait_send()

        @pl.when(is_owner)
        def _(step=step):
            most = coeffs.at[step, pl.ds(0, (owners - 1) * ROWS), :]
            pltpu.make_async_copy(most, most, mode_send.at[step]).wait()
            some = plane_out.at[step, pl.ds(0, sec_count - 1)]
            pltpu.make_async_copy(some, some, back_send.at[step]).wait()
            last = plane_out.at[step, sec_count - 1, pl.ds(0, group - ROWS), :]
            pltpu.make_async_copy(last, last, back_send.at[step]).wait()

        @pl.when(jnp.logical_not(is_owner))
        def _(step=step):
            pltpu.make_async_copy(coeffs.at[step], coeffs.at[step], mode_send.at[step]).wait()


def direct(sec_count, tile_count, velocity, prev_tendency, disk_cells, disk_kind, rotor_weights):
    _, slab_x, tile_y, depth_z = velocity.shape
    constants = [
        jnp.asarray(table) for table in tables(sec_count, tile_count, slab_x, tile_y, depth_z)
    ]
    wide_x = constants[4].shape[1]
    full_y = tile_y * tile_count
    group = tile_count * ROWS
    flat = (3, slab_x * tile_y, depth_z)
    vmem = pl.BlockSpec(memory_space=pltpu.VMEM)
    smem = pl.BlockSpec(memory_space=pltpu.SMEM)
    dma = pltpu.SemaphoreType.DMA
    outs = pl.pallas_call(
        functools.partial(step_kernel, sec_count, tile_count, slab_x, tile_y, depth_z),
        out_shape=[jax.ShapeDtypeStruct(flat, jnp.float32)] * 2,
        in_specs=[vmem] * 4 + [smem] + [vmem] * len(constants),
        out_specs=[vmem] * 2,
        scratch_shapes=[
            pltpu.VMEM((STEPS, 3, tile_y + 4, slab_x + 2 * ROWS, depth_z), jnp.float32),
            pltpu.VMEM((STEPS, 3, tile_y, slab_x, depth_z), jnp.float32),
            pltpu.VMEM((LANES, depth_z), jnp.float32),
            pltpu.VMEM((STEPS, depth_z, LANES), jnp.float32),
            pltpu.VMEM((STEPS, sec_count, group, LANES), jnp.float32),
            pltpu.VMEM((STEPS, sec_count, group, LANES), jnp.float32),
            pltpu.VMEM((STEPS, depth_z, LANES), jnp.float32),
            pltpu.VMEM((LANES, depth_z), jnp.float32),
            pltpu.VMEM((tile_y * slab_x, depth_z), jnp.float32),
            pltpu.VMEM((full_y * ROWS, wide_x), jnp.float32),
            dma((STEPS, 8)),
            dma((STEPS, 8)),
            dma((STEPS, 4)),
            dma((STEPS,)),
            dma((STEPS,)),
            dma((STEPS,)),
            dma((STEPS,)),
            dma((STEPS,)),
        ],
        compiler_params=pltpu.CompilerParams(
            collective_id=0, has_side_effects=True, vmem_limit_bytes=32 * 1024 * 1024
        ),
        name="les_steps",
    )(
        velocity.reshape(flat),
        prev_tendency.reshape(flat),
        disk_cells.reshape(1, -1),
        disk_kind.reshape(1, -1),
        rotor_weights,
        *constants,
    )
    return tuple(out.reshape(velocity.shape) for out in outs)


def solution(mesh):
    sec_count, tile_count = mesh.shape["sec"], mesh.shape["tile"]
    in_specs = (
        P(None, "sec", "tile", None),
        P(None, "sec", "tile", None),
        P("sec", "tile", None),
        P("sec", "tile", None),
        P(),
    )
    out_specs = (P(None, "sec", "tile", None), P(None, "sec", "tile", None))

    def pick(velocity, *others):
        _, slab_x, tile_y, depth_z = velocity.shape
        owners = depth_z // ROWS
        fits = (
            owners <= sec_count * tile_count
            and (sec_count * tile_count) % owners == 0
            and depth_z % LANES == 0
            and slab_x % ROWS == 0
            and tile_y >= 2
            and (tile_y + 2) * slab_x + 2 * tile_y <= LANES
            and tile_y * tile_count * ROWS <= 512
            and sec_count >= 3
            and tile_count >= 3
        )
        if fits:
            return direct(sec_count, tile_count, velocity, *others)
        return local(velocity, *others)

    return jax.shard_map(pick, mesh=mesh, in_specs=in_specs, out_specs=out_specs, check_vma=False)
```

```python
import functools
import math

import jax
import jax.numpy as jnp
import numpy as np
from jax import lax
from jax.experimental import pallas as pl
from jax.experimental.pallas import tpu as pltpu
from jax.sharding import PartitionSpec as P

STEPS = 2
KINDS = 16
ROWS = 8
LANES = 128
MESH = pl.DeviceIdType.MESH

precise = lax.Precision.HIGHEST
time_step = 0.1
fringe_rate = 2.0
smag_coef = 0.04


def extended_2(block, sides, width):
    for axis, dim in sides:
        count = lax.axis_size(axis)
        forward = [(i, i + 1) for i in range(count - 1)]
        forward.append((count - 1, 0))
        backward = [(target, source) for source, target in forward]
        low = lax.ppermute(
            lax.slice_in_dim(block, block.shape[dim] - width, None, axis=dim), axis, forward
        )
        high = lax.ppermute(lax.slice_in_dim(block, 0, width, axis=dim), axis, backward)
        block = jnp.concatenate([low, block, high], axis=dim)
    return block


def from_root(block, axis, owner):
    block = jnp.where(lax.axis_index(axis) == owner, block, jnp.zeros_like(block))
    return lax.psum(block, axis)


def gradients(padded, z_sign):
    centre = padded[:, 1:-1, 1:-1, :]
    grad_x = 0.5 * (padded[:, 2:, 1:-1, :] - padded[:, :-2, 1:-1, :])
    grad_y = 0.5 * (padded[:, 1:-1, 2:, :] - padded[:, 1:-1, :-2, :])
    extended = jnp.concatenate(
        [z_sign * centre[..., :1], centre, z_sign * centre[..., -1:]], axis=-1
    )
    grad_z = 0.5 * (extended[..., 2:] - extended[..., :-2])
    return (grad_x, grad_y, grad_z)


def strain_stress(slopes):

    def strain(first, second):
        return 0.5 * (slopes[second][first] + slopes[first][second])

    strain_xx = strain(0, 0)
    strain_yy = strain(1, 1)
    strain_zz = strain(2, 2)
    strain_xy = strain(0, 1)
    strain_xz = strain(0, 2)
    strain_yz = strain(1, 2)
    squared = strain_xx * strain_xx + strain_yy * strain_yy + strain_zz * strain_zz
    squared = squared + 2.0 * (
        strain_xy * strain_xy + strain_xz * strain_xz + strain_yz * strain_yz
    )
    double = 2.0 * (smag_coef * jnp.sqrt(2.0 * squared + 0.01))
    return jnp.stack(
        [
            double * strain_xx,
            double * strain_yy,
            double * strain_zz,
            double * strain_xy,
            double * strain_xz,
            double * strain_yz,
        ]
    )


def advection(slopes, centre):
    return centre[0:1] * slopes[0] + centre[1:2] * slopes[1] + centre[2:3] * slopes[2]


def stress_force(padded):
    grad_x, grad_y, grad_z = gradients(padded, 0.0)
    return jnp.stack(
        [
            grad_x[0] + grad_y[3] + grad_z[4],
            grad_x[3] + grad_y[1] + grad_z[5],
            grad_x[4] + grad_y[5] + grad_z[2],
        ]
    )


def faces(source):
    return extended_2(source, (("sec", 1), ("tile", 2)), 1)


def sec_turn(blocks):
    return lax.all_to_all(blocks, "sec", split_axis=0, concat_axis=0, tiled=True)


def tile_turn(blocks):
    return lax.all_to_all(blocks, "tile", split_axis=0, concat_axis=0, tiled=True)


def hartley_table(length):
    index_row = jnp.arange(length)
    product = index_row[:, None] * index_row[None, :] % length
    angle = 2.0 * math.pi / length * product.astype(jnp.float32)
    return jnp.cos(angle) + jnp.sin(angle)


def local(velocity, prev_tendency, disk_cells, disk_kind, rotor_weights):
    sec_count = lax.axis_size("sec")
    tile_count = lax.axis_size("tile")
    sec_at = lax.axis_index("sec")
    tile_at = lax.axis_index("tile")
    slab_x = velocity.shape[1]
    tile_y = velocity.shape[2]
    depth_z = velocity.shape[3]
    full_x = slab_x * sec_count
    full_y = tile_y * tile_count
    part_z = depth_z // sec_count
    modes_each = slab_x * depth_z // tile_count
    cell_count = slab_x * tile_y * depth_z
    modes = jnp.arange(depth_z).astype(jnp.float32)[:, None]
    points = jnp.arange(depth_z).astype(jnp.float32)[None, :] + 0.5
    cos_blocks = jnp.cos(math.pi * modes * points / depth_z).reshape(sec_count, part_z, depth_z)
    weight_blocks = jnp.where(jnp.arange(depth_z) == 0, 1.0 / depth_z, 2.0 / depth_z).astype(
        jnp.float32
    )
    weight_blocks = weight_blocks.reshape(sec_count, part_z)
    x_table = hartley_table(full_x)
    y_table = hartley_table(full_y).reshape(full_y, tile_count, tile_y)
    flat_ids = tile_at * modes_each + jnp.arange(modes_each)
    mode_x = flat_ids // part_z
    mode_z = sec_at * part_z + flat_ids % part_z
    mode_y = jnp.arange(full_y)
    sin_x = jnp.sin(2.0 * math.pi * mode_x.astype(jnp.float32) / full_x)
    sin_y = jnp.sin(2.0 * math.pi * mode_y.astype(jnp.float32) / full_y)
    sin_z = jnp.sin(math.pi * mode_z.astype(jnp.float32) / depth_z)
    eigen = -((sin_x * sin_x)[:, None] + (sin_y * sin_y)[None, :] + (sin_z * sin_z)[:, None])
    zero_mode = (
        (mode_x % (full_x // 2) == 0)[:, None]
        & (mode_y % (full_y // 2) == 0)[None, :]
        & (mode_z == 0)[:, None]
    )
    recip = jnp.where(zero_mode, 0.0, 1.0 / jnp.where(zero_mode, 1.0, eigen))
    slab_pos = jnp.sin(math.pi * (jnp.arange(slab_x).astype(jnp.float32) + 0.5) / slab_x)
    lam_x = fringe_rate * (slab_pos * slab_pos)
    flag = (
        (sec_at == 0)
        | (sec_at == sec_count // 2)
        | (sec_at == 3 * sec_count // 4)
        | (sec_at == sec_count - 1)
    ).astype(jnp.float32)
    picked = disk_cells.reshape(-1)
    kinds = disk_kind.reshape(-1)
    live = picked < cell_count
    safe = jnp.minimum(picked, cell_count - 1)
    weight = jnp.sum(
        jnp.where(kinds[:, None] == jnp.arange(KINDS)[None, :], rotor_weights[None, :], 0.0), axis=1
    )
    current = velocity
    tendency_old = prev_tendency
    tendency = prev_tendency
    for step_no in range(STEPS):
        wide = extended_2(current, (("sec", 1), ("tile", 2)), 2)
        wide_slopes = gradients(wide, -1.0)
        push_field = stress_force(strain_stress(wide_slopes))
        slopes = tuple((piece[:, 1:-1, 1:-1, :] for piece in wide_slopes))
        advect = advection(slopes, current)
        target = from_root(current, "sec", sec_count // 2 - 1)
        fringe = flag * lam_x[None, :, None, None] * (target - current)
        sampled = current[0].reshape(-1)[safe]
        push = jnp.where(live, -(weight * sampled * jnp.abs(sampled)), 0.0)
        turbine = (
            jnp.zeros((cell_count,), jnp.float32)
            .at[safe]
            .add(push)
            .reshape(slab_x, tile_y, depth_z)
        )
        empty = jnp.zeros_like(turbine)
        tendency = push_field - advect + jnp.stack([turbine, empty, empty]) + fringe
        interim = current + time_step * (1.5 * tendency - 0.5 * tendency_old)
        grad_x, grad_y, grad_z = gradients(faces(interim), -1.0)
        rhs = grad_x[0] + grad_y[1] + grad_z[2]
        coeffs = jnp.einsum("xyz,bcz->bxyc", rhs, cos_blocks, precision=precise)
        gathered = sec_turn(coeffs).reshape(full_x, tile_y, part_z)
        along_x = jnp.einsum("xyc,kx->kcy", gathered, x_table, precision=precise)
        spread = tile_turn(along_x.reshape(tile_count, modes_each, tile_y))
        along_y = jnp.einsum("sqt,lst->ql", spread, y_table, precision=precise)
        scaled = along_y * recip
        back_y = jnp.einsum("ql,lst->sqt", scaled, y_table, precision=precise) / (full_x * full_y)
        returned = tile_turn(back_y).reshape(full_x, part_z, tile_y)
        back_x = jnp.einsum("kcy,kx->xyc", returned, x_table, precision=precise)
        home = sec_turn(back_x.reshape(sec_count, slab_x, tile_y, part_z))
        pressure = jnp.einsum(
            "bxyc,bcz->xyz", home * weight_blocks[:, None, None, :], cos_blocks, precision=precise
        )
        press_x, press_y, press_z = gradients(faces(pressure[None]), 1.0)
        current = interim - jnp.concatenate([press_x, press_y, press_z], axis=0)
        tendency_old = tendency
    return (current, tendency)


def cas_table(first, second, length):
    angle = 2.0 * np.pi / length * (np.outer(first, second) % length)
    return np.cos(angle) + np.sin(angle)


def halves(table):
    high = table.astype(np.float32).astype(jnp.bfloat16)
    low = (table - high.astype(np.float64)).astype(np.float32).astype(jnp.bfloat16)
    stacked = np.concatenate([high, low], axis=0)
    return np.concatenate(np.split(stacked, stacked.shape[1] // LANES, axis=1), axis=0)


def whole(table, columns):
    count = table.shape[0] * LANES // columns
    parts = [table[i * count : (i + 1) * count] for i in range(columns // LANES)]
    return jnp.concatenate(parts, axis=1)


def tables(sec_count, tile_count, slab_x, tile_y, depth_z):
    full_x, full_y = slab_x * sec_count, tile_y * tile_count
    wide_x = -(-full_x // LANES) * LANES
    planes, block = tile_y + 2, slab_x + ROWS
    z_at = np.arange(depth_z)
    cos_z = np.cos(np.pi / depth_z * np.outer(z_at, z_at + 0.5))
    x_cas = np.zeros((sec_count, LANES, wide_x))
    for sec in range(sec_count):
        start = sec * slab_x
        cells = np.concatenate([start + np.arange(slab_x), [start - 1, start + slab_x]]) % full_x
        for plane in range(planes):
            x_cas[sec, plane * block : plane * block + slab_x + 2, :full_x] = cas_table(
                cells, np.arange(full_x), full_x
            )
    x_cas = x_cas.reshape(sec_count * LANES, wide_x)
    y_blocks = []
    for plane in range(planes):
        y_at = (np.arange(tile_count) * tile_y + plane - 1) % full_y
        y_blocks.append(np.kron(cas_table(np.arange(full_y), y_at, full_y), np.eye(ROWS)))
    y_cas = np.concatenate(y_blocks, axis=1)
    k_x, k_y = np.arange(full_x), np.arange(full_y)
    sin_x = np.where(k_x % (full_x // 2) == 0, 0.0, np.sin(2.0 * np.pi * k_x / full_x) ** 2)
    sin_y = np.where(k_y % (full_y // 2) == 0, 0.0, np.sin(2.0 * np.pi * k_y / full_y) ** 2)
    sin_xy = np.ones((full_y * ROWS, wide_x), np.float32)
    sin_xy[:, :full_x] = np.repeat(sin_y, ROWS)[:, None] + sin_x[None, :]
    sin_z = np.sin(np.pi * z_at / depth_z) ** 2
    weight_z = -np.where(z_at == 0, 1.0, 2.0) / (depth_z * full_x * full_y)
    mode_z = np.stack([sin_z, weight_z]).astype(np.float32)
    mode_z = np.ascontiguousarray(np.broadcast_to(mode_z[:, :, None], (2, depth_z, wide_x)))
    lam = fringe_rate * np.sin(np.pi * (np.arange(slab_x) + 0.5) / slab_x) ** 2
    lam = np.ascontiguousarray(np.broadcast_to(lam.astype(np.float32)[:, None], (slab_x, depth_z)))
    return (
        halves(cos_z),
        halves(x_cas),
        halves(x_cas.T),
        halves(y_cas),
        halves(y_cas.T),
        sin_xy,
        mode_z,
        lam,
    )


def split(value):
    high = value.astype(jnp.bfloat16)
    return high, (value - high.astype(jnp.float32)).astype(jnp.bfloat16)


def dot(first, second, dims):
    return lax.dot_general(first, second, (dims, ((), ())), preferred_element_type=jnp.float32)


def table_first(table, second, dims):
    count = table.shape[0] // 2
    high, low = split(second)
    both = dot(table, high, dims)
    return both[:count] + (both[count:] + dot(table[:count], low, dims))


def table_second(first, table):
    count, depth = first.shape[0], table.shape[0] // 2
    high, low = split(first)
    both = dot(jnp.concatenate([high, low], axis=0), table[:depth], NN)
    return both[:count] + (both[count:] + dot(high, table[depth:], NN))


NN = ((1,), (0,))
NT = ((1,), (1,))


def slope_z(value, z_sign):
    depth = value.shape[1]
    lane = lax.broadcasted_iota(jnp.int32, value.shape, 1)
    edge = value * z_sign
    above = jnp.where(lane == depth - 1, edge, pltpu.roll(value, depth - 1, 1))
    below = jnp.where(lane == 0, edge, pltpu.roll(value, 1, 1))
    return 0.5 * (above - below)


def slope_x(value, low=None, high=None):
    count = value.shape[0]
    after = pltpu.roll(value, count - 1, 0)
    before = pltpu.roll(value, 1, 0)
    if low is not None:
        row = lax.broadcasted_iota(jnp.int32, value.shape, 0)
        after = jnp.where(row == count - 1, high, after)
        before = jnp.where(row == 0, low, before)
    return 0.5 * (after - before)


def step_kernel(
    sec_count,
    tile_count,
    slab_x,
    tile_y,
    depth_z,
    vel_hbm,
    old_hbm,
    cells_hbm,
    kinds_hbm,
    weights_ref,
    cos_hbm,
    x_hbm,
    xt_hbm,
    y_hbm,
    yt_hbm,
    sin_xy_hbm,
    mode_z_hbm,
    lam_hbm,
    vel_out,
    tend_out,
    wide,
    target,
    share,
    coeffs,
    plane_in,
    plane_out,
    returned,
    press,
    thrust,
    recip,
    vel_ref,
    old_ref,
    cells_ref,
    kinds_ref,
    cos_ref,
    x_ref,
    xt_ref,
    y_ref,
    yt_ref,
    sin_xy_ref,
    mode_z_ref,
    lam_ref,
    load_sem,
    halo_send,
    halo_recv,
    target_send,
    target_recv,
    mode_send,
    mode_recv,
    back_send,
    back_recv,
):
    sec = lax.axis_index("sec")
    tile = lax.axis_index("tile")
    devices = sec_count * tile_count
    me = tile * sec_count + sec
    owners = depth_z // ROWS
    spacing = devices // owners
    planes = tile_y + 2
    deep = tile_y + 4
    group = tile_count * ROWS
    block = slab_x + ROWS
    root = sec_count // 2 - 1
    fringes = sorted({0, sec_count // 2, 3 * sec_count // 4, sec_count - 1} - {root})
    is_owner = lax.rem(me, spacing) == 0
    owner_at = lax.div(me, spacing)
    in_fringe = functools.reduce(jnp.logical_or, [sec == which for which in fringes])
    low_sec, high_sec = lax.rem(sec + sec_count - 1, sec_count), lax.rem(sec + 1, sec_count)
    low_tile, high_tile = lax.rem(tile + tile_count - 1, tile_count), lax.rem(tile + 1, tile_count)
    end_x = ROWS + slab_x
    own_x, own_y = slice(ROWS, end_x), slice(2, 2 + tile_y)

    loads = [
        pltpu.make_async_copy(source, held, load_sem.at[place])
        for place, (source, held) in enumerate(
            (
                (vel_hbm, vel_ref),
                (cells_hbm, cells_ref),
                (kinds_hbm, kinds_ref),
                (sin_xy_hbm, sin_xy_ref),
                (mode_z_hbm, mode_z_ref),
                (old_hbm, old_ref),
                (lam_hbm, lam_ref),
                (cos_hbm, cos_ref),
                (y_hbm, y_ref),
                (x_hbm, x_ref),
                (xt_hbm, xt_ref),
                (yt_hbm, yt_ref),
            )
        )
    ]
    for load in loads:
        load.start()

    barrier = pltpu.get_barrier_semaphore()

    def greet(ahead, carry):
        other = lax.rem(me + ahead, devices)
        pl.semaphore_signal(
            barrier,
            inc=1,
            device_id=(lax.rem(other, sec_count), lax.div(other, sec_count)),
            device_id_type=MESH,
        )
        return carry

    lax.fori_loop(1, devices, greet, 0)

    share[...] = jnp.zeros_like(share)
    loads[0].wait()
    for part in range(3):
        for row in range(tile_y):
            wide[0, part, 2 + row, own_x, :] = vel_ref[part, pl.ds(row, slab_x, stride=tile_y), :]

    pl.semaphore_wait(barrier, devices - 1)

    def start_halo(step):
        xs = {
            -1: (low_sec, slice(ROWS, 2 * ROWS), slice(end_x, end_x + ROWS)),
            0: (sec, own_x, own_x),
            1: (high_sec, slice(end_x - ROWS, end_x), slice(0, ROWS)),
        }
        ys = {
            -1: (low_tile, slice(2, 4), slice(2 + tile_y, deep)),
            0: (tile, own_y, own_y),
            1: (high_tile, slice(tile_y, 2 + tile_y), slice(0, 2)),
        }
        copies = []
        for x_way in (-1, 0, 1):
            for y_way in (-1, 0, 1):
                if x_way == 0 and y_way == 0:
                    continue
                slot = len(copies)
                to_sec, x_from, x_to = xs[x_way]
                to_tile, y_from, y_to = ys[y_way]
                if x_way != 0 and y_way == -1:
                    y_from, y_to = slice(2, 3), slice(2 + tile_y, 3 + tile_y)
                if x_way != 0 and y_way == 1:
                    y_from, y_to = slice(1 + tile_y, 2 + tile_y), slice(1, 2)
                copy = pltpu.make_async_remote_copy(
                    src_ref=wide.at[step, :, y_from, x_from, :],
                    dst_ref=wide.at[step, :, y_to, x_to, :],
                    send_sem=halo_send.at[step, slot],
                    recv_sem=halo_recv.at[step, slot],
                    device_id=(to_sec, to_tile),
                    device_id_type=MESH,
                )
                copies.append(copy)
        sends = [
            pltpu.make_async_remote_copy(
                src_ref=wide.at[step, :, own_y, own_x, :],
                dst_ref=target.at[step],
                send_sem=target_send.at[step, place],
                recv_sem=target_recv.at[step],
                device_id=(which, tile),
                device_id_type=MESH,
            )
            for place, which in enumerate(fringes)
        ]

        @pl.when(sec == root)
        def _():
            for send in sends:
                send.start()

        for copy in copies:
            copy.start()
        return copies, sends

    halo = start_halo(0)
    pending = [halo]

    for load in loads[1:5]:
        load.wait()
    cells = cells_ref[...]
    kinds = kinds_ref[...]
    weight = jnp.zeros(cells.shape, jnp.float32)
    for kind in range(KINDS):
        weight = jnp.where(kinds == kind, weights_ref[kind], weight)
    weight = jnp.where(cells < slab_x * tile_y * depth_z, weight, 0.0)
    column = lax.div(cells, depth_z)
    row_of = lax.rem(column, tile_y) * slab_x + lax.div(column, tile_y)
    slots = cells.shape[1]
    hit_row = lax.broadcasted_iota(jnp.int32, (tile_y * slab_x, slots), 0) == row_of
    hit_z = lax.broadcasted_iota(jnp.int32, (depth_z, slots), 0) == lax.rem(cells, depth_z)
    hit_z = hit_z.astype(jnp.float32).astype(jnp.bfloat16)
    rest = jnp.where(hit_row, weight, 0.0)
    summed = jnp.zeros((tile_y * slab_x, depth_z), jnp.float32)
    for _ in range(3):
        piece, rest_next = rest.astype(jnp.bfloat16), None
        rest_next = rest - piece.astype(jnp.float32)
        summed = summed + lax.dot_general(
            piece, hit_z, (NT, ((), ())), preferred_element_type=jnp.float32
        )
        rest = rest_next
    thrust[...] = summed

    @pl.when(is_owner)
    def _():
        rows = pl.ds(pl.multiple_of(owner_at * ROWS, ROWS), ROWS)
        full_y = tile_y * tile_count
        sum_sin = sin_xy_ref[...] + jnp.concatenate([mode_z_ref[0, rows, :]] * full_y, axis=0)
        scale = jnp.concatenate([mode_z_ref[1, rows, :]] * full_y, axis=0)
        zero_mode = sum_sin == 0.0
        recip[...] = jnp.where(zero_mode, 0.0, scale / jnp.where(zero_mode, 1.0, sum_sin))

    for load in loads[5:]:
        load.wait()
    old = [
        [old_ref[part, pl.ds(row, slab_x, stride=tile_y), :] for row in range(tile_y)]
        for part in range(3)
    ]

    for step in range(STEPS):
        copies, sends = halo

        for copy in copies:
            copy.wait_recv()

        centre, stress, advect = {}, {}, {}
        for plane in range(1, deep - 1):
            here = [wide[step, part, plane] for part in range(3)]
            d_x = [slope_x(value) for value in here]
            d_y = [
                0.5 * (wide[step, part, plane + 1] - wide[step, part, plane - 1])
                for part in range(3)
            ]
            d_z = [slope_z(value, -1.0) for value in here]
            s_xx, s_yy, s_zz = d_x[0], d_y[1], d_z[2]
            s_xy = 0.5 * (d_x[1] + d_y[0])
            s_xz = 0.5 * (d_x[2] + d_z[0])
            s_yz = 0.5 * (d_y[2] + d_z[1])
            squared = s_xx * s_xx + s_yy * s_yy + s_zz * s_zz
            squared = squared + 2.0 * (s_xy * s_xy + s_xz * s_xz + s_yz * s_yz)
            double = (2.0 * smag_coef) * jnp.sqrt(2.0 * squared + 0.01)
            stress[plane] = [double * s for s in (s_xx, s_yy, s_zz, s_xy, s_xz, s_yz)]
            centre[plane] = here
            advect[plane] = [
                here[0] * d_x[part] + here[1] * d_y[part] + here[2] * d_z[part]
                for part in range(3)
            ]

        @pl.when(in_fringe)
        def _(step=step):
            pltpu.make_async_copy(target.at[step], target.at[step], target_recv.at[step]).wait()

        @pl.when(jnp.logical_not(in_fringe))
        def _(step=step):
            target[step] = wide[step, :, own_y, own_x, :]

        interim, tendency = [], []
        for row in range(tile_y):
            plane = 2 + row
            xx, yy, zz, xy, xz, yz = stress[plane]
            before, after = stress[plane - 1], stress[plane + 1]
            push = [
                slope_x(xx) + 0.5 * (after[3] - before[3]) + slope_z(xz, 0.0),
                slope_x(xy) + 0.5 * (after[1] - before[1]) + slope_z(yz, 0.0),
                slope_x(xz) + 0.5 * (after[5] - before[5]) + slope_z(zz, 0.0),
            ]
            lam = lam_ref[...]
            tend, mid = [], []
            for part in range(3):
                here = centre[plane][part][own_x]
                total = (push[part] - advect[plane][part])[own_x]
                if part == 0:
                    force = thrust[row * slab_x : (row + 1) * slab_x, :]
                    total = total - force * here * jnp.abs(here)
                total = total + lam * (target[step, part, row] - here)
                tend.append(total)
                mid.append(here + time_step * (1.5 * total - 0.5 * old[part][row]))
                if step == STEPS - 1:
                    tend_out[part, pl.ds(row, slab_x, stride=tile_y), :] = total
            tendency.append(tend)
            interim.append(mid)
        old = [[tendency[row][part] for row in range(tile_y)] for part in range(3)]

        share[0:slab_x, :] = 0.5 * interim[0][1]
        last = (planes - 1) * block
        share[last : last + slab_x, :] = -0.5 * interim[tile_y - 1][1]
        for row in range(tile_y):
            along_x, _, along_z = interim[row]
            total = slope_x(along_x, 0.0, 0.0) + slope_z(along_z, -1.0)
            if row + 1 < tile_y:
                total = total + 0.5 * interim[row + 1][1]
            if row > 0:
                total = total - 0.5 * interim[row - 1][1]
            start = (row + 1) * block
            edge = start + slab_x
            share[start:edge, :] = total
            share[edge : edge + 1, :] = 0.5 * along_x[0:1]
            share[edge + 1 : edge + 2, :] = -0.5 * along_x[slab_x - 1 : slab_x]
        coeffs[step] = table_first(cos_ref[...], share[...], NT)

        my_rows = pl.ds(pl.multiple_of(tile * ROWS, ROWS), ROWS)

        def send_modes(ahead, carry, step=step):
            owner = lax.rem(owner_at + ahead, owners)
            flat = owner * spacing
            rows = pl.ds(pl.multiple_of(owner * ROWS, ROWS), ROWS)

            @pl.when(flat == me)
            def _():
                pltpu.make_async_copy(
                    coeffs.at[step, rows, :], plane_in.at[step, sec, my_rows, :], mode_recv.at[step]
                ).start()

            @pl.when(flat != me)
            def _():
                pltpu.make_async_remote_copy(
                    src_ref=coeffs.at[step, rows, :],
                    dst_ref=plane_in.at[step, sec, my_rows, :],
                    send_sem=mode_send.at[step],
                    recv_sem=mode_recv.at[step],
                    device_id=(lax.rem(flat, sec_count), lax.div(flat, sec_count)),
                    device_id_type=MESH,
                ).start()

            return carry

        lax.fori_loop(0, owners, send_modes, 0)

        @pl.when(is_owner)
        def _(step=step):
            pltpu.make_async_copy(
                plane_in.at[step], plane_in.at[step], mode_recv.at[step]
            ).wait()
            lane_plane = lax.broadcasted_iota(jnp.int32, (group, LANES), 1) // block
            arrived = [plane_in[step, part] for part in range(sec_count)]
            masked = jnp.concatenate(
                [
                    jnp.concatenate(
                        [jnp.where(lane_plane == plane, piece, 0.0) for piece in arrived], axis=1
                    )
                    for plane in range(planes)
                ],
                axis=0,
            )
            modes = table_second(table_first(whole(y_ref[...], planes * group), masked, NN), whole(x_ref[...], recip.shape[1])) * recip[...]
            spread = table_first(whole(yt_ref[...], recip.shape[0]), table_second(modes, whole(xt_ref[...], sec_count * LANES)), NN)
            for part in range(sec_count):
                lanes = slice(part * LANES, (part + 1) * LANES)
                piece = spread[:group, lanes]
                for plane in range(1, planes):
                    other = spread[plane * group : (plane + 1) * group, lanes]
                    piece = jnp.where(lane_plane == plane, other, piece)
                plane_out[step, part] = piece
            rows = pl.ds(pl.multiple_of(owner_at * ROWS, ROWS), ROWS)

            pltpu.make_async_copy(
                plane_out.at[step, sec, my_rows, :], returned.at[step, rows, :], back_recv.at[step]
            ).start()

            def send_back(ahead, carry):
                other = lax.rem(me + ahead, devices)
                to_sec, to_tile = lax.rem(other, sec_count), lax.div(other, sec_count)
                pltpu.make_async_remote_copy(
                    src_ref=plane_out.at[
                        step, to_sec, pl.ds(pl.multiple_of(to_tile * ROWS, ROWS), ROWS), :
                    ],
                    dst_ref=returned.at[step, rows, :],
                    send_sem=back_send.at[step],
                    recv_sem=back_recv.at[step],
                    device_id=(to_sec, to_tile),
                    device_id_type=MESH,
                ).start()
                return carry

            lax.fori_loop(1, devices, send_back, 0)

        pltpu.make_async_copy(returned.at[step], returned.at[step], back_recv.at[step]).wait()
        press[...] = table_second(returned[step].T, cos_ref[...])
        for row in range(tile_y):
            start = (row + 1) * block
            edge = start + slab_x
            here = press[start:edge, :]
            above = press[start + block : edge + block, :]
            below = press[start - block : edge - block, :]
            slopes = [
                slope_x(here, press[edge : edge + 1, :], press[edge + 1 : edge + 2, :]),
                0.5 * (above - below),
                slope_z(here, 1.0),
            ]
            for part in range(3):
                value = interim[row][part] - slopes[part]
                if step == STEPS - 1:
                    vel_out[part, pl.ds(row, slab_x, stride=tile_y), :] = value
                else:
                    wide[step + 1, part, 2 + row, own_x, :] = value
        if step < STEPS - 1:
            halo = start_halo(step + 1)
            pending.append(halo)

    for step, (copies, sends) in enumerate(pending):
        for copy in copies:
            copy.wait_send()

        @pl.when(sec == root)
        def _(sends=sends):
            for send in sends:
                send.wait_send()

        @pl.when(is_owner)
        def _(step=step):
            most = coeffs.at[step, pl.ds(0, (owners - 1) * ROWS), :]
            pltpu.make_async_copy(most, most, mode_send.at[step]).wait()
            some = plane_out.at[step, pl.ds(0, sec_count - 1)]
            pltpu.make_async_copy(some, some, back_send.at[step]).wait()
            last = plane_out.at[step, sec_count - 1, pl.ds(0, group - ROWS), :]
            pltpu.make_async_copy(last, last, back_send.at[step]).wait()

        @pl.when(jnp.logical_not(is_owner))
        def _(step=step):
            pltpu.make_async_copy(coeffs.at[step], coeffs.at[step], mode_send.at[step]).wait()


def direct(sec_count, tile_count, velocity, prev_tendency, disk_cells, disk_kind, rotor_weights):
    _, slab_x, tile_y, depth_z = velocity.shape
    constants = [
        jnp.asarray(table) for table in tables(sec_count, tile_count, slab_x, tile_y, depth_z)
    ]
    wide_x = constants[5].shape[1]
    full_y = tile_y * tile_count
    group = tile_count * ROWS
    flat = (3, slab_x * tile_y, depth_z)
    vmem = pl.BlockSpec(memory_space=pltpu.VMEM)
    hbm = pl.BlockSpec(memory_space=pltpu.HBM)
    operands = [
        velocity.reshape(flat),
        prev_tendency.reshape(flat),
        disk_cells.reshape(1, -1),
        disk_kind.reshape(1, -1),
        *constants,
    ]
    smem = pl.BlockSpec(memory_space=pltpu.SMEM)
    dma = pltpu.SemaphoreType.DMA
    outs = pl.pallas_call(
        functools.partial(step_kernel, sec_count, tile_count, slab_x, tile_y, depth_z),
        out_shape=[jax.ShapeDtypeStruct(flat, jnp.float32)] * 2,
        in_specs=[hbm] * 4 + [smem] + [hbm] * len(constants),
        out_specs=[vmem] * 2,
        scratch_shapes=[
            pltpu.VMEM((STEPS, 3, tile_y + 4, slab_x + 2 * ROWS, depth_z), jnp.float32),
            pltpu.VMEM((STEPS, 3, tile_y, slab_x, depth_z), jnp.float32),
            pltpu.VMEM((LANES, depth_z), jnp.float32),
            pltpu.VMEM((STEPS, depth_z, LANES), jnp.float32),
            pltpu.VMEM((STEPS, sec_count, group, LANES), jnp.float32),
            pltpu.VMEM((STEPS, sec_count, group, LANES), jnp.float32),
            pltpu.VMEM((STEPS, depth_z, LANES), jnp.float32),
            pltpu.VMEM((LANES, depth_z), jnp.float32),
            pltpu.VMEM((tile_y * slab_x, depth_z), jnp.float32),
            pltpu.VMEM((full_y * ROWS, wide_x), jnp.float32),
            *[pltpu.VMEM(operand.shape, operand.dtype) for operand in operands],
            dma((len(operands),)),
            dma((STEPS, 8)),
            dma((STEPS, 8)),
            dma((STEPS, 4)),
            dma((STEPS,)),
            dma((STEPS,)),
            dma((STEPS,)),
            dma((STEPS,)),
            dma((STEPS,)),
        ],
        compiler_params=pltpu.CompilerParams(
            collective_id=0, has_side_effects=True, vmem_limit_bytes=63 * 1024 * 1024
        ),
        name="les_steps",
    )(*operands[:4], rotor_weights, *operands[4:])
    return tuple(out.reshape(velocity.shape) for out in outs)


def solution(mesh):
    sec_count, tile_count = mesh.shape["sec"], mesh.shape["tile"]
    in_specs = (
        P(None, "sec", "tile", None),
        P(None, "sec", "tile", None),
        P("sec", "tile", None),
        P("sec", "tile", None),
        P(),
    )
    out_specs = (P(None, "sec", "tile", None), P(None, "sec", "tile", None))

    def pick(velocity, *others):
        _, slab_x, tile_y, depth_z = velocity.shape
        owners = depth_z // ROWS
        fits = (
            owners <= sec_count * tile_count
            and (sec_count * tile_count) % owners == 0
            and depth_z % LANES == 0
            and slab_x % ROWS == 0
            and tile_y >= 2
            and (tile_y + 2) * (slab_x + ROWS) <= LANES
            and tile_y * tile_count * ROWS <= 512
            and sec_count >= 3
            and tile_count >= 3
        )
        if fits:
            return direct(sec_count, tile_count, velocity, *others)
        return local(velocity, *others)

    return jax.shard_map(pick, mesh=mesh, in_specs=in_specs, out_specs=out_specs, check_vma=False)
```

```python
import functools
import math

import jax
import jax.numpy as jnp
import numpy as np
from jax import lax
from jax.experimental import pallas as pl
from jax.experimental.pallas import tpu as pltpu
from jax.sharding import PartitionSpec as P

STEPS = 2
KINDS = 16
ROWS = 8
LANES = 128
MESH = pl.DeviceIdType.MESH

precise = lax.Precision.HIGHEST
time_step = 0.1
fringe_rate = 2.0
smag_coef = 0.04


def extended_2(block, sides, width):
    for axis, dim in sides:
        count = lax.axis_size(axis)
        forward = [(i, i + 1) for i in range(count - 1)]
        forward.append((count - 1, 0))
        backward = [(target, source) for source, target in forward]
        low = lax.ppermute(
            lax.slice_in_dim(block, block.shape[dim] - width, None, axis=dim), axis, forward
        )
        high = lax.ppermute(lax.slice_in_dim(block, 0, width, axis=dim), axis, backward)
        block = jnp.concatenate([low, block, high], axis=dim)
    return block


def from_root(block, axis, owner):
    block = jnp.where(lax.axis_index(axis) == owner, block, jnp.zeros_like(block))
    return lax.psum(block, axis)


def gradients(padded, z_sign):
    centre = padded[:, 1:-1, 1:-1, :]
    grad_x = 0.5 * (padded[:, 2:, 1:-1, :] - padded[:, :-2, 1:-1, :])
    grad_y = 0.5 * (padded[:, 1:-1, 2:, :] - padded[:, 1:-1, :-2, :])
    extended = jnp.concatenate(
        [z_sign * centre[..., :1], centre, z_sign * centre[..., -1:]], axis=-1
    )
    grad_z = 0.5 * (extended[..., 2:] - extended[..., :-2])
    return (grad_x, grad_y, grad_z)


def strain_stress(slopes):

    def strain(first, second):
        return 0.5 * (slopes[second][first] + slopes[first][second])

    strain_xx = strain(0, 0)
    strain_yy = strain(1, 1)
    strain_zz = strain(2, 2)
    strain_xy = strain(0, 1)
    strain_xz = strain(0, 2)
    strain_yz = strain(1, 2)
    squared = strain_xx * strain_xx + strain_yy * strain_yy + strain_zz * strain_zz
    squared = squared + 2.0 * (
        strain_xy * strain_xy + strain_xz * strain_xz + strain_yz * strain_yz
    )
    double = 2.0 * (smag_coef * jnp.sqrt(2.0 * squared + 0.01))
    return jnp.stack(
        [
            double * strain_xx,
            double * strain_yy,
            double * strain_zz,
            double * strain_xy,
            double * strain_xz,
            double * strain_yz,
        ]
    )


def advection(slopes, centre):
    return centre[0:1] * slopes[0] + centre[1:2] * slopes[1] + centre[2:3] * slopes[2]


def stress_force(padded):
    grad_x, grad_y, grad_z = gradients(padded, 0.0)
    return jnp.stack(
        [
            grad_x[0] + grad_y[3] + grad_z[4],
            grad_x[3] + grad_y[1] + grad_z[5],
            grad_x[4] + grad_y[5] + grad_z[2],
        ]
    )


def faces(source):
    return extended_2(source, (("sec", 1), ("tile", 2)), 1)


def sec_turn(blocks):
    return lax.all_to_all(blocks, "sec", split_axis=0, concat_axis=0, tiled=True)


def tile_turn(blocks):
    return lax.all_to_all(blocks, "tile", split_axis=0, concat_axis=0, tiled=True)


def hartley_table(length):
    index_row = jnp.arange(length)
    product = index_row[:, None] * index_row[None, :] % length
    angle = 2.0 * math.pi / length * product.astype(jnp.float32)
    return jnp.cos(angle) + jnp.sin(angle)


def local(velocity, prev_tendency, disk_cells, disk_kind, rotor_weights):
    sec_count = lax.axis_size("sec")
    tile_count = lax.axis_size("tile")
    sec_at = lax.axis_index("sec")
    tile_at = lax.axis_index("tile")
    slab_x = velocity.shape[1]
    tile_y = velocity.shape[2]
    depth_z = velocity.shape[3]
    full_x = slab_x * sec_count
    full_y = tile_y * tile_count
    part_z = depth_z // sec_count
    modes_each = slab_x * depth_z // tile_count
    cell_count = slab_x * tile_y * depth_z
    modes = jnp.arange(depth_z).astype(jnp.float32)[:, None]
    points = jnp.arange(depth_z).astype(jnp.float32)[None, :] + 0.5
    cos_blocks = jnp.cos(math.pi * modes * points / depth_z).reshape(sec_count, part_z, depth_z)
    weight_blocks = jnp.where(jnp.arange(depth_z) == 0, 1.0 / depth_z, 2.0 / depth_z).astype(
        jnp.float32
    )
    weight_blocks = weight_blocks.reshape(sec_count, part_z)
    x_table = hartley_table(full_x)
    y_table = hartley_table(full_y).reshape(full_y, tile_count, tile_y)
    flat_ids = tile_at * modes_each + jnp.arange(modes_each)
    mode_x = flat_ids // part_z
    mode_z = sec_at * part_z + flat_ids % part_z
    mode_y = jnp.arange(full_y)
    sin_x = jnp.sin(2.0 * math.pi * mode_x.astype(jnp.float32) / full_x)
    sin_y = jnp.sin(2.0 * math.pi * mode_y.astype(jnp.float32) / full_y)
    sin_z = jnp.sin(math.pi * mode_z.astype(jnp.float32) / depth_z)
    eigen = -((sin_x * sin_x)[:, None] + (sin_y * sin_y)[None, :] + (sin_z * sin_z)[:, None])
    zero_mode = (
        (mode_x % (full_x // 2) == 0)[:, None]
        & (mode_y % (full_y // 2) == 0)[None, :]
        & (mode_z == 0)[:, None]
    )
    recip = jnp.where(zero_mode, 0.0, 1.0 / jnp.where(zero_mode, 1.0, eigen))
    slab_pos = jnp.sin(math.pi * (jnp.arange(slab_x).astype(jnp.float32) + 0.5) / slab_x)
    lam_x = fringe_rate * (slab_pos * slab_pos)
    flag = (
        (sec_at == 0)
        | (sec_at == sec_count // 2)
        | (sec_at == 3 * sec_count // 4)
        | (sec_at == sec_count - 1)
    ).astype(jnp.float32)
    picked = disk_cells.reshape(-1)
    kinds = disk_kind.reshape(-1)
    live = picked < cell_count
    safe = jnp.minimum(picked, cell_count - 1)
    weight = jnp.sum(
        jnp.where(kinds[:, None] == jnp.arange(KINDS)[None, :], rotor_weights[None, :], 0.0), axis=1
    )
    current = velocity
    tendency_old = prev_tendency
    tendency = prev_tendency
    for step_no in range(STEPS):
        wide = extended_2(current, (("sec", 1), ("tile", 2)), 2)
        wide_slopes = gradients(wide, -1.0)
        push_field = stress_force(strain_stress(wide_slopes))
        slopes = tuple((piece[:, 1:-1, 1:-1, :] for piece in wide_slopes))
        advect = advection(slopes, current)
        target = from_root(current, "sec", sec_count // 2 - 1)
        fringe = flag * lam_x[None, :, None, None] * (target - current)
        sampled = current[0].reshape(-1)[safe]
        push = jnp.where(live, -(weight * sampled * jnp.abs(sampled)), 0.0)
        turbine = (
            jnp.zeros((cell_count,), jnp.float32)
            .at[safe]
            .add(push)
            .reshape(slab_x, tile_y, depth_z)
        )
        empty = jnp.zeros_like(turbine)
        tendency = push_field - advect + jnp.stack([turbine, empty, empty]) + fringe
        interim = current + time_step * (1.5 * tendency - 0.5 * tendency_old)
        grad_x, grad_y, grad_z = gradients(faces(interim), -1.0)
        rhs = grad_x[0] + grad_y[1] + grad_z[2]
        coeffs = jnp.einsum("xyz,bcz->bxyc", rhs, cos_blocks, precision=precise)
        gathered = sec_turn(coeffs).reshape(full_x, tile_y, part_z)
        along_x = jnp.einsum("xyc,kx->kcy", gathered, x_table, precision=precise)
        spread = tile_turn(along_x.reshape(tile_count, modes_each, tile_y))
        along_y = jnp.einsum("sqt,lst->ql", spread, y_table, precision=precise)
        scaled = along_y * recip
        back_y = jnp.einsum("ql,lst->sqt", scaled, y_table, precision=precise) / (full_x * full_y)
        returned = tile_turn(back_y).reshape(full_x, part_z, tile_y)
        back_x = jnp.einsum("kcy,kx->xyc", returned, x_table, precision=precise)
        home = sec_turn(back_x.reshape(sec_count, slab_x, tile_y, part_z))
        pressure = jnp.einsum(
            "bxyc,bcz->xyz", home * weight_blocks[:, None, None, :], cos_blocks, precision=precise
        )
        press_x, press_y, press_z = gradients(faces(pressure[None]), 1.0)
        current = interim - jnp.concatenate([press_x, press_y, press_z], axis=0)
        tendency_old = tendency
    return (current, tendency)


def cas_table(first, second, length):
    angle = 2.0 * np.pi / length * (np.outer(first, second) % length)
    return np.cos(angle) + np.sin(angle)


def halves(table):
    high = table.astype(np.float32).astype(jnp.bfloat16)
    low = (table - high.astype(np.float64)).astype(np.float32).astype(jnp.bfloat16)
    stacked = np.concatenate([high, low], axis=0)
    return np.concatenate(np.split(stacked, stacked.shape[1] // LANES, axis=1), axis=0)


def whole(table, columns):
    count = table.shape[0] * LANES // columns
    parts = [table[i * count : (i + 1) * count] for i in range(columns // LANES)]
    return jnp.concatenate(parts, axis=1)


def tables(sec_count, tile_count, slab_x, tile_y, depth_z):
    full_x, full_y = slab_x * sec_count, tile_y * tile_count
    wide_x = -(-full_x // LANES) * LANES
    planes, block = tile_y + 2, slab_x + ROWS
    z_at = np.arange(depth_z)
    cos_z = np.cos(np.pi / depth_z * np.outer(z_at, z_at + 0.5))
    x_cas = np.zeros((LANES, wide_x))
    for sec in range(sec_count):
        start = sec * slab_x
        cells = np.concatenate([start + np.arange(slab_x), [start - 1, start + slab_x]]) % full_x
        x_cas[sec * block : sec * block + slab_x + 2, :full_x] = cas_table(
            cells, np.arange(full_x), full_x
        )
    y_blocks = []
    for plane in range(planes):
        y_at = (np.arange(tile_count) * tile_y + plane - 1) % full_y
        y_blocks.append(np.kron(cas_table(np.arange(full_y), y_at, full_y), np.eye(ROWS)))
    y_cas = np.concatenate(y_blocks, axis=1)
    k_x, k_y = np.arange(full_x), np.arange(full_y)
    sin_x = np.where(k_x % (full_x // 2) == 0, 0.0, np.sin(2.0 * np.pi * k_x / full_x) ** 2)
    sin_y = np.where(k_y % (full_y // 2) == 0, 0.0, np.sin(2.0 * np.pi * k_y / full_y) ** 2)
    sin_xy = np.ones((full_y * ROWS, wide_x), np.float32)
    sin_xy[:, :full_x] = np.repeat(sin_y, ROWS)[:, None] + sin_x[None, :]
    sin_z = np.sin(np.pi * z_at / depth_z) ** 2
    weight_z = -np.where(z_at == 0, 1.0, 2.0) / (depth_z * full_x * full_y)
    mode_z = np.stack([sin_z, weight_z]).astype(np.float32)
    mode_z = np.ascontiguousarray(np.broadcast_to(mode_z[:, :, None], (2, depth_z, wide_x)))
    lam = fringe_rate * np.sin(np.pi * (np.arange(slab_x) + 0.5) / slab_x) ** 2
    lam = np.ascontiguousarray(np.broadcast_to(lam.astype(np.float32)[:, None], (slab_x, depth_z)))
    return (
        halves(cos_z),
        halves(x_cas),
        halves(x_cas.T),
        halves(y_cas),
        halves(y_cas.T),
        sin_xy,
        mode_z,
        lam,
    )


def split(value):
    high = value.astype(jnp.bfloat16)
    return high, (value - high.astype(jnp.float32)).astype(jnp.bfloat16)


def dot(first, second, dims):
    return lax.dot_general(first, second, (dims, ((), ())), preferred_element_type=jnp.float32)


def table_first(table, second, dims):
    count = table.shape[0] // 2
    high, low = split(second)
    both = dot(table, high, dims)
    return both[:count] + (both[count:] + dot(table[:count], low, dims))


def table_second(first, table):
    count, depth = first.shape[0], table.shape[0] // 2
    high, low = split(first)
    both = dot(jnp.concatenate([high, low], axis=0), table[:depth], NN)
    return both[:count] + (both[count:] + dot(high, table[depth:], NN))


NN = ((1,), (0,))
NT = ((1,), (1,))


def slope_z(value, z_sign):
    depth = value.shape[1]
    lane = lax.broadcasted_iota(jnp.int32, value.shape, 1)
    edge = value * z_sign
    above = jnp.where(lane == depth - 1, edge, pltpu.roll(value, depth - 1, 1))
    below = jnp.where(lane == 0, edge, pltpu.roll(value, 1, 1))
    return 0.5 * (above - below)


def slope_x(value, low=None, high=None):
    count = value.shape[0]
    after = pltpu.roll(value, count - 1, 0)
    before = pltpu.roll(value, 1, 0)
    if low is not None:
        row = lax.broadcasted_iota(jnp.int32, value.shape, 0)
        after = jnp.where(row == count - 1, high, after)
        before = jnp.where(row == 0, low, before)
    return 0.5 * (after - before)


def step_kernel(
    sec_count,
    tile_count,
    slab_x,
    tile_y,
    depth_z,
    vel_hbm,
    old_hbm,
    cells_hbm,
    kinds_hbm,
    weights_ref,
    cos_hbm,
    x_hbm,
    xt_hbm,
    y_hbm,
    yt_hbm,
    sin_xy_hbm,
    mode_z_hbm,
    lam_hbm,
    vel_result,
    tend_result,
    wide,
    target,
    share,
    coeffs,
    plane_in,
    plane_out,
    returned,
    press,
    thrust,
    recip,
    vel_ref,
    old_ref,
    cells_ref,
    kinds_ref,
    cos_ref,
    x_ref,
    xt_ref,
    y_ref,
    yt_ref,
    sin_xy_ref,
    mode_z_ref,
    lam_ref,
    vel_out,
    tend_out,
    load_sem,
    result_sem,
    halo_send,
    halo_recv,
    target_send,
    target_recv,
    mode_send,
    mode_recv,
    back_send,
    back_recv,
):
    sec = lax.axis_index("sec")
    tile = lax.axis_index("tile")
    devices = sec_count * tile_count
    me = tile * sec_count + sec
    owners = depth_z // ROWS
    planes = tile_y + 2
    deep = tile_y + 4
    group = tile_count * ROWS
    block = slab_x + ROWS
    root = sec_count // 2 - 1
    fringes = sorted({0, sec_count // 2, 3 * sec_count // 4, sec_count - 1} - {root})
    first_tile = (tile_count - owners // sec_count) // 2
    is_owner = (tile >= first_tile) & (tile < first_tile + owners // sec_count)
    owner_at = (tile - first_tile) * sec_count + sec
    in_fringe = functools.reduce(jnp.logical_or, [sec == which for which in fringes])
    low_sec, high_sec = lax.rem(sec + sec_count - 1, sec_count), lax.rem(sec + 1, sec_count)
    low_tile, high_tile = lax.rem(tile + tile_count - 1, tile_count), lax.rem(tile + 1, tile_count)
    end_x = ROWS + slab_x
    own_x, own_y = slice(ROWS, end_x), slice(2, 2 + tile_y)

    loads = [
        pltpu.make_async_copy(source, held, load_sem.at[place])
        for place, (source, held) in enumerate(
            (
                (vel_hbm, vel_ref),
                (cells_hbm, cells_ref),
                (kinds_hbm, kinds_ref),
                (sin_xy_hbm, sin_xy_ref),
                (mode_z_hbm, mode_z_ref),
                (old_hbm, old_ref),
                (lam_hbm, lam_ref),
                (cos_hbm, cos_ref),
                (y_hbm, y_ref),
                (x_hbm, x_ref),
                (xt_hbm, xt_ref),
                (yt_hbm, yt_ref),
            )
        )
    ]
    for load in loads:
        load.start()

    results = [
        pltpu.make_async_copy(vel_out, vel_result, result_sem.at[0]),
        pltpu.make_async_copy(tend_out, tend_result, result_sem.at[1]),
    ]

    barrier = pltpu.get_barrier_semaphore()

    def greet(ahead, carry):
        other = lax.rem(me + ahead, devices)
        pl.semaphore_signal(
            barrier,
            inc=1,
            device_id=(lax.rem(other, sec_count), lax.div(other, sec_count)),
            device_id_type=MESH,
        )
        return carry

    lax.fori_loop(1, devices, greet, 0)

    share[...] = jnp.zeros_like(share)
    loads[0].wait()
    for part in range(3):
        for row in range(tile_y):
            wide[0, part, 2 + row, own_x, :] = vel_ref[part, pl.ds(row, slab_x, stride=tile_y), :]

    pl.semaphore_wait(barrier, devices - 1)

    def start_halo(step):
        xs = {
            -1: (low_sec, slice(ROWS, 2 * ROWS), slice(end_x, end_x + ROWS)),
            0: (sec, own_x, own_x),
            1: (high_sec, slice(end_x - ROWS, end_x), slice(0, ROWS)),
        }
        ys = {
            -1: (low_tile, slice(2, 4), slice(2 + tile_y, deep)),
            0: (tile, own_y, own_y),
            1: (high_tile, slice(tile_y, 2 + tile_y), slice(0, 2)),
        }
        copies = []
        for x_way in (-1, 0, 1):
            for y_way in (-1, 0, 1):
                if x_way == 0 and y_way == 0:
                    continue
                slot = len(copies)
                to_sec, x_from, x_to = xs[x_way]
                to_tile, y_from, y_to = ys[y_way]
                if x_way != 0 and y_way == -1:
                    y_from, y_to = slice(2, 3), slice(2 + tile_y, 3 + tile_y)
                if x_way != 0 and y_way == 1:
                    y_from, y_to = slice(1 + tile_y, 2 + tile_y), slice(1, 2)
                copy = pltpu.make_async_remote_copy(
                    src_ref=wide.at[step, :, y_from, x_from, :],
                    dst_ref=wide.at[step, :, y_to, x_to, :],
                    send_sem=halo_send.at[step, slot],
                    recv_sem=halo_recv.at[step, slot],
                    device_id=(to_sec, to_tile),
                    device_id_type=MESH,
                )
                copies.append(copy)
        sends = [
            pltpu.make_async_remote_copy(
                src_ref=wide.at[step, :, own_y, own_x, :],
                dst_ref=target.at[step],
                send_sem=target_send.at[step, place],
                recv_sem=target_recv.at[step],
                device_id=(which, tile),
                device_id_type=MESH,
            )
            for place, which in enumerate(fringes)
        ]

        @pl.when(sec == root)
        def _():
            for send in sends:
                send.start()

        for copy in copies:
            copy.start()
        return copies, sends

    halo = start_halo(0)
    pending = [halo]

    for load in loads[1:5]:
        load.wait()
    cells = cells_ref[...]
    kinds = kinds_ref[...]
    weight = jnp.zeros(cells.shape, jnp.float32)
    for kind in range(KINDS):
        weight = jnp.where(kinds == kind, weights_ref[kind], weight)
    weight = jnp.where(cells < slab_x * tile_y * depth_z, weight, 0.0)
    column = lax.div(cells, depth_z)
    row_of = lax.rem(column, tile_y) * slab_x + lax.div(column, tile_y)
    slots = cells.shape[1]
    hit_row = lax.broadcasted_iota(jnp.int32, (tile_y * slab_x, slots), 0) == row_of
    hit_z = lax.broadcasted_iota(jnp.int32, (depth_z, slots), 0) == lax.rem(cells, depth_z)
    hit_z = hit_z.astype(jnp.float32).astype(jnp.bfloat16)
    rest = jnp.where(hit_row, weight, 0.0)
    summed = jnp.zeros((tile_y * slab_x, depth_z), jnp.float32)
    for _ in range(3):
        piece, rest_next = rest.astype(jnp.bfloat16), None
        rest_next = rest - piece.astype(jnp.float32)
        summed = summed + lax.dot_general(
            piece, hit_z, (NT, ((), ())), preferred_element_type=jnp.float32
        )
        rest = rest_next
    thrust[...] = summed

    @pl.when(is_owner)
    def _():
        rows = pl.ds(pl.multiple_of(owner_at * ROWS, ROWS), ROWS)
        full_y = tile_y * tile_count
        sum_sin = sin_xy_ref[...] + jnp.concatenate([mode_z_ref[0, rows, :]] * full_y, axis=0)
        scale = jnp.concatenate([mode_z_ref[1, rows, :]] * full_y, axis=0)
        zero_mode = sum_sin == 0.0
        recip[...] = jnp.where(zero_mode, 0.0, scale / jnp.where(zero_mode, 1.0, sum_sin))

    for load in loads[5:]:
        load.wait()
    old = [
        [old_ref[part, pl.ds(row, slab_x, stride=tile_y), :] for row in range(tile_y)]
        for part in range(3)
    ]

    for step in range(STEPS):
        copies, sends = halo

        for copy in copies:
            copy.wait_recv()

        centre, stress, advect = {}, {}, {}
        for plane in range(1, deep - 1):
            here = [wide[step, part, plane] for part in range(3)]
            d_x = [slope_x(value) for value in here]
            d_y = [
                0.5 * (wide[step, part, plane + 1] - wide[step, part, plane - 1])
                for part in range(3)
            ]
            d_z = [slope_z(value, -1.0) for value in here]
            s_xx, s_yy, s_zz = d_x[0], d_y[1], d_z[2]
            s_xy = 0.5 * (d_x[1] + d_y[0])
            s_xz = 0.5 * (d_x[2] + d_z[0])
            s_yz = 0.5 * (d_y[2] + d_z[1])
            squared = s_xx * s_xx + s_yy * s_yy + s_zz * s_zz
            squared = squared + 2.0 * (s_xy * s_xy + s_xz * s_xz + s_yz * s_yz)
            double = (2.0 * smag_coef) * jnp.sqrt(2.0 * squared + 0.01)
            stress[plane] = [double * s for s in (s_xx, s_yy, s_zz, s_xy, s_xz, s_yz)]
            centre[plane] = here
            advect[plane] = [
                here[0] * d_x[part] + here[1] * d_y[part] + here[2] * d_z[part]
                for part in range(3)
            ]

        @pl.when(in_fringe)
        def _(step=step):
            pltpu.make_async_copy(target.at[step], target.at[step], target_recv.at[step]).wait()

        @pl.when(jnp.logical_not(in_fringe))
        def _(step=step):
            target[step] = wide[step, :, own_y, own_x, :]

        interim, tendency = [], []
        for row in range(tile_y):
            plane = 2 + row
            xx, yy, zz, xy, xz, yz = stress[plane]
            before, after = stress[plane - 1], stress[plane + 1]
            push = [
                slope_x(xx) + 0.5 * (after[3] - before[3]) + slope_z(xz, 0.0),
                slope_x(xy) + 0.5 * (after[1] - before[1]) + slope_z(yz, 0.0),
                slope_x(xz) + 0.5 * (after[5] - before[5]) + slope_z(zz, 0.0),
            ]
            lam = lam_ref[...]
            tend, mid = [], []
            for part in range(3):
                here = centre[plane][part][own_x]
                total = (push[part] - advect[plane][part])[own_x]
                if part == 0:
                    force = thrust[row * slab_x : (row + 1) * slab_x, :]
                    total = total - force * here * jnp.abs(here)
                total = total + lam * (target[step, part, row] - here)
                tend.append(total)
                mid.append(here + time_step * (1.5 * total - 0.5 * old[part][row]))
                if step == STEPS - 1:
                    tend_out[part, pl.ds(row, slab_x, stride=tile_y), :] = total
            tendency.append(tend)
            interim.append(mid)
        if step == STEPS - 1:
            results[1].start()
        old = [[tendency[row][part] for row in range(tile_y)] for part in range(3)]

        share[0:slab_x, :] = 0.5 * interim[0][1]
        last = (planes - 1) * block
        share[last : last + slab_x, :] = -0.5 * interim[tile_y - 1][1]
        for row in range(tile_y):
            along_x, _, along_z = interim[row]
            total = slope_x(along_x, 0.0, 0.0) + slope_z(along_z, -1.0)
            if row + 1 < tile_y:
                total = total + 0.5 * interim[row + 1][1]
            if row > 0:
                total = total - 0.5 * interim[row - 1][1]
            start = (row + 1) * block
            edge = start + slab_x
            share[start:edge, :] = total
            share[edge : edge + 1, :] = 0.5 * along_x[0:1]
            share[edge + 1 : edge + 2, :] = -0.5 * along_x[slab_x - 1 : slab_x]
        coeffs[step] = table_first(cos_ref[...], share[...], NT)

        my_rows = pl.ds(pl.multiple_of(tile * ROWS, ROWS), ROWS)

        def send_modes(ahead, carry, step=step):
            owner = lax.rem(me + ahead, owners)
            flat = owner + first_tile * sec_count
            rows = pl.ds(pl.multiple_of(owner * ROWS, ROWS), ROWS)

            @pl.when(flat == me)
            def _():
                pltpu.make_async_copy(
                    coeffs.at[step, rows, :], plane_in.at[step, sec, my_rows, :], mode_recv.at[step]
                ).start()

            @pl.when(flat != me)
            def _():
                pltpu.make_async_remote_copy(
                    src_ref=coeffs.at[step, rows, :],
                    dst_ref=plane_in.at[step, sec, my_rows, :],
                    send_sem=mode_send.at[step],
                    recv_sem=mode_recv.at[step],
                    device_id=(lax.rem(flat, sec_count), lax.div(flat, sec_count)),
                    device_id_type=MESH,
                ).start()

            return carry

        lax.fori_loop(0, owners, send_modes, 0)

        @pl.when(is_owner)
        def _(step=step):
            pltpu.make_async_copy(
                plane_in.at[step], plane_in.at[step], mode_recv.at[step]
            ).wait()
            lane_block = lax.broadcasted_iota(jnp.int32, (group, LANES), 1) // block
            arrived = [plane_in[step, part] for part in range(sec_count)]
            blocks = []
            for plane in range(planes):
                piece = pltpu.roll(arrived[0], -plane * block % LANES, 1)
                for part in range(1, sec_count):
                    other = pltpu.roll(arrived[part], (part - plane) * block % LANES, 1)
                    piece = jnp.where(lane_block == part, other, piece)
                blocks.append(piece)
            stacked = jnp.concatenate(blocks, axis=0)
            modes = table_second(table_first(whole(y_ref[...], planes * group), stacked, NN), whole(x_ref[...], recip.shape[1])) * recip[...]
            spread = table_first(whole(yt_ref[...], recip.shape[0]), table_second(modes, whole(xt_ref[...], LANES)), NN)
            for part in range(sec_count):
                piece = pltpu.roll(spread[:group], -part * block % LANES, 1)
                for plane in range(1, planes):
                    other = spread[plane * group : (plane + 1) * group]
                    other = pltpu.roll(other, (plane - part) * block % LANES, 1)
                    piece = jnp.where(lane_block == plane, other, piece)
                plane_out[step, part] = piece
            rows = pl.ds(pl.multiple_of(owner_at * ROWS, ROWS), ROWS)

            pltpu.make_async_copy(
                plane_out.at[step, sec, my_rows, :], returned.at[step, rows, :], back_recv.at[step]
            ).start()

            def send_back(ahead, carry):
                other = lax.rem(me + ahead, devices)
                to_sec, to_tile = lax.rem(other, sec_count), lax.div(other, sec_count)
                pltpu.make_async_remote_copy(
                    src_ref=plane_out.at[
                        step, to_sec, pl.ds(pl.multiple_of(to_tile * ROWS, ROWS), ROWS), :
                    ],
                    dst_ref=returned.at[step, rows, :],
                    send_sem=back_send.at[step],
                    recv_sem=back_recv.at[step],
                    device_id=(to_sec, to_tile),
                    device_id_type=MESH,
                ).start()
                return carry

            lax.fori_loop(1, devices, send_back, 0)

        pltpu.make_async_copy(returned.at[step], returned.at[step], back_recv.at[step]).wait()
        press[...] = table_second(returned[step].T, cos_ref[...])
        for row in range(tile_y):
            start = (row + 1) * block
            edge = start + slab_x
            here = press[start:edge, :]
            above = press[start + block : edge + block, :]
            below = press[start - block : edge - block, :]
            slopes = [
                slope_x(here, press[edge : edge + 1, :], press[edge + 1 : edge + 2, :]),
                0.5 * (above - below),
                slope_z(here, 1.0),
            ]
            for part in range(3):
                value = interim[row][part] - slopes[part]
                if step == STEPS - 1:
                    vel_out[part, pl.ds(row, slab_x, stride=tile_y), :] = value
                else:
                    wide[step + 1, part, 2 + row, own_x, :] = value
        if step < STEPS - 1:
            halo = start_halo(step + 1)
            pending.append(halo)

    results[0].start()
    for step, (copies, sends) in enumerate(pending):
        for copy in copies:
            copy.wait_send()

        @pl.when(sec == root)
        def _(sends=sends):
            for send in sends:
                send.wait_send()

        @pl.when(is_owner)
        def _(step=step):
            most = coeffs.at[step, pl.ds(0, (owners - 1) * ROWS), :]
            pltpu.make_async_copy(most, most, mode_send.at[step]).wait()
            some = plane_out.at[step, pl.ds(0, sec_count - 1)]
            pltpu.make_async_copy(some, some, back_send.at[step]).wait()
            last = plane_out.at[step, sec_count - 1, pl.ds(0, group - ROWS), :]
            pltpu.make_async_copy(last, last, back_send.at[step]).wait()

        @pl.when(jnp.logical_not(is_owner))
        def _(step=step):
            pltpu.make_async_copy(coeffs.at[step], coeffs.at[step], mode_send.at[step]).wait()

    for result in results:
        result.wait()


def hand_over(vel_from, tend_from, vel_to, tend_to, sems):
    copies = [
        pltpu.make_async_copy(vel_from, vel_to, sems.at[0]),
        pltpu.make_async_copy(tend_from, tend_to, sems.at[1]),
    ]
    for copy in copies:
        copy.start()
    for copy in copies:
        copy.wait()


def direct(sec_count, tile_count, velocity, prev_tendency, disk_cells, disk_kind, rotor_weights):
    _, slab_x, tile_y, depth_z = velocity.shape
    constants = [
        jnp.asarray(table) for table in tables(sec_count, tile_count, slab_x, tile_y, depth_z)
    ]
    wide_x = constants[5].shape[1]
    full_y = tile_y * tile_count
    group = tile_count * ROWS
    flat = (3, slab_x * tile_y, depth_z)
    hbm = pl.BlockSpec(memory_space=pltpu.HBM)
    operands = [
        velocity.reshape(flat),
        prev_tendency.reshape(flat),
        disk_cells.reshape(1, -1),
        disk_kind.reshape(1, -1),
        *constants,
    ]
    smem = pl.BlockSpec(memory_space=pltpu.SMEM)
    dma = pltpu.SemaphoreType.DMA
    outs = pl.pallas_call(
        functools.partial(step_kernel, sec_count, tile_count, slab_x, tile_y, depth_z),
        out_shape=[jax.ShapeDtypeStruct(flat, jnp.float32)] * 2,
        in_specs=[hbm] * 4 + [smem] + [hbm] * len(constants),
        out_specs=[hbm] * 2,
        scratch_shapes=[
            pltpu.VMEM((STEPS, 3, tile_y + 4, slab_x + 2 * ROWS, depth_z), jnp.float32),
            pltpu.VMEM((STEPS, 3, tile_y, slab_x, depth_z), jnp.float32),
            pltpu.VMEM((LANES, depth_z), jnp.float32),
            pltpu.VMEM((STEPS, depth_z, LANES), jnp.float32),
            pltpu.VMEM((STEPS, sec_count, group, LANES), jnp.float32),
            pltpu.VMEM((STEPS, sec_count, group, LANES), jnp.float32),
            pltpu.VMEM((STEPS, depth_z, LANES), jnp.float32),
            pltpu.VMEM((LANES, depth_z), jnp.float32),
            pltpu.VMEM((tile_y * slab_x, depth_z), jnp.float32),
            pltpu.VMEM((full_y * ROWS, wide_x), jnp.float32),
            *[pltpu.VMEM(operand.shape, operand.dtype) for operand in operands],
            pltpu.VMEM(flat, jnp.float32),
            pltpu.VMEM(flat, jnp.float32),
            dma((len(operands),)),
            dma((2,)),
            dma((STEPS, 8)),
            dma((STEPS, 8)),
            dma((STEPS, 4)),
            dma((STEPS,)),
            dma((STEPS,)),
            dma((STEPS,)),
            dma((STEPS,)),
            dma((STEPS,)),
        ],
        compiler_params=pltpu.CompilerParams(
            collective_id=0, has_side_effects=True, vmem_limit_bytes=63 * 1024 * 1024
        ),
        name="les_steps",
    )(*operands[:4], rotor_weights, *operands[4:])
    outs = pl.pallas_call(
        hand_over,
        out_shape=[jax.ShapeDtypeStruct(flat, jnp.float32)] * 2,
        in_specs=[hbm] * 2,
        out_specs=[hbm] * 2,
        scratch_shapes=[dma((2,))],
        name="hand_over",
    )(*outs)
    return tuple(out.reshape(velocity.shape) for out in outs)


def solution(mesh):
    sec_count, tile_count = mesh.shape["sec"], mesh.shape["tile"]
    in_specs = (
        P(None, "sec", "tile", None),
        P(None, "sec", "tile", None),
        P("sec", "tile", None),
        P("sec", "tile", None),
        P(),
    )
    out_specs = (P(None, "sec", "tile", None), P(None, "sec", "tile", None))

    def pick(velocity, *others):
        _, slab_x, tile_y, depth_z = velocity.shape
        owners = depth_z // ROWS
        fits = (
            owners <= sec_count * tile_count
            and owners % sec_count == 0
            and sec_count * (slab_x + ROWS) <= LANES
            and depth_z % LANES == 0
            and slab_x % ROWS == 0
            and tile_y >= 2
            and (tile_y + 2) * (slab_x + ROWS) <= LANES
            and tile_y * tile_count * ROWS <= 512
            and sec_count >= 3
            and tile_count >= 3
        )
        if fits:
            return direct(sec_count, tile_count, velocity, *others)
        return local(velocity, *others)

    return jax.shard_map(pick, mesh=mesh, in_specs=in_specs, out_specs=out_specs, check_vma=False)
```

```python
import functools
import math

import jax
import jax.numpy as jnp
import numpy as np
from jax import lax
from jax.experimental import pallas as pl
from jax.experimental.pallas import tpu as pltpu
from jax.sharding import PartitionSpec as P

STEPS = 2
KINDS = 16
ROWS = 8
LANES = 128
EDGE = 3
MESH = pl.DeviceIdType.MESH

precise = lax.Precision.HIGHEST
time_step = 0.1
fringe_rate = 2.0
smag_coef = 0.04


def extended_2(block, sides, width):
    for axis, dim in sides:
        count = lax.axis_size(axis)
        forward = [(i, i + 1) for i in range(count - 1)]
        forward.append((count - 1, 0))
        backward = [(target, source) for source, target in forward]
        low = lax.ppermute(
            lax.slice_in_dim(block, block.shape[dim] - width, None, axis=dim), axis, forward
        )
        high = lax.ppermute(lax.slice_in_dim(block, 0, width, axis=dim), axis, backward)
        block = jnp.concatenate([low, block, high], axis=dim)
    return block


def from_root(block, axis, owner):
    block = jnp.where(lax.axis_index(axis) == owner, block, jnp.zeros_like(block))
    return lax.psum(block, axis)


def gradients(padded, z_sign):
    centre = padded[:, 1:-1, 1:-1, :]
    grad_x = 0.5 * (padded[:, 2:, 1:-1, :] - padded[:, :-2, 1:-1, :])
    grad_y = 0.5 * (padded[:, 1:-1, 2:, :] - padded[:, 1:-1, :-2, :])
    extended = jnp.concatenate(
        [z_sign * centre[..., :1], centre, z_sign * centre[..., -1:]], axis=-1
    )
    grad_z = 0.5 * (extended[..., 2:] - extended[..., :-2])
    return (grad_x, grad_y, grad_z)


def strain_stress(slopes):

    def strain(first, second):
        return 0.5 * (slopes[second][first] + slopes[first][second])

    strain_xx = strain(0, 0)
    strain_yy = strain(1, 1)
    strain_zz = strain(2, 2)
    strain_xy = strain(0, 1)
    strain_xz = strain(0, 2)
    strain_yz = strain(1, 2)
    squared = strain_xx * strain_xx + strain_yy * strain_yy + strain_zz * strain_zz
    squared = squared + 2.0 * (
        strain_xy * strain_xy + strain_xz * strain_xz + strain_yz * strain_yz
    )
    double = 2.0 * (smag_coef * jnp.sqrt(2.0 * squared + 0.01))
    return jnp.stack(
        [
            double * strain_xx,
            double * strain_yy,
            double * strain_zz,
            double * strain_xy,
            double * strain_xz,
            double * strain_yz,
        ]
    )


def advection(slopes, centre):
    return centre[0:1] * slopes[0] + centre[1:2] * slopes[1] + centre[2:3] * slopes[2]


def stress_force(padded):
    grad_x, grad_y, grad_z = gradients(padded, 0.0)
    return jnp.stack(
        [
            grad_x[0] + grad_y[3] + grad_z[4],
            grad_x[3] + grad_y[1] + grad_z[5],
            grad_x[4] + grad_y[5] + grad_z[2],
        ]
    )


def faces(source):
    return extended_2(source, (("sec", 1), ("tile", 2)), 1)


def sec_turn(blocks):
    return lax.all_to_all(blocks, "sec", split_axis=0, concat_axis=0, tiled=True)


def tile_turn(blocks):
    return lax.all_to_all(blocks, "tile", split_axis=0, concat_axis=0, tiled=True)


def hartley_table(length):
    index_row = jnp.arange(length)
    product = index_row[:, None] * index_row[None, :] % length
    angle = 2.0 * math.pi / length * product.astype(jnp.float32)
    return jnp.cos(angle) + jnp.sin(angle)


def local(velocity, prev_tendency, disk_cells, disk_kind, rotor_weights):
    sec_count = lax.axis_size("sec")
    tile_count = lax.axis_size("tile")
    sec_at = lax.axis_index("sec")
    tile_at = lax.axis_index("tile")
    slab_x = velocity.shape[1]
    tile_y = velocity.shape[2]
    depth_z = velocity.shape[3]
    full_x = slab_x * sec_count
    full_y = tile_y * tile_count
    part_z = depth_z // sec_count
    modes_each = slab_x * depth_z // tile_count
    cell_count = slab_x * tile_y * depth_z
    modes = jnp.arange(depth_z).astype(jnp.float32)[:, None]
    points = jnp.arange(depth_z).astype(jnp.float32)[None, :] + 0.5
    cos_blocks = jnp.cos(math.pi * modes * points / depth_z).reshape(sec_count, part_z, depth_z)
    weight_blocks = jnp.where(jnp.arange(depth_z) == 0, 1.0 / depth_z, 2.0 / depth_z).astype(
        jnp.float32
    )
    weight_blocks = weight_blocks.reshape(sec_count, part_z)
    x_table = hartley_table(full_x)
    y_table = hartley_table(full_y).reshape(full_y, tile_count, tile_y)
    flat_ids = tile_at * modes_each + jnp.arange(modes_each)
    mode_x = flat_ids // part_z
    mode_z = sec_at * part_z + flat_ids % part_z
    mode_y = jnp.arange(full_y)
    sin_x = jnp.sin(2.0 * math.pi * mode_x.astype(jnp.float32) / full_x)
    sin_y = jnp.sin(2.0 * math.pi * mode_y.astype(jnp.float32) / full_y)
    sin_z = jnp.sin(math.pi * mode_z.astype(jnp.float32) / depth_z)
    eigen = -((sin_x * sin_x)[:, None] + (sin_y * sin_y)[None, :] + (sin_z * sin_z)[:, None])
    zero_mode = (
        (mode_x % (full_x // 2) == 0)[:, None]
        & (mode_y % (full_y // 2) == 0)[None, :]
        & (mode_z == 0)[:, None]
    )
    recip = jnp.where(zero_mode, 0.0, 1.0 / jnp.where(zero_mode, 1.0, eigen))
    slab_pos = jnp.sin(math.pi * (jnp.arange(slab_x).astype(jnp.float32) + 0.5) / slab_x)
    lam_x = fringe_rate * (slab_pos * slab_pos)
    flag = (
        (sec_at == 0)
        | (sec_at == sec_count // 2)
        | (sec_at == 3 * sec_count // 4)
        | (sec_at == sec_count - 1)
    ).astype(jnp.float32)
    picked = disk_cells.reshape(-1)
    kinds = disk_kind.reshape(-1)
    live = picked < cell_count
    safe = jnp.minimum(picked, cell_count - 1)
    weight = jnp.sum(
        jnp.where(kinds[:, None] == jnp.arange(KINDS)[None, :], rotor_weights[None, :], 0.0), axis=1
    )
    current = velocity
    tendency_old = prev_tendency
    tendency = prev_tendency
    for step_no in range(STEPS):
        wide = extended_2(current, (("sec", 1), ("tile", 2)), 2)
        wide_slopes = gradients(wide, -1.0)
        push_field = stress_force(strain_stress(wide_slopes))
        slopes = tuple((piece[:, 1:-1, 1:-1, :] for piece in wide_slopes))
        advect = advection(slopes, current)
        target = from_root(current, "sec", sec_count // 2 - 1)
        fringe = flag * lam_x[None, :, None, None] * (target - current)
        sampled = current[0].reshape(-1)[safe]
        push = jnp.where(live, -(weight * sampled * jnp.abs(sampled)), 0.0)
        turbine = (
            jnp.zeros((cell_count,), jnp.float32)
            .at[safe]
            .add(push)
            .reshape(slab_x, tile_y, depth_z)
        )
        empty = jnp.zeros_like(turbine)
        tendency = push_field - advect + jnp.stack([turbine, empty, empty]) + fringe
        interim = current + time_step * (1.5 * tendency - 0.5 * tendency_old)
        grad_x, grad_y, grad_z = gradients(faces(interim), -1.0)
        rhs = grad_x[0] + grad_y[1] + grad_z[2]
        coeffs = jnp.einsum("xyz,bcz->bxyc", rhs, cos_blocks, precision=precise)
        gathered = sec_turn(coeffs).reshape(full_x, tile_y, part_z)
        along_x = jnp.einsum("xyc,kx->kcy", gathered, x_table, precision=precise)
        spread = tile_turn(along_x.reshape(tile_count, modes_each, tile_y))
        along_y = jnp.einsum("sqt,lst->ql", spread, y_table, precision=precise)
        scaled = along_y * recip
        back_y = jnp.einsum("ql,lst->sqt", scaled, y_table, precision=precise) / (full_x * full_y)
        returned = tile_turn(back_y).reshape(full_x, part_z, tile_y)
        back_x = jnp.einsum("kcy,kx->xyc", returned, x_table, precision=precise)
        home = sec_turn(back_x.reshape(sec_count, slab_x, tile_y, part_z))
        pressure = jnp.einsum(
            "bxyc,bcz->xyz", home * weight_blocks[:, None, None, :], cos_blocks, precision=precise
        )
        press_x, press_y, press_z = gradients(faces(pressure[None]), 1.0)
        current = interim - jnp.concatenate([press_x, press_y, press_z], axis=0)
        tendency_old = tendency
    return (current, tendency)


def cas_table(first, second, length):
    angle = 2.0 * np.pi / length * (np.outer(first, second) % length)
    return np.cos(angle) + np.sin(angle)


def halves(table):
    high = table.astype(np.float32).astype(jnp.bfloat16)
    low = (table - high.astype(np.float64)).astype(np.float32).astype(jnp.bfloat16)
    stacked = np.concatenate([high, low], axis=0)
    return np.concatenate(np.split(stacked, stacked.shape[1] // LANES, axis=1), axis=0)


def whole(table, columns):
    count = table.shape[0] * LANES // columns
    parts = [table[i * count : (i + 1) * count] for i in range(columns // LANES)]
    return jnp.concatenate(parts, axis=1)


def tables(sec_count, tile_count, slab_x, tile_y, depth_z):
    full_x, full_y = slab_x * sec_count, tile_y * tile_count
    wide_x = -(-full_x // LANES) * LANES
    planes, block = tile_y + 2, slab_x + ROWS
    z_at = np.arange(depth_z)
    cos_z = np.cos(np.pi / depth_z * np.outer(z_at, z_at + 0.5))
    x_cas = np.zeros((LANES, wide_x))
    x_back = np.zeros((LANES, wide_x))
    for sec in range(sec_count):
        start = sec * slab_x
        cells = np.concatenate([start + np.arange(slab_x), [start - 1, start + slab_x]]) % full_x
        x_cas[sec * block : sec * block + slab_x + 2, :full_x] = cas_table(
            cells, np.arange(full_x), full_x
        )
        cells = np.arange(start - EDGE, start + slab_x + EDGE) % full_x
        x_back[sec * block : sec * block + slab_x + 2 * EDGE, :full_x] = cas_table(
            cells, np.arange(full_x), full_x
        )
    y_blocks = []
    for plane in range(1 - EDGE, planes + EDGE - 1):
        y_at = (np.arange(tile_count) * tile_y + plane - 1) % full_y
        y_blocks.append(np.kron(cas_table(np.arange(full_y), y_at, full_y), np.eye(ROWS)))
    y_cas = np.concatenate(y_blocks[EDGE - 1 : EDGE - 1 + planes], axis=1)
    y_back = np.concatenate(y_blocks, axis=1).T
    k_x, k_y = np.arange(full_x), np.arange(full_y)
    sin_x = np.where(k_x % (full_x // 2) == 0, 0.0, np.sin(2.0 * np.pi * k_x / full_x) ** 2)
    sin_y = np.where(k_y % (full_y // 2) == 0, 0.0, np.sin(2.0 * np.pi * k_y / full_y) ** 2)
    sin_xy = np.ones((full_y * ROWS, wide_x), np.float32)
    sin_xy[:, :full_x] = np.repeat(sin_y, ROWS)[:, None] + sin_x[None, :]
    sin_z = np.sin(np.pi * z_at / depth_z) ** 2
    weight_z = -np.where(z_at == 0, 1.0, 2.0) / (depth_z * full_x * full_y)
    mode_z = np.stack([sin_z, weight_z]).astype(np.float32)
    mode_z = np.ascontiguousarray(np.broadcast_to(mode_z[:, :, None], (2, depth_z, wide_x)))
    lam = fringe_rate * np.sin(np.pi * (np.arange(slab_x) + 0.5) / slab_x) ** 2
    lam = np.ascontiguousarray(np.broadcast_to(lam.astype(np.float32)[:, None], (slab_x, depth_z)))
    return (
        halves(cos_z),
        halves(x_cas),
        halves(x_back.T),
        halves(y_cas),
        halves(y_back),
        sin_xy,
        mode_z,
        lam,
    )


def split(value):
    high = value.astype(jnp.bfloat16)
    return high, (value - high.astype(jnp.float32)).astype(jnp.bfloat16)


def dot(first, second, dims):
    return lax.dot_general(first, second, (dims, ((), ())), preferred_element_type=jnp.float32)


def table_first(table, second, dims):
    count = table.shape[0] // 2
    high, low = split(second)
    both = dot(table, high, dims)
    return both[:count] + (both[count:] + dot(table[:count], low, dims))


def table_second(first, table):
    count, depth = first.shape[0], table.shape[0] // 2
    high, low = split(first)
    both = dot(jnp.concatenate([high, low], axis=0), table[:depth], NN)
    return both[:count] + (both[count:] + dot(high, table[depth:], NN))


NN = ((1,), (0,))
NT = ((1,), (1,))


def slope_z(value, z_sign):
    depth = value.shape[1]
    lane = lax.broadcasted_iota(jnp.int32, value.shape, 1)
    edge = value * z_sign
    above = jnp.where(lane == depth - 1, edge, pltpu.roll(value, depth - 1, 1))
    below = jnp.where(lane == 0, edge, pltpu.roll(value, 1, 1))
    return 0.5 * (above - below)


def slope_x(value, low=None, high=None):
    count = value.shape[0]
    after = pltpu.roll(value, count - 1, 0)
    before = pltpu.roll(value, 1, 0)
    if low is not None:
        row = lax.broadcasted_iota(jnp.int32, value.shape, 0)
        after = jnp.where(row == count - 1, high, after)
        before = jnp.where(row == 0, low, before)
    return 0.5 * (after - before)


def step_kernel(
    sec_count,
    tile_count,
    slab_x,
    tile_y,
    depth_z,
    vel_hbm,
    old_hbm,
    cells_hbm,
    kinds_hbm,
    weights_ref,
    cos_hbm,
    x_hbm,
    xt_hbm,
    y_hbm,
    yt_hbm,
    sin_xy_hbm,
    mode_z_hbm,
    lam_hbm,
    vel_result,
    tend_result,
    wide,
    target,
    share,
    coeffs,
    plane_in,
    wide_out,
    last_out,
    wide_returned,
    last_returned,
    press,
    thrust,
    recip,
    vel_ref,
    old_ref,
    cells_ref,
    kinds_ref,
    cos_ref,
    x_ref,
    xt_ref,
    y_ref,
    yt_ref,
    sin_xy_ref,
    mode_z_ref,
    lam_ref,
    vel_out,
    tend_out,
    load_sem,
    result_sem,
    halo_send,
    halo_recv,
    target_send,
    target_recv,
    mode_send,
    mode_recv,
    back_send,
    back_recv,
):
    sec = lax.axis_index("sec")
    tile = lax.axis_index("tile")
    devices = sec_count * tile_count
    me = tile * sec_count + sec
    owners = depth_z // ROWS
    planes = tile_y + 2
    deep = tile_y + 4
    group = tile_count * ROWS
    block = slab_x + ROWS
    root = sec_count // 2 - 1
    fringes = sorted({0, sec_count // 2, 3 * sec_count // 4, sec_count - 1} - {root})
    first_tile = (tile_count - owners // sec_count) // 2
    is_owner = (tile >= first_tile) & (tile < first_tile + owners // sec_count)
    owner_at = (tile - first_tile) * sec_count + sec
    in_fringe = functools.reduce(jnp.logical_or, [sec == which for which in fringes])
    low_sec, high_sec = lax.rem(sec + sec_count - 1, sec_count), lax.rem(sec + 1, sec_count)
    low_tile, high_tile = lax.rem(tile + tile_count - 1, tile_count), lax.rem(tile + 1, tile_count)
    end_x = ROWS + slab_x
    own_x, own_y = slice(ROWS, end_x), slice(2, 2 + tile_y)

    loads = [
        pltpu.make_async_copy(source, held, load_sem.at[place])
        for place, (source, held) in enumerate(
            (
                (vel_hbm, vel_ref),
                (cells_hbm, cells_ref),
                (kinds_hbm, kinds_ref),
                (sin_xy_hbm, sin_xy_ref),
                (mode_z_hbm, mode_z_ref),
                (old_hbm, old_ref),
                (lam_hbm, lam_ref),
                (cos_hbm, cos_ref),
                (y_hbm, y_ref),
                (x_hbm, x_ref),
                (xt_hbm, xt_ref),
                (yt_hbm, yt_ref),
            )
        )
    ]
    for load in loads:
        load.start()

    results = [
        pltpu.make_async_copy(vel_out, vel_result, result_sem.at[0]),
        pltpu.make_async_copy(tend_out, tend_result, result_sem.at[1]),
    ]

    barrier = pltpu.get_barrier_semaphore()

    def greet(ahead, carry):
        other = lax.rem(me + ahead, devices)
        pl.semaphore_signal(
            barrier,
            inc=1,
            device_id=(lax.rem(other, sec_count), lax.div(other, sec_count)),
            device_id_type=MESH,
        )
        return carry

    lax.fori_loop(1, devices, greet, 0)

    share[...] = jnp.zeros_like(share)
    loads[0].wait()
    for part in range(3):
        for row in range(tile_y):
            wide[0, part, 2 + row, own_x, :] = vel_ref[part, pl.ds(row, slab_x, stride=tile_y), :]

    pl.semaphore_wait(barrier, devices - 1)

    def start_halo(step):
        xs = {
            -1: (low_sec, slice(ROWS, 2 * ROWS), slice(end_x, end_x + ROWS)),
            0: (sec, own_x, own_x),
            1: (high_sec, slice(end_x - ROWS, end_x), slice(0, ROWS)),
        }
        ys = {
            -1: (low_tile, slice(2, 4), slice(2 + tile_y, deep)),
            0: (tile, own_y, own_y),
            1: (high_tile, slice(tile_y, 2 + tile_y), slice(0, 2)),
        }
        copies = []
        for x_way in (-1, 0, 1):
            for y_way in (-1, 0, 1):
                if x_way == 0 and y_way == 0:
                    continue
                slot = len(copies)
                to_sec, x_from, x_to = xs[x_way]
                to_tile, y_from, y_to = ys[y_way]
                if x_way != 0 and y_way == -1:
                    y_from, y_to = slice(2, 3), slice(2 + tile_y, 3 + tile_y)
                if x_way != 0 and y_way == 1:
                    y_from, y_to = slice(1 + tile_y, 2 + tile_y), slice(1, 2)
                copy = pltpu.make_async_remote_copy(
                    src_ref=wide.at[step, :, y_from, x_from, :],
                    dst_ref=wide.at[step, :, y_to, x_to, :],
                    send_sem=halo_send.at[step, slot],
                    recv_sem=halo_recv.at[step, slot],
                    device_id=(to_sec, to_tile),
                    device_id_type=MESH,
                )
                copies.append(copy)
        for copy in copies:
            copy.start()
        return copies

    def start_target(step):
        sends = [
            pltpu.make_async_remote_copy(
                src_ref=wide.at[step, :, own_y, own_x, :],
                dst_ref=target.at[step],
                send_sem=target_send.at[step, place],
                recv_sem=target_recv.at[step],
                device_id=(which, tile),
                device_id_type=MESH,
            )
            for place, which in enumerate(fringes)
        ]

        @pl.when(sec == root)
        def _():
            for send in sends:
                send.start()

        return sends

    halos = {0: start_halo(0)}
    targets = {0: start_target(0)}

    for load in loads[1:5]:
        load.wait()
    cells = cells_ref[...]
    kinds = kinds_ref[...]
    weight = jnp.zeros(cells.shape, jnp.float32)
    for kind in range(KINDS):
        weight = jnp.where(kinds == kind, weights_ref[kind], weight)
    weight = jnp.where(cells < slab_x * tile_y * depth_z, weight, 0.0)
    column = lax.div(cells, depth_z)
    row_of = lax.rem(column, tile_y) * slab_x + lax.div(column, tile_y)
    slots = cells.shape[1]
    hit_row = lax.broadcasted_iota(jnp.int32, (tile_y * slab_x, slots), 0) == row_of
    hit_z = lax.broadcasted_iota(jnp.int32, (depth_z, slots), 0) == lax.rem(cells, depth_z)
    hit_z = hit_z.astype(jnp.float32).astype(jnp.bfloat16)
    rest = jnp.where(hit_row, weight, 0.0)
    summed = jnp.zeros((tile_y * slab_x, depth_z), jnp.float32)
    for _ in range(3):
        piece, rest_next = rest.astype(jnp.bfloat16), None
        rest_next = rest - piece.astype(jnp.float32)
        summed = summed + lax.dot_general(
            piece, hit_z, (NT, ((), ())), preferred_element_type=jnp.float32
        )
        rest = rest_next
    thrust[...] = summed

    @pl.when(is_owner)
    def _():
        rows = pl.ds(pl.multiple_of(owner_at * ROWS, ROWS), ROWS)
        full_y = tile_y * tile_count
        sum_sin = sin_xy_ref[...] + jnp.concatenate([mode_z_ref[0, rows, :]] * full_y, axis=0)
        scale = jnp.concatenate([mode_z_ref[1, rows, :]] * full_y, axis=0)
        zero_mode = sum_sin == 0.0
        recip[...] = jnp.where(zero_mode, 0.0, scale / jnp.where(zero_mode, 1.0, sum_sin))

    for load in loads[5:]:
        load.wait()
    old = [
        [old_ref[part, pl.ds(row, slab_x, stride=tile_y), :] for row in range(tile_y)]
        for part in range(3)
    ]

    for step in range(STEPS):
        if step == 0:
            for copy in halos[0]:
                copy.wait_recv()

        centre, stress, advect = {}, {}, {}
        for plane in range(1, deep - 1):
            here = [wide[step, part, plane] for part in range(3)]
            d_x = [slope_x(value) for value in here]
            d_y = [
                0.5 * (wide[step, part, plane + 1] - wide[step, part, plane - 1])
                for part in range(3)
            ]
            d_z = [slope_z(value, -1.0) for value in here]
            s_xx, s_yy, s_zz = d_x[0], d_y[1], d_z[2]
            s_xy = 0.5 * (d_x[1] + d_y[0])
            s_xz = 0.5 * (d_x[2] + d_z[0])
            s_yz = 0.5 * (d_y[2] + d_z[1])
            squared = s_xx * s_xx + s_yy * s_yy + s_zz * s_zz
            squared = squared + 2.0 * (s_xy * s_xy + s_xz * s_xz + s_yz * s_yz)
            double = (2.0 * smag_coef) * jnp.sqrt(2.0 * squared + 0.01)
            stress[plane] = [double * s for s in (s_xx, s_yy, s_zz, s_xy, s_xz, s_yz)]
            centre[plane] = here
            advect[plane] = [
                here[0] * d_x[part] + here[1] * d_y[part] + here[2] * d_z[part]
                for part in range(3)
            ]

        @pl.when(in_fringe)
        def _(step=step):
            pltpu.make_async_copy(target.at[step], target.at[step], target_recv.at[step]).wait()

        @pl.when(jnp.logical_not(in_fringe))
        def _(step=step):
            target[step] = wide[step, :, own_y, own_x, :]

        interim, tendency = [], []
        for row in range(tile_y):
            plane = 2 + row
            xx, yy, zz, xy, xz, yz = stress[plane]
            before, after = stress[plane - 1], stress[plane + 1]
            push = [
                slope_x(xx) + 0.5 * (after[3] - before[3]) + slope_z(xz, 0.0),
                slope_x(xy) + 0.5 * (after[1] - before[1]) + slope_z(yz, 0.0),
                slope_x(xz) + 0.5 * (after[5] - before[5]) + slope_z(zz, 0.0),
            ]
            lam = lam_ref[...]
            tend, mid = [], []
            for part in range(3):
                here = centre[plane][part][own_x]
                total = (push[part] - advect[plane][part])[own_x]
                if part == 0:
                    force = thrust[row * slab_x : (row + 1) * slab_x, :]
                    total = total - force * here * jnp.abs(here)
                total = total + lam * (target[step, part, row] - here)
                tend.append(total)
                mid.append(here + time_step * (1.5 * total - 0.5 * old[part][row]))
                if step == STEPS - 1:
                    tend_out[part, pl.ds(row, slab_x, stride=tile_y), :] = total
            tendency.append(tend)
            interim.append(mid)
        if step == STEPS - 1:
            results[1].start()
        old = [[tendency[row][part] for row in range(tile_y)] for part in range(3)]

        share[0:slab_x, :] = 0.5 * interim[0][1]
        last = (planes - 1) * block
        share[last : last + slab_x, :] = -0.5 * interim[tile_y - 1][1]
        for row in range(tile_y):
            along_x, _, along_z = interim[row]
            total = slope_x(along_x, 0.0, 0.0) + slope_z(along_z, -1.0)
            if row + 1 < tile_y:
                total = total + 0.5 * interim[row + 1][1]
            if row > 0:
                total = total - 0.5 * interim[row - 1][1]
            start = (row + 1) * block
            edge = start + slab_x
            share[start:edge, :] = total
            share[edge : edge + 1, :] = 0.5 * along_x[0:1]
            share[edge + 1 : edge + 2, :] = -0.5 * along_x[slab_x - 1 : slab_x]
        coeffs[step] = table_first(cos_ref[...], share[...], NT)

        my_rows = pl.ds(pl.multiple_of(tile * ROWS, ROWS), ROWS)

        def send_modes(ahead, carry, step=step):
            owner = lax.rem(me + ahead, owners)
            flat = owner + first_tile * sec_count
            rows = pl.ds(pl.multiple_of(owner * ROWS, ROWS), ROWS)

            @pl.when(flat == me)
            def _():
                pltpu.make_async_copy(
                    coeffs.at[step, rows, :], plane_in.at[step, sec, my_rows, :], mode_recv.at[step]
                ).start()

            @pl.when(flat != me)
            def _():
                pltpu.make_async_remote_copy(
                    src_ref=coeffs.at[step, rows, :],
                    dst_ref=plane_in.at[step, sec, my_rows, :],
                    send_sem=mode_send.at[step],
                    recv_sem=mode_recv.at[step],
                    device_id=(lax.rem(flat, sec_count), lax.div(flat, sec_count)),
                    device_id_type=MESH,
                ).start()

            return carry

        lax.fori_loop(0, owners, send_modes, 0)
        final = step == STEPS - 1
        if not final:
            for part in range(3):
                for row in range(tile_y):
                    wide[step + 1, part, 2 + row, own_x, :] = interim[row][part]
            halos[step + 1] = start_halo(step + 1)
        reach = 1 if final else EDGE
        plane_out, returned = (last_out, last_returned) if final else (wide_out, wide_returned)
        per_tile = LANES // block
        back_planes = tile_y + 2 * reach

        @pl.when(is_owner)
        def _(step=step):
            pltpu.make_async_copy(
                plane_in.at[step], plane_in.at[step], mode_recv.at[step]
            ).wait()
            lane_block = lax.broadcasted_iota(jnp.int32, (group, LANES), 1) // block
            arrived = [plane_in[step, part] for part in range(sec_count)]
            blocks = []
            for plane in range(planes):
                piece = pltpu.roll(arrived[0], -plane * block % LANES, 1)
                for part in range(1, sec_count):
                    other = pltpu.roll(arrived[part], (part - plane) * block % LANES, 1)
                    piece = jnp.where(lane_block == part, other, piece)
                blocks.append(piece)
            stacked = jnp.concatenate(blocks, axis=0)
            modes = table_second(table_first(whole(y_ref[...], planes * group), stacked, NN), whole(x_ref[...], recip.shape[1])) * recip[...]
            skip = (EDGE - reach) * group
            kept = back_planes * group
            back_table = yt_ref[...]
            half = back_table.shape[0] // 2
            back_table = jnp.concatenate(
                [back_table[skip : skip + kept], back_table[half + skip : half + skip + kept]], axis=0
            )
            back_x = table_second(modes, whole(xt_ref[...], LANES))
            spread = table_first(back_table, back_x, NN)
            for part in range(sec_count):
                for first in range(0, back_planes, per_tile):
                    piece = None
                    for place in range(min(per_tile, back_planes - first)):
                        start = (first + place) * group
                        other = spread[start : start + group]
                        other = pltpu.roll(other, (place - part) * block % LANES, 1)
                        piece = other if piece is None else jnp.where(lane_block == place, other, piece)
                    lanes = slice(first // per_tile * LANES, (first // per_tile + 1) * LANES)
                    plane_out[part, :, lanes] = piece
            rows = pl.ds(pl.multiple_of(owner_at * ROWS, ROWS), ROWS)

            pltpu.make_async_copy(
                plane_out.at[sec, my_rows, :], returned.at[rows, :], back_recv.at[step]
            ).start()

            def send_back(ahead, carry):
                other = lax.rem(me + ahead, devices)
                to_sec, to_tile = lax.rem(other, sec_count), lax.div(other, sec_count)
                pltpu.make_async_remote_copy(
                    src_ref=plane_out.at[
                        to_sec, pl.ds(pl.multiple_of(to_tile * ROWS, ROWS), ROWS), :
                    ],
                    dst_ref=returned.at[rows, :],
                    send_sem=back_send.at[step],
                    recv_sem=back_recv.at[step],
                    device_id=(to_sec, to_tile),
                    device_id_type=MESH,
                ).start()
                return carry

            lax.fori_loop(1, devices, send_back, 0)

        pltpu.make_async_copy(returned, returned, back_recv.at[step]).wait()
        columns = returned[...]
        columns = jnp.concatenate(
            [columns[:, i : i + LANES].T for i in range(0, columns.shape[1], LANES)], axis=0
        )
        press[0 : columns.shape[0], :] = table_second(columns, cos_ref[...])

        def press_slopes(start, count):
            here = press[start : start + count, :]
            above = press[start + block : start + block + count, :]
            below = press[start - block : start - block + count, :]
            return here, 0.5 * (above - below), slope_z(here, 1.0)

        if final:
            for row in range(tile_y):
                start = (row + 1) * block + EDGE
                here, along_y, along_z = press_slopes(start, slab_x)
                low = press[start - 1 : start, :]
                high = press[start + slab_x : start + slab_x + 1, :]
                slopes = [slope_x(here, low, high), along_y, along_z]
                for part in range(3):
                    vel_out[part, pl.ds(row, slab_x, stride=tile_y), :] = (
                        interim[row][part] - slopes[part]
                    )
        else:
            for copy in halos[step + 1]:
                copy.wait()
            span = slice(ROWS - EDGE, ROWS - EDGE + block)
            for plane in range(deep):
                here, along_y, along_z = press_slopes((plane + 1) * block, block)
                slopes = [slope_x(here), along_y, along_z]
                for part in range(3):
                    wide[step + 1, part, plane, span, :] = (
                        wide[step + 1, part, plane, span, :] - slopes[part]
                    )
            targets[step + 1] = start_target(step + 1)

    results[0].start()
    for copy in halos[0]:
        copy.wait_send()
    for step, sends in targets.items():
        plane_out = last_out if step == STEPS - 1 else wide_out

        @pl.when(sec == root)
        def _(sends=sends):
            for send in sends:
                send.wait_send()

        @pl.when(is_owner)
        def _(step=step, plane_out=plane_out):
            most = coeffs.at[step, pl.ds(0, (owners - 1) * ROWS), :]
            pltpu.make_async_copy(most, most, mode_send.at[step]).wait()
            some = plane_out.at[pl.ds(0, sec_count - 1)]
            pltpu.make_async_copy(some, some, back_send.at[step]).wait()
            last = plane_out.at[sec_count - 1, pl.ds(0, group - ROWS), :]
            pltpu.make_async_copy(last, last, back_send.at[step]).wait()

        @pl.when(jnp.logical_not(is_owner))
        def _(step=step):
            pltpu.make_async_copy(coeffs.at[step], coeffs.at[step], mode_send.at[step]).wait()

    for result in results:
        result.wait()


def hand_over(vel_from, tend_from, vel_to, tend_to):
    vel_to[...] = vel_from[...]
    tend_to[...] = tend_from[...]


def direct(sec_count, tile_count, velocity, prev_tendency, disk_cells, disk_kind, rotor_weights):
    _, slab_x, tile_y, depth_z = velocity.shape
    constants = [
        jnp.asarray(table) for table in tables(sec_count, tile_count, slab_x, tile_y, depth_z)
    ]
    wide_x = constants[5].shape[1]
    full_y = tile_y * tile_count
    group = tile_count * ROWS
    wide_lanes = (tile_y + 2 * EDGE) * (slab_x + ROWS)
    wide_lanes = -(-wide_lanes // LANES) * LANES
    flat = (3, slab_x * tile_y, depth_z)
    vmem = pl.BlockSpec(memory_space=pltpu.VMEM)
    hbm = pl.BlockSpec(memory_space=pltpu.HBM)
    operands = [
        velocity.reshape(flat),
        prev_tendency.reshape(flat),
        disk_cells.reshape(1, -1),
        disk_kind.reshape(1, -1),
        *constants,
    ]
    smem = pl.BlockSpec(memory_space=pltpu.SMEM)
    dma = pltpu.SemaphoreType.DMA
    outs = pl.pallas_call(
        functools.partial(step_kernel, sec_count, tile_count, slab_x, tile_y, depth_z),
        out_shape=[jax.ShapeDtypeStruct(flat, jnp.float32)] * 2,
        in_specs=[hbm] * 4 + [smem] + [hbm] * len(constants),
        out_specs=[hbm] * 2,
        scratch_shapes=[
            pltpu.VMEM((STEPS, 3, tile_y + 4, slab_x + 2 * ROWS, depth_z), jnp.float32),
            pltpu.VMEM((STEPS, 3, tile_y, slab_x, depth_z), jnp.float32),
            pltpu.VMEM((LANES, depth_z), jnp.float32),
            pltpu.VMEM((STEPS, depth_z, LANES), jnp.float32),
            pltpu.VMEM((STEPS, sec_count, group, LANES), jnp.float32),
            pltpu.VMEM((sec_count, group, wide_lanes), jnp.float32),
            pltpu.VMEM((sec_count, group, LANES), jnp.float32),
            pltpu.VMEM((depth_z, wide_lanes), jnp.float32),
            pltpu.VMEM((depth_z, LANES), jnp.float32),
            pltpu.VMEM((wide_lanes, depth_z), jnp.float32),
            pltpu.VMEM((tile_y * slab_x, depth_z), jnp.float32),
            pltpu.VMEM((full_y * ROWS, wide_x), jnp.float32),
            *[pltpu.VMEM(operand.shape, operand.dtype) for operand in operands],
            pltpu.VMEM(flat, jnp.float32),
            pltpu.VMEM(flat, jnp.float32),
            dma((len(operands),)),
            dma((2,)),
            dma((STEPS, 8)),
            dma((STEPS, 8)),
            dma((STEPS, 4)),
            dma((STEPS,)),
            dma((STEPS,)),
            dma((STEPS,)),
            dma((STEPS,)),
            dma((STEPS,)),
        ],
        compiler_params=pltpu.CompilerParams(
            collective_id=0, has_side_effects=True, vmem_limit_bytes=60 * 1024 * 1024
        ),
        name="les_steps",
    )(*operands[:4], rotor_weights, *operands[4:])
    outs = pl.pallas_call(
        hand_over,
        out_shape=[jax.ShapeDtypeStruct(flat, jnp.float32)] * 2,
        in_specs=[vmem] * 2,
        out_specs=[vmem] * 2,
        name="hand_over",
    )(*outs)
    return tuple(out.reshape(velocity.shape) for out in outs)


def solution(mesh):
    sec_count, tile_count = mesh.shape["sec"], mesh.shape["tile"]
    in_specs = (
        P(None, "sec", "tile", None),
        P(None, "sec", "tile", None),
        P("sec", "tile", None),
        P("sec", "tile", None),
        P(),
    )
    out_specs = (P(None, "sec", "tile", None), P(None, "sec", "tile", None))

    def pick(velocity, *others):
        _, slab_x, tile_y, depth_z = velocity.shape
        owners = depth_z // ROWS
        fits = (
            owners <= sec_count * tile_count
            and owners % sec_count == 0
            and sec_count * (slab_x + ROWS) <= LANES
            and LANES % (slab_x + ROWS) == 0
            and depth_z % LANES == 0
            and slab_x % ROWS == 0
            and tile_y >= 2
            and (tile_y + 2) * (slab_x + ROWS) <= LANES
            and tile_y * tile_count * ROWS <= 512
            and sec_count >= 3
            and tile_count >= 3
        )
        if fits:
            return direct(sec_count, tile_count, velocity, *others)
        return local(velocity, *others)

    return jax.shard_map(pick, mesh=mesh, in_specs=in_specs, out_specs=out_specs, check_vma=False)
```

```python
import functools
import math

import jax
import jax.numpy as jnp
import numpy as np
from jax import lax
from jax.experimental import pallas as pl
from jax.experimental.pallas import tpu as pltpu
from jax.sharding import PartitionSpec as P

STEPS = 2
KINDS = 16
ROWS = 8
LANES = 128
EDGE = 3
COPIES = 2
MESH = pl.DeviceIdType.MESH

precise = lax.Precision.HIGHEST
time_step = 0.1
fringe_rate = 2.0
smag_coef = 0.04


def extended_2(block, sides, width):
    for axis, dim in sides:
        count = lax.axis_size(axis)
        forward = [(i, i + 1) for i in range(count - 1)]
        forward.append((count - 1, 0))
        backward = [(target, source) for source, target in forward]
        low = lax.ppermute(
            lax.slice_in_dim(block, block.shape[dim] - width, None, axis=dim), axis, forward
        )
        high = lax.ppermute(lax.slice_in_dim(block, 0, width, axis=dim), axis, backward)
        block = jnp.concatenate([low, block, high], axis=dim)
    return block


def from_root(block, axis, owner):
    block = jnp.where(lax.axis_index(axis) == owner, block, jnp.zeros_like(block))
    return lax.psum(block, axis)


def gradients(padded, z_sign):
    centre = padded[:, 1:-1, 1:-1, :]
    grad_x = 0.5 * (padded[:, 2:, 1:-1, :] - padded[:, :-2, 1:-1, :])
    grad_y = 0.5 * (padded[:, 1:-1, 2:, :] - padded[:, 1:-1, :-2, :])
    extended = jnp.concatenate(
        [z_sign * centre[..., :1], centre, z_sign * centre[..., -1:]], axis=-1
    )
    grad_z = 0.5 * (extended[..., 2:] - extended[..., :-2])
    return (grad_x, grad_y, grad_z)


def strain_stress(slopes):

    def strain(first, second):
        return 0.5 * (slopes[second][first] + slopes[first][second])

    strain_xx = strain(0, 0)
    strain_yy = strain(1, 1)
    strain_zz = strain(2, 2)
    strain_xy = strain(0, 1)
    strain_xz = strain(0, 2)
    strain_yz = strain(1, 2)
    squared = strain_xx * strain_xx + strain_yy * strain_yy + strain_zz * strain_zz
    squared = squared + 2.0 * (
        strain_xy * strain_xy + strain_xz * strain_xz + strain_yz * strain_yz
    )
    double = 2.0 * (smag_coef * jnp.sqrt(2.0 * squared + 0.01))
    return jnp.stack(
        [
            double * strain_xx,
            double * strain_yy,
            double * strain_zz,
            double * strain_xy,
            double * strain_xz,
            double * strain_yz,
        ]
    )


def advection(slopes, centre):
    return centre[0:1] * slopes[0] + centre[1:2] * slopes[1] + centre[2:3] * slopes[2]


def stress_force(padded):
    grad_x, grad_y, grad_z = gradients(padded, 0.0)
    return jnp.stack(
        [
            grad_x[0] + grad_y[3] + grad_z[4],
            grad_x[3] + grad_y[1] + grad_z[5],
            grad_x[4] + grad_y[5] + grad_z[2],
        ]
    )


def faces(source):
    return extended_2(source, (("sec", 1), ("tile", 2)), 1)


def sec_turn(blocks):
    return lax.all_to_all(blocks, "sec", split_axis=0, concat_axis=0, tiled=True)


def tile_turn(blocks):
    return lax.all_to_all(blocks, "tile", split_axis=0, concat_axis=0, tiled=True)


def hartley_table(length):
    index_row = jnp.arange(length)
    product = index_row[:, None] * index_row[None, :] % length
    angle = 2.0 * math.pi / length * product.astype(jnp.float32)
    return jnp.cos(angle) + jnp.sin(angle)


def local(velocity, prev_tendency, disk_cells, disk_kind, rotor_weights):
    sec_count = lax.axis_size("sec")
    tile_count = lax.axis_size("tile")
    sec_at = lax.axis_index("sec")
    tile_at = lax.axis_index("tile")
    slab_x = velocity.shape[1]
    tile_y = velocity.shape[2]
    depth_z = velocity.shape[3]
    full_x = slab_x * sec_count
    full_y = tile_y * tile_count
    part_z = depth_z // sec_count
    modes_each = slab_x * depth_z // tile_count
    cell_count = slab_x * tile_y * depth_z
    modes = jnp.arange(depth_z).astype(jnp.float32)[:, None]
    points = jnp.arange(depth_z).astype(jnp.float32)[None, :] + 0.5
    cos_blocks = jnp.cos(math.pi * modes * points / depth_z).reshape(sec_count, part_z, depth_z)
    weight_blocks = jnp.where(jnp.arange(depth_z) == 0, 1.0 / depth_z, 2.0 / depth_z).astype(
        jnp.float32
    )
    weight_blocks = weight_blocks.reshape(sec_count, part_z)
    x_table = hartley_table(full_x)
    y_table = hartley_table(full_y).reshape(full_y, tile_count, tile_y)
    flat_ids = tile_at * modes_each + jnp.arange(modes_each)
    mode_x = flat_ids // part_z
    mode_z = sec_at * part_z + flat_ids % part_z
    mode_y = jnp.arange(full_y)
    sin_x = jnp.sin(2.0 * math.pi * mode_x.astype(jnp.float32) / full_x)
    sin_y = jnp.sin(2.0 * math.pi * mode_y.astype(jnp.float32) / full_y)
    sin_z = jnp.sin(math.pi * mode_z.astype(jnp.float32) / depth_z)
    eigen = -((sin_x * sin_x)[:, None] + (sin_y * sin_y)[None, :] + (sin_z * sin_z)[:, None])
    zero_mode = (
        (mode_x % (full_x // 2) == 0)[:, None]
        & (mode_y % (full_y // 2) == 0)[None, :]
        & (mode_z == 0)[:, None]
    )
    recip = jnp.where(zero_mode, 0.0, 1.0 / jnp.where(zero_mode, 1.0, eigen))
    slab_pos = jnp.sin(math.pi * (jnp.arange(slab_x).astype(jnp.float32) + 0.5) / slab_x)
    lam_x = fringe_rate * (slab_pos * slab_pos)
    flag = (
        (sec_at == 0)
        | (sec_at == sec_count // 2)
        | (sec_at == 3 * sec_count // 4)
        | (sec_at == sec_count - 1)
    ).astype(jnp.float32)
    picked = disk_cells.reshape(-1)
    kinds = disk_kind.reshape(-1)
    live = picked < cell_count
    safe = jnp.minimum(picked, cell_count - 1)
    weight = jnp.sum(
        jnp.where(kinds[:, None] == jnp.arange(KINDS)[None, :], rotor_weights[None, :], 0.0), axis=1
    )
    current = velocity
    tendency_old = prev_tendency
    tendency = prev_tendency
    for step_no in range(STEPS):
        wide = extended_2(current, (("sec", 1), ("tile", 2)), 2)
        wide_slopes = gradients(wide, -1.0)
        push_field = stress_force(strain_stress(wide_slopes))
        slopes = tuple((piece[:, 1:-1, 1:-1, :] for piece in wide_slopes))
        advect = advection(slopes, current)
        target = from_root(current, "sec", sec_count // 2 - 1)
        fringe = flag * lam_x[None, :, None, None] * (target - current)
        sampled = current[0].reshape(-1)[safe]
        push = jnp.where(live, -(weight * sampled * jnp.abs(sampled)), 0.0)
        turbine = (
            jnp.zeros((cell_count,), jnp.float32)
            .at[safe]
            .add(push)
            .reshape(slab_x, tile_y, depth_z)
        )
        empty = jnp.zeros_like(turbine)
        tendency = push_field - advect + jnp.stack([turbine, empty, empty]) + fringe
        interim = current + time_step * (1.5 * tendency - 0.5 * tendency_old)
        grad_x, grad_y, grad_z = gradients(faces(interim), -1.0)
        rhs = grad_x[0] + grad_y[1] + grad_z[2]
        coeffs = jnp.einsum("xyz,bcz->bxyc", rhs, cos_blocks, precision=precise)
        gathered = sec_turn(coeffs).reshape(full_x, tile_y, part_z)
        along_x = jnp.einsum("xyc,kx->kcy", gathered, x_table, precision=precise)
        spread = tile_turn(along_x.reshape(tile_count, modes_each, tile_y))
        along_y = jnp.einsum("sqt,lst->ql", spread, y_table, precision=precise)
        scaled = along_y * recip
        back_y = jnp.einsum("ql,lst->sqt", scaled, y_table, precision=precise) / (full_x * full_y)
        returned = tile_turn(back_y).reshape(full_x, part_z, tile_y)
        back_x = jnp.einsum("kcy,kx->xyc", returned, x_table, precision=precise)
        home = sec_turn(back_x.reshape(sec_count, slab_x, tile_y, part_z))
        pressure = jnp.einsum(
            "bxyc,bcz->xyz", home * weight_blocks[:, None, None, :], cos_blocks, precision=precise
        )
        press_x, press_y, press_z = gradients(faces(pressure[None]), 1.0)
        current = interim - jnp.concatenate([press_x, press_y, press_z], axis=0)
        tendency_old = tendency
    return (current, tendency)


def cas_table(first, second, length):
    angle = 2.0 * np.pi / length * (np.outer(first, second) % length)
    return np.cos(angle) + np.sin(angle)


def halves(table):
    high = table.astype(np.float32).astype(jnp.bfloat16)
    low = (table - high.astype(np.float64)).astype(np.float32).astype(jnp.bfloat16)
    stacked = np.concatenate([high, low], axis=0)
    return np.concatenate(np.split(stacked, stacked.shape[1] // LANES, axis=1), axis=0)


def whole(table, columns):
    count = table.shape[0] * LANES // columns
    parts = [table[i * count : (i + 1) * count] for i in range(columns // LANES)]
    return jnp.concatenate(parts, axis=1)


def tables(sec_count, tile_count, slab_x, tile_y, depth_z):
    full_x, full_y = slab_x * sec_count, tile_y * tile_count
    wide_x = -(-full_x // LANES) * LANES
    planes, block = tile_y + 2, slab_x + ROWS
    z_at = np.arange(depth_z)
    cos_z = np.cos(np.pi / depth_z * np.outer(z_at, z_at + 0.5))
    x_cas = np.zeros((LANES, wide_x))
    x_back = np.zeros((LANES, wide_x))
    for sec in range(sec_count):
        start = sec * slab_x
        cells = np.concatenate([start + np.arange(slab_x), [start - 1, start + slab_x]]) % full_x
        x_cas[sec * block : sec * block + slab_x + 2, :full_x] = cas_table(
            cells, np.arange(full_x), full_x
        )
        cells = np.arange(start - EDGE, start + slab_x + EDGE) % full_x
        x_back[sec * block : sec * block + slab_x + 2 * EDGE, :full_x] = cas_table(
            cells, np.arange(full_x), full_x
        )
    y_blocks = []
    for plane in range(1 - EDGE, planes + EDGE - 1):
        y_at = (np.arange(tile_count) * tile_y + plane - 1) % full_y
        y_blocks.append(np.kron(cas_table(np.arange(full_y), y_at, full_y), np.eye(ROWS)))
    y_cas = np.concatenate(y_blocks[EDGE - 1 : EDGE - 1 + planes], axis=1)
    half = tile_count // COPIES * ROWS
    y_back = [
        halves(np.concatenate([y[:, i * half : (i + 1) * half] for y in y_blocks], axis=1).T)
        for i in range(COPIES)
    ]
    k_x, k_y = np.arange(full_x), np.arange(full_y)
    sin_x = np.where(k_x % (full_x // 2) == 0, 0.0, np.sin(2.0 * np.pi * k_x / full_x) ** 2)
    sin_y = np.where(k_y % (full_y // 2) == 0, 0.0, np.sin(2.0 * np.pi * k_y / full_y) ** 2)
    sin_xy = np.ones((full_y * ROWS, wide_x), np.float32)
    sin_xy[:, :full_x] = np.repeat(sin_y, ROWS)[:, None] + sin_x[None, :]
    sin_z = np.sin(np.pi * z_at / depth_z) ** 2
    weight_z = -np.where(z_at == 0, 1.0, 2.0) / (depth_z * full_x * full_y)
    mode_z = np.stack([sin_z, weight_z]).astype(np.float32)
    mode_z = np.ascontiguousarray(np.broadcast_to(mode_z[:, :, None], (2, depth_z, wide_x)))
    lam = fringe_rate * np.sin(np.pi * (np.arange(slab_x) + 0.5) / slab_x) ** 2
    lam = np.ascontiguousarray(np.broadcast_to(lam.astype(np.float32)[:, None], (slab_x, depth_z)))
    return (
        halves(cos_z),
        halves(x_cas),
        halves(x_back.T),
        halves(y_cas),
        np.concatenate(y_back, axis=0),
        sin_xy,
        mode_z,
        lam,
    )


def split(value):
    high = value.astype(jnp.bfloat16)
    return high, (value - high.astype(jnp.float32)).astype(jnp.bfloat16)


def dot(first, second, dims):
    return lax.dot_general(first, second, (dims, ((), ())), preferred_element_type=jnp.float32)


def table_first(table, second, dims):
    count = table.shape[0] // 2
    high, low = split(second)
    both = dot(table, high, dims)
    return both[:count] + (both[count:] + dot(table[:count], low, dims))


def table_second(first, table):
    count, depth = first.shape[0], table.shape[0] // 2
    high, low = split(first)
    both = dot(jnp.concatenate([high, low], axis=0), table[:depth], NN)
    return both[:count] + (both[count:] + dot(high, table[depth:], NN))


NN = ((1,), (0,))
NT = ((1,), (1,))


def slope_z(value, z_sign):
    depth = value.shape[1]
    lane = lax.broadcasted_iota(jnp.int32, value.shape, 1)
    edge = value * z_sign
    above = jnp.where(lane == depth - 1, edge, pltpu.roll(value, depth - 1, 1))
    below = jnp.where(lane == 0, edge, pltpu.roll(value, 1, 1))
    return 0.5 * (above - below)


def slope_x(value, low=None, high=None):
    count = value.shape[0]
    after = pltpu.roll(value, count - 1, 0)
    before = pltpu.roll(value, 1, 0)
    if low is not None:
        row = lax.broadcasted_iota(jnp.int32, value.shape, 0)
        after = jnp.where(row == count - 1, high, after)
        before = jnp.where(row == 0, low, before)
    return 0.5 * (after - before)


def step_kernel(
    sec_count,
    tile_count,
    slab_x,
    tile_y,
    depth_z,
    vel_hbm,
    old_hbm,
    cells_hbm,
    kinds_hbm,
    weights_ref,
    cos_hbm,
    x_hbm,
    xt_hbm,
    y_hbm,
    yt_hbm,
    sin_xy_hbm,
    mode_z_hbm,
    lam_hbm,
    vel_result,
    tend_result,
    wide,
    target,
    share,
    coeffs,
    plane_in,
    wide_out,
    last_out,
    wide_returned,
    last_returned,
    press,
    thrust,
    recip,
    vel_ref,
    old_ref,
    cells_ref,
    kinds_ref,
    cos_ref,
    x_ref,
    xt_ref,
    y_ref,
    yt_ref,
    sin_xy_ref,
    mode_z_ref,
    lam_ref,
    vel_out,
    tend_out,
    load_sem,
    result_sem,
    halo_send,
    halo_recv,
    target_send,
    target_recv,
    mode_send,
    mode_recv,
    back_send,
    back_recv,
):
    sec = lax.axis_index("sec")
    tile = lax.axis_index("tile")
    devices = sec_count * tile_count
    me = tile * sec_count + sec
    owners = depth_z // ROWS
    planes = tile_y + 2
    deep = tile_y + 4
    group = tile_count * ROWS
    block = slab_x + ROWS
    root = sec_count // 2 - 1
    fringes = sorted({0, sec_count // 2, 3 * sec_count // 4, sec_count - 1} - {root})
    first_tile = (tile_count - owners // sec_count) // 2
    is_owner = (tile >= first_tile) & (tile < first_tile + owners // sec_count)
    owner_at = (tile - first_tile) * sec_count + sec
    groups = owners // COPIES
    my_group, my_copy = lax.rem(owner_at, groups), lax.div(owner_at, groups)
    half_tiles = tile_count // COPIES
    half_group = half_tiles * ROWS
    in_fringe = functools.reduce(jnp.logical_or, [sec == which for which in fringes])
    low_sec, high_sec = lax.rem(sec + sec_count - 1, sec_count), lax.rem(sec + 1, sec_count)
    low_tile, high_tile = lax.rem(tile + tile_count - 1, tile_count), lax.rem(tile + 1, tile_count)
    end_x = ROWS + slab_x
    own_x, own_y = slice(ROWS, end_x), slice(2, 2 + tile_y)

    loads = [
        pltpu.make_async_copy(source, held, load_sem.at[place])
        for place, (source, held) in enumerate(
            (
                (vel_hbm, vel_ref),
                (cells_hbm, cells_ref),
                (kinds_hbm, kinds_ref),
                (sin_xy_hbm, sin_xy_ref),
                (mode_z_hbm, mode_z_ref),
                (old_hbm, old_ref),
                (lam_hbm, lam_ref),
                (cos_hbm, cos_ref),
                (y_hbm, y_ref),
                (x_hbm, x_ref),
                (xt_hbm, xt_ref),
                (yt_hbm, yt_ref),
            )
        )
    ]
    for load in loads:
        load.start()

    results = [
        pltpu.make_async_copy(vel_out, vel_result, result_sem.at[0]),
        pltpu.make_async_copy(tend_out, tend_result, result_sem.at[1]),
    ]

    barrier = pltpu.get_barrier_semaphore()

    def greet(ahead, carry):
        other = lax.rem(me + ahead, devices)
        pl.semaphore_signal(
            barrier,
            inc=1,
            device_id=(lax.rem(other, sec_count), lax.div(other, sec_count)),
            device_id_type=MESH,
        )
        return carry

    lax.fori_loop(1, devices, greet, 0)

    share[...] = jnp.zeros_like(share)
    loads[0].wait()
    for part in range(3):
        for row in range(tile_y):
            wide[0, part, 2 + row, own_x, :] = vel_ref[part, pl.ds(row, slab_x, stride=tile_y), :]

    pl.semaphore_wait(barrier, devices - 1)

    def start_halo(step):
        xs = {
            -1: (low_sec, slice(ROWS, 2 * ROWS), slice(end_x, end_x + ROWS)),
            0: (sec, own_x, own_x),
            1: (high_sec, slice(end_x - ROWS, end_x), slice(0, ROWS)),
        }
        ys = {
            -1: (low_tile, slice(2, 4), slice(2 + tile_y, deep)),
            0: (tile, own_y, own_y),
            1: (high_tile, slice(tile_y, 2 + tile_y), slice(0, 2)),
        }
        copies = []
        for x_way in (-1, 0, 1):
            for y_way in (-1, 0, 1):
                if x_way == 0 and y_way == 0:
                    continue
                slot = len(copies)
                to_sec, x_from, x_to = xs[x_way]
                to_tile, y_from, y_to = ys[y_way]
                if x_way != 0 and y_way == -1:
                    y_from, y_to = slice(2, 3), slice(2 + tile_y, 3 + tile_y)
                if x_way != 0 and y_way == 1:
                    y_from, y_to = slice(1 + tile_y, 2 + tile_y), slice(1, 2)
                copy = pltpu.make_async_remote_copy(
                    src_ref=wide.at[step, :, y_from, x_from, :],
                    dst_ref=wide.at[step, :, y_to, x_to, :],
                    send_sem=halo_send.at[step, slot],
                    recv_sem=halo_recv.at[step, slot],
                    device_id=(to_sec, to_tile),
                    device_id_type=MESH,
                )
                copies.append(copy)
        for copy in copies:
            copy.start()
        return copies

    def start_target(step):
        sends = [
            pltpu.make_async_remote_copy(
                src_ref=wide.at[step, :, own_y, own_x, :],
                dst_ref=target.at[step],
                send_sem=target_send.at[step, place],
                recv_sem=target_recv.at[step],
                device_id=(which, tile),
                device_id_type=MESH,
            )
            for place, which in enumerate(fringes)
        ]

        @pl.when(sec == root)
        def _():
            for send in sends:
                send.start()

        return sends

    halos = {0: start_halo(0)}
    targets = {0: start_target(0)}

    for load in loads[1:5]:
        load.wait()
    cells = cells_ref[...]
    kinds = kinds_ref[...]
    weight = jnp.zeros(cells.shape, jnp.float32)
    for kind in range(KINDS):
        weight = jnp.where(kinds == kind, weights_ref[kind], weight)
    weight = jnp.where(cells < slab_x * tile_y * depth_z, weight, 0.0)
    column = lax.div(cells, depth_z)
    row_of = lax.rem(column, tile_y) * slab_x + lax.div(column, tile_y)
    slots = cells.shape[1]
    hit_row = lax.broadcasted_iota(jnp.int32, (tile_y * slab_x, slots), 0) == row_of
    hit_z = lax.broadcasted_iota(jnp.int32, (depth_z, slots), 0) == lax.rem(cells, depth_z)
    hit_z = hit_z.astype(jnp.float32).astype(jnp.bfloat16)
    rest = jnp.where(hit_row, weight, 0.0)
    summed = jnp.zeros((tile_y * slab_x, depth_z), jnp.float32)
    for _ in range(3):
        piece, rest_next = rest.astype(jnp.bfloat16), None
        rest_next = rest - piece.astype(jnp.float32)
        summed = summed + lax.dot_general(
            piece, hit_z, (NT, ((), ())), preferred_element_type=jnp.float32
        )
        rest = rest_next
    thrust[...] = summed

    @pl.when(is_owner)
    def _():
        full_y = tile_y * tile_count
        for batch in range(COPIES):
            rows = pl.ds(pl.multiple_of((my_group * COPIES + batch) * ROWS, ROWS), ROWS)
            sum_sin = sin_xy_ref[...] + jnp.concatenate([mode_z_ref[0, rows, :]] * full_y, axis=0)
            scale = jnp.concatenate([mode_z_ref[1, rows, :]] * full_y, axis=0)
            zero_mode = sum_sin == 0.0
            value = jnp.where(zero_mode, 0.0, scale / jnp.where(zero_mode, 1.0, sum_sin))
            recip[batch * full_y * ROWS : (batch + 1) * full_y * ROWS, :] = value

    for load in loads[5:]:
        load.wait()
    old = [
        [old_ref[part, pl.ds(row, slab_x, stride=tile_y), :] for row in range(tile_y)]
        for part in range(3)
    ]

    for step in range(STEPS):
        if step == 0:
            for copy in halos[0]:
                copy.wait_recv()

        centre, stress, advect = {}, {}, {}
        for plane in range(1, deep - 1):
            here = [wide[step, part, plane] for part in range(3)]
            d_x = [slope_x(value) for value in here]
            d_y = [
                0.5 * (wide[step, part, plane + 1] - wide[step, part, plane - 1])
                for part in range(3)
            ]
            d_z = [slope_z(value, -1.0) for value in here]
            s_xx, s_yy, s_zz = d_x[0], d_y[1], d_z[2]
            s_xy = 0.5 * (d_x[1] + d_y[0])
            s_xz = 0.5 * (d_x[2] + d_z[0])
            s_yz = 0.5 * (d_y[2] + d_z[1])
            squared = s_xx * s_xx + s_yy * s_yy + s_zz * s_zz
            squared = squared + 2.0 * (s_xy * s_xy + s_xz * s_xz + s_yz * s_yz)
            double = (2.0 * smag_coef) * jnp.sqrt(2.0 * squared + 0.01)
            stress[plane] = [double * s for s in (s_xx, s_yy, s_zz, s_xy, s_xz, s_yz)]
            centre[plane] = here
            advect[plane] = [
                here[0] * d_x[part] + here[1] * d_y[part] + here[2] * d_z[part]
                for part in range(3)
            ]

        @pl.when(in_fringe)
        def _(step=step):
            pltpu.make_async_copy(target.at[step], target.at[step], target_recv.at[step]).wait()

        @pl.when(jnp.logical_not(in_fringe))
        def _(step=step):
            target[step] = wide[step, :, own_y, own_x, :]

        interim, tendency = [], []
        for row in range(tile_y):
            plane = 2 + row
            xx, yy, zz, xy, xz, yz = stress[plane]
            before, after = stress[plane - 1], stress[plane + 1]
            push = [
                slope_x(xx) + 0.5 * (after[3] - before[3]) + slope_z(xz, 0.0),
                slope_x(xy) + 0.5 * (after[1] - before[1]) + slope_z(yz, 0.0),
                slope_x(xz) + 0.5 * (after[5] - before[5]) + slope_z(zz, 0.0),
            ]
            lam = lam_ref[...]
            tend, mid = [], []
            for part in range(3):
                here = centre[plane][part][own_x]
                total = (push[part] - advect[plane][part])[own_x]
                if part == 0:
                    force = thrust[row * slab_x : (row + 1) * slab_x, :]
                    total = total - force * here * jnp.abs(here)
                total = total + lam * (target[step, part, row] - here)
                tend.append(total)
                mid.append(here + time_step * (1.5 * total - 0.5 * old[part][row]))
                if step == STEPS - 1:
                    tend_out[part, pl.ds(row, slab_x, stride=tile_y), :] = total
            tendency.append(tend)
            interim.append(mid)
        if step == STEPS - 1:
            results[1].start()
        old = [[tendency[row][part] for row in range(tile_y)] for part in range(3)]

        share[0:slab_x, :] = 0.5 * interim[0][1]
        last = (planes - 1) * block
        share[last : last + slab_x, :] = -0.5 * interim[tile_y - 1][1]
        for row in range(tile_y):
            along_x, _, along_z = interim[row]
            total = slope_x(along_x, 0.0, 0.0) + slope_z(along_z, -1.0)
            if row + 1 < tile_y:
                total = total + 0.5 * interim[row + 1][1]
            if row > 0:
                total = total - 0.5 * interim[row - 1][1]
            start = (row + 1) * block
            edge = start + slab_x
            share[start:edge, :] = total
            share[edge : edge + 1, :] = 0.5 * along_x[0:1]
            share[edge + 1 : edge + 2, :] = -0.5 * along_x[slab_x - 1 : slab_x]
        coeffs[step] = table_first(cos_ref[...], share[...], NT).reshape(owners, ROWS, LANES)

        my_rows = pl.ds(pl.multiple_of(tile * ROWS, ROWS), ROWS)

        first_owner = jnp.where(is_owner, owner_at, lax.rem(me, owners))

        def modes_to(owner, step=step):
            flat = owner + first_tile * sec_count
            return pltpu.make_async_remote_copy(
                src_ref=coeffs.at[step, pl.ds(lax.rem(owner, groups) * COPIES, COPIES)],
                dst_ref=plane_in.at[step, sec, :, my_rows, :],
                send_sem=mode_send.at[step],
                recv_sem=mode_recv.at[step],
                device_id=(lax.rem(flat, sec_count), lax.div(flat, sec_count)),
                device_id_type=MESH,
            )

        def send_modes(ahead, carry):
            modes_to(lax.rem(first_owner + ahead, owners)).start()
            return carry

        lax.fori_loop(1, owners, send_modes, 0, unroll=True)

        @pl.when(is_owner)
        def _(step=step):
            pltpu.make_async_copy(
                coeffs.at[step, pl.ds(my_group * COPIES, COPIES)],
                plane_in.at[step, sec, :, my_rows, :],
                mode_recv.at[step],
            ).start()

        @pl.when(jnp.logical_not(is_owner))
        def _(first_owner=first_owner):
            modes_to(first_owner).start()

        final = step == STEPS - 1
        if not final:
            for part in range(3):
                for row in range(tile_y):
                    wide[step + 1, part, 2 + row, own_x, :] = interim[row][part]
            halos[step + 1] = start_halo(step + 1)
        reach = 1 if final else EDGE
        plane_out, returned = (last_out, last_returned) if final else (wide_out, wide_returned)
        per_tile = LANES // block
        back_planes = tile_y + 2 * reach

        @pl.when(is_owner)
        def _(step=step):
            pltpu.make_async_copy(
                plane_in.at[step], plane_in.at[step], mode_recv.at[step]
            ).wait()
            lane_block = lax.broadcasted_iota(jnp.int32, (group, LANES), 1) // block
            batches = []
            for batch in range(COPIES):
                arrived = [plane_in[step, part, batch] for part in range(sec_count)]
                blocks = []
                for plane in range(planes):
                    piece = pltpu.roll(arrived[0], -plane * block % LANES, 1)
                    for part in range(1, sec_count):
                        other = pltpu.roll(arrived[part], (part - plane) * block % LANES, 1)
                        piece = jnp.where(lane_block == part, other, piece)
                    blocks.append(piece)
                batches.append(jnp.concatenate(blocks, axis=0))
            along_y = table_first(
                whole(y_ref[...], planes * group), jnp.concatenate(batches, axis=1), NN
            )
            along_y = jnp.concatenate(
                [along_y[:, i * LANES : (i + 1) * LANES] for i in range(COPIES)], axis=0
            )
            modes = table_second(along_y, whole(x_ref[...], recip.shape[1])) * recip[...]
            back_x = table_second(modes, whole(xt_ref[...], LANES))
            count = back_x.shape[0] // COPIES
            back_x = jnp.concatenate(
                [back_x[i * count : (i + 1) * count] for i in range(COPIES)], axis=1
            )
            skip = (EDGE - reach) * half_group
            kept = back_planes * half_group
            full = (tile_y + 2 * EDGE) * half_group
            high_at = pl.multiple_of(my_copy * 2 * full + skip, 2 * ROWS)
            low_at = pl.multiple_of(my_copy * 2 * full + full + skip, 2 * ROWS)
            back_table = jnp.concatenate(
                [yt_ref[pl.ds(high_at, kept), :], yt_ref[pl.ds(low_at, kept), :]], axis=0
            )
            spread = table_first(back_table, back_x, NN)
            back_block = lane_block[:half_group]
            for batch in range(COPIES):
                for part in range(sec_count):
                    for first in range(0, back_planes, per_tile):
                        piece = None
                        for place in range(min(per_tile, back_planes - first)):
                            start = (first + place) * half_group
                            other = spread[
                                start : start + half_group, batch * LANES : (batch + 1) * LANES
                            ]
                            other = pltpu.roll(other, (place - part) * block % LANES, 1)
                            if piece is None:
                                piece = other
                            else:
                                piece = jnp.where(back_block == place, other, piece)
                        lanes = slice(first // per_tile * LANES, (first // per_tile + 1) * LANES)
                        plane_out[part, batch, :, lanes] = piece
            rows = pl.ds(my_group * COPIES, COPIES)
            half_devices = half_tiles * sec_count
            my_place = me - my_copy * half_devices

            def out_rows(place):
                start = lax.div(place, sec_count) * ROWS
                return pl.ds(pl.multiple_of(start, ROWS), ROWS)

            pltpu.make_async_copy(
                plane_out.at[sec, :, out_rows(my_place), :], returned.at[rows], back_recv.at[step]
            ).start()

            def send_back(ahead, carry):
                place = lax.rem(my_place + ahead, half_devices)
                to_sec = lax.rem(place, sec_count)
                to_tile = lax.div(place, sec_count) + my_copy * half_tiles
                pltpu.make_async_remote_copy(
                    src_ref=plane_out.at[to_sec, :, out_rows(place), :],
                    dst_ref=returned.at[rows],
                    send_sem=back_send.at[step],
                    recv_sem=back_recv.at[step],
                    device_id=(to_sec, to_tile),
                    device_id_type=MESH,
                ).start()
                return carry

            lax.fori_loop(1, half_devices, send_back, 0, unroll=True)

        pltpu.make_async_copy(returned, returned, back_recv.at[step]).wait()
        columns = returned[...].reshape(depth_z, returned.shape[2])
        columns = jnp.concatenate(
            [columns[:, i : i + LANES].T for i in range(0, columns.shape[1], LANES)], axis=0
        )
        press[0 : columns.shape[0], :] = table_second(columns, cos_ref[...])

        def press_slopes(start, count):
            here = press[start : start + count, :]
            above = press[start + block : start + block + count, :]
            below = press[start - block : start - block + count, :]
            return here, 0.5 * (above - below), slope_z(here, 1.0)

        if final:
            for row in range(tile_y):
                start = (row + 1) * block + EDGE
                here, along_y, along_z = press_slopes(start, slab_x)
                low = press[start - 1 : start, :]
                high = press[start + slab_x : start + slab_x + 1, :]
                slopes = [slope_x(here, low, high), along_y, along_z]
                for part in range(3):
                    vel_out[part, pl.ds(row, slab_x, stride=tile_y), :] = (
                        interim[row][part] - slopes[part]
                    )
        else:
            for copy in halos[step + 1]:
                copy.wait()
            span = slice(ROWS - EDGE, ROWS - EDGE + block)
            for plane in range(deep):
                here, along_y, along_z = press_slopes((plane + 1) * block, block)
                slopes = [slope_x(here), along_y, along_z]
                for part in range(3):
                    wide[step + 1, part, plane, span, :] = (
                        wide[step + 1, part, plane, span, :] - slopes[part]
                    )
            targets[step + 1] = start_target(step + 1)

    results[0].start()
    for copy in halos[0]:
        copy.wait_send()
    for step, sends in targets.items():
        plane_out = last_out if step == STEPS - 1 else wide_out

        @pl.when(sec == root)
        def _(sends=sends):
            for send in sends:
                send.wait_send()

        @pl.when(is_owner)
        def _(step=step, plane_out=plane_out):
            pltpu.make_async_copy(coeffs.at[step], coeffs.at[step], mode_send.at[step]).wait()
            most = coeffs.at[step, pl.ds(0, owners - COPIES)]
            pltpu.make_async_copy(most, most, mode_send.at[step]).wait()
            some = plane_out.at[pl.ds(0, sec_count - 1)]
            pltpu.make_async_copy(some, some, back_send.at[step]).wait()
            last = plane_out.at[sec_count - 1, :, pl.ds(0, half_group - ROWS), :]
            pltpu.make_async_copy(last, last, back_send.at[step]).wait()

        @pl.when(jnp.logical_not(is_owner))
        def _(step=step):
            for _ in range(COPIES):
                pltpu.make_async_copy(coeffs.at[step], coeffs.at[step], mode_send.at[step]).wait()

    for result in results:
        result.wait()


def hand_over(vel_from, tend_from, vel_to, tend_to):
    vel_to[...] = vel_from[...]
    tend_to[...] = tend_from[...]


def direct(sec_count, tile_count, velocity, prev_tendency, disk_cells, disk_kind, rotor_weights):
    _, slab_x, tile_y, depth_z = velocity.shape
    constants = [
        jnp.asarray(table) for table in tables(sec_count, tile_count, slab_x, tile_y, depth_z)
    ]
    wide_x = constants[5].shape[1]
    full_y = tile_y * tile_count
    group = tile_count * ROWS
    wide_lanes = (tile_y + 2 * EDGE) * (slab_x + ROWS)
    wide_lanes = -(-wide_lanes // LANES) * LANES
    flat = (3, slab_x * tile_y, depth_z)
    vmem = pl.BlockSpec(memory_space=pltpu.VMEM)
    hbm = pl.BlockSpec(memory_space=pltpu.HBM)
    operands = [
        velocity.reshape(flat),
        prev_tendency.reshape(flat),
        disk_cells.reshape(1, -1),
        disk_kind.reshape(1, -1),
        *constants,
    ]
    smem = pl.BlockSpec(memory_space=pltpu.SMEM)
    dma = pltpu.SemaphoreType.DMA
    outs = pl.pallas_call(
        functools.partial(step_kernel, sec_count, tile_count, slab_x, tile_y, depth_z),
        out_shape=[jax.ShapeDtypeStruct(flat, jnp.float32)] * 2,
        in_specs=[hbm] * 4 + [smem] + [hbm] * len(constants),
        out_specs=[hbm] * 2,
        scratch_shapes=[
            pltpu.VMEM((STEPS, 3, tile_y + 4, slab_x + 2 * ROWS, depth_z), jnp.float32),
            pltpu.VMEM((STEPS, 3, tile_y, slab_x, depth_z), jnp.float32),
            pltpu.VMEM((LANES, depth_z), jnp.float32),
            pltpu.VMEM((STEPS, depth_z // ROWS, ROWS, LANES), jnp.float32),
            pltpu.VMEM((STEPS, sec_count, COPIES, group, LANES), jnp.float32),
            pltpu.VMEM((sec_count, COPIES, group // COPIES, wide_lanes), jnp.float32),
            pltpu.VMEM((sec_count, COPIES, group // COPIES, LANES), jnp.float32),
            pltpu.VMEM((depth_z // ROWS, ROWS, wide_lanes), jnp.float32),
            pltpu.VMEM((depth_z // ROWS, ROWS, LANES), jnp.float32),
            pltpu.VMEM((wide_lanes, depth_z), jnp.float32),
            pltpu.VMEM((tile_y * slab_x, depth_z), jnp.float32),
            pltpu.VMEM((COPIES * full_y * ROWS, wide_x), jnp.float32),
            *[pltpu.VMEM(operand.shape, operand.dtype) for operand in operands],
            pltpu.VMEM(flat, jnp.float32),
            pltpu.VMEM(flat, jnp.float32),
            dma((len(operands),)),
            dma((2,)),
            dma((STEPS, 8)),
            dma((STEPS, 8)),
            dma((STEPS, 4)),
            dma((STEPS,)),
            dma((STEPS,)),
            dma((STEPS,)),
            dma((STEPS,)),
            dma((STEPS,)),
        ],
        compiler_params=pltpu.CompilerParams(
            collective_id=0, has_side_effects=True, vmem_limit_bytes=60 * 1024 * 1024
        ),
        name="les_steps",
    )(*operands[:4], rotor_weights, *operands[4:])
    outs = pl.pallas_call(
        hand_over,
        out_shape=[jax.ShapeDtypeStruct(flat, jnp.float32)] * 2,
        in_specs=[vmem] * 2,
        out_specs=[vmem] * 2,
        name="hand_over",
    )(*outs)
    return tuple(out.reshape(velocity.shape) for out in outs)


def solution(mesh):
    sec_count, tile_count = mesh.shape["sec"], mesh.shape["tile"]
    in_specs = (
        P(None, "sec", "tile", None),
        P(None, "sec", "tile", None),
        P("sec", "tile", None),
        P("sec", "tile", None),
        P(),
    )
    out_specs = (P(None, "sec", "tile", None), P(None, "sec", "tile", None))

    def pick(velocity, *others):
        _, slab_x, tile_y, depth_z = velocity.shape
        owners = depth_z // ROWS
        fits = (
            owners <= sec_count * tile_count
            and owners % (COPIES * sec_count) == 0
            and tile_count % (2 * COPIES) == 0
            and sec_count * (slab_x + ROWS) <= LANES
            and LANES % (slab_x + ROWS) == 0
            and depth_z % LANES == 0
            and slab_x % ROWS == 0
            and tile_y >= 2
            and (tile_y + 2) * (slab_x + ROWS) <= LANES
            and tile_y * tile_count * ROWS <= 512
            and sec_count >= 3
            and tile_count >= 3
        )
        if fits:
            return direct(sec_count, tile_count, velocity, *others)
        return local(velocity, *others)

    return jax.shard_map(pick, mesh=mesh, in_specs=in_specs, out_specs=out_specs, check_vma=False)
```

```python
import functools
import math

import jax
import jax.numpy as jnp
import numpy as np
from jax import lax
from jax.experimental import pallas as pl
from jax.experimental.pallas import tpu as pltpu
from jax.sharding import PartitionSpec as P

STEPS = 2
KINDS = 16
ROWS = 8
LANES = 128
EDGE = 3
MESH = pl.DeviceIdType.MESH

precise = lax.Precision.HIGHEST
time_step = 0.1
fringe_rate = 2.0
smag_coef = 0.04


def extended_2(block, sides, width):
    for axis, dim in sides:
        count = lax.axis_size(axis)
        forward = [(i, i + 1) for i in range(count - 1)]
        forward.append((count - 1, 0))
        backward = [(target, source) for source, target in forward]
        low = lax.ppermute(
            lax.slice_in_dim(block, block.shape[dim] - width, None, axis=dim), axis, forward
        )
        high = lax.ppermute(lax.slice_in_dim(block, 0, width, axis=dim), axis, backward)
        block = jnp.concatenate([low, block, high], axis=dim)
    return block


def from_root(block, axis, owner):
    block = jnp.where(lax.axis_index(axis) == owner, block, jnp.zeros_like(block))
    return lax.psum(block, axis)


def gradients(padded, z_sign):
    centre = padded[:, 1:-1, 1:-1, :]
    grad_x = 0.5 * (padded[:, 2:, 1:-1, :] - padded[:, :-2, 1:-1, :])
    grad_y = 0.5 * (padded[:, 1:-1, 2:, :] - padded[:, 1:-1, :-2, :])
    extended = jnp.concatenate(
        [z_sign * centre[..., :1], centre, z_sign * centre[..., -1:]], axis=-1
    )
    grad_z = 0.5 * (extended[..., 2:] - extended[..., :-2])
    return (grad_x, grad_y, grad_z)


def strain_stress(slopes):

    def strain(first, second):
        return 0.5 * (slopes[second][first] + slopes[first][second])

    strain_xx = strain(0, 0)
    strain_yy = strain(1, 1)
    strain_zz = strain(2, 2)
    strain_xy = strain(0, 1)
    strain_xz = strain(0, 2)
    strain_yz = strain(1, 2)
    squared = strain_xx * strain_xx + strain_yy * strain_yy + strain_zz * strain_zz
    squared = squared + 2.0 * (
        strain_xy * strain_xy + strain_xz * strain_xz + strain_yz * strain_yz
    )
    double = 2.0 * (smag_coef * jnp.sqrt(2.0 * squared + 0.01))
    return jnp.stack(
        [
            double * strain_xx,
            double * strain_yy,
            double * strain_zz,
            double * strain_xy,
            double * strain_xz,
            double * strain_yz,
        ]
    )


def advection(slopes, centre):
    return centre[0:1] * slopes[0] + centre[1:2] * slopes[1] + centre[2:3] * slopes[2]


def stress_force(padded):
    grad_x, grad_y, grad_z = gradients(padded, 0.0)
    return jnp.stack(
        [
            grad_x[0] + grad_y[3] + grad_z[4],
            grad_x[3] + grad_y[1] + grad_z[5],
            grad_x[4] + grad_y[5] + grad_z[2],
        ]
    )


def faces(source):
    return extended_2(source, (("sec", 1), ("tile", 2)), 1)


def sec_turn(blocks):
    return lax.all_to_all(blocks, "sec", split_axis=0, concat_axis=0, tiled=True)


def tile_turn(blocks):
    return lax.all_to_all(blocks, "tile", split_axis=0, concat_axis=0, tiled=True)


def hartley_table(length):
    index_row = jnp.arange(length)
    product = index_row[:, None] * index_row[None, :] % length
    angle = 2.0 * math.pi / length * product.astype(jnp.float32)
    return jnp.cos(angle) + jnp.sin(angle)


def local(velocity, prev_tendency, disk_cells, disk_kind, rotor_weights):
    sec_count = lax.axis_size("sec")
    tile_count = lax.axis_size("tile")
    sec_at = lax.axis_index("sec")
    tile_at = lax.axis_index("tile")
    slab_x = velocity.shape[1]
    tile_y = velocity.shape[2]
    depth_z = velocity.shape[3]
    full_x = slab_x * sec_count
    full_y = tile_y * tile_count
    part_z = depth_z // sec_count
    modes_each = slab_x * depth_z // tile_count
    cell_count = slab_x * tile_y * depth_z
    modes = jnp.arange(depth_z).astype(jnp.float32)[:, None]
    points = jnp.arange(depth_z).astype(jnp.float32)[None, :] + 0.5
    cos_blocks = jnp.cos(math.pi * modes * points / depth_z).reshape(sec_count, part_z, depth_z)
    weight_blocks = jnp.where(jnp.arange(depth_z) == 0, 1.0 / depth_z, 2.0 / depth_z).astype(
        jnp.float32
    )
    weight_blocks = weight_blocks.reshape(sec_count, part_z)
    x_table = hartley_table(full_x)
    y_table = hartley_table(full_y).reshape(full_y, tile_count, tile_y)
    flat_ids = tile_at * modes_each + jnp.arange(modes_each)
    mode_x = flat_ids // part_z
    mode_z = sec_at * part_z + flat_ids % part_z
    mode_y = jnp.arange(full_y)
    sin_x = jnp.sin(2.0 * math.pi * mode_x.astype(jnp.float32) / full_x)
    sin_y = jnp.sin(2.0 * math.pi * mode_y.astype(jnp.float32) / full_y)
    sin_z = jnp.sin(math.pi * mode_z.astype(jnp.float32) / depth_z)
    eigen = -((sin_x * sin_x)[:, None] + (sin_y * sin_y)[None, :] + (sin_z * sin_z)[:, None])
    zero_mode = (
        (mode_x % (full_x // 2) == 0)[:, None]
        & (mode_y % (full_y // 2) == 0)[None, :]
        & (mode_z == 0)[:, None]
    )
    recip = jnp.where(zero_mode, 0.0, 1.0 / jnp.where(zero_mode, 1.0, eigen))
    slab_pos = jnp.sin(math.pi * (jnp.arange(slab_x).astype(jnp.float32) + 0.5) / slab_x)
    lam_x = fringe_rate * (slab_pos * slab_pos)
    flag = (
        (sec_at == 0)
        | (sec_at == sec_count // 2)
        | (sec_at == 3 * sec_count // 4)
        | (sec_at == sec_count - 1)
    ).astype(jnp.float32)
    picked = disk_cells.reshape(-1)
    kinds = disk_kind.reshape(-1)
    live = picked < cell_count
    safe = jnp.minimum(picked, cell_count - 1)
    weight = jnp.sum(
        jnp.where(kinds[:, None] == jnp.arange(KINDS)[None, :], rotor_weights[None, :], 0.0), axis=1
    )
    current = velocity
    tendency_old = prev_tendency
    tendency = prev_tendency
    for step_no in range(STEPS):
        wide = extended_2(current, (("sec", 1), ("tile", 2)), 2)
        wide_slopes = gradients(wide, -1.0)
        push_field = stress_force(strain_stress(wide_slopes))
        slopes = tuple((piece[:, 1:-1, 1:-1, :] for piece in wide_slopes))
        advect = advection(slopes, current)
        target = from_root(current, "sec", sec_count // 2 - 1)
        fringe = flag * lam_x[None, :, None, None] * (target - current)
        sampled = current[0].reshape(-1)[safe]
        push = jnp.where(live, -(weight * sampled * jnp.abs(sampled)), 0.0)
        turbine = (
            jnp.zeros((cell_count,), jnp.float32)
            .at[safe]
            .add(push)
            .reshape(slab_x, tile_y, depth_z)
        )
        empty = jnp.zeros_like(turbine)
        tendency = push_field - advect + jnp.stack([turbine, empty, empty]) + fringe
        interim = current + time_step * (1.5 * tendency - 0.5 * tendency_old)
        grad_x, grad_y, grad_z = gradients(faces(interim), -1.0)
        rhs = grad_x[0] + grad_y[1] + grad_z[2]
        coeffs = jnp.einsum("xyz,bcz->bxyc", rhs, cos_blocks, precision=precise)
        gathered = sec_turn(coeffs).reshape(full_x, tile_y, part_z)
        along_x = jnp.einsum("xyc,kx->kcy", gathered, x_table, precision=precise)
        spread = tile_turn(along_x.reshape(tile_count, modes_each, tile_y))
        along_y = jnp.einsum("sqt,lst->ql", spread, y_table, precision=precise)
        scaled = along_y * recip
        back_y = jnp.einsum("ql,lst->sqt", scaled, y_table, precision=precise) / (full_x * full_y)
        returned = tile_turn(back_y).reshape(full_x, part_z, tile_y)
        back_x = jnp.einsum("kcy,kx->xyc", returned, x_table, precision=precise)
        home = sec_turn(back_x.reshape(sec_count, slab_x, tile_y, part_z))
        pressure = jnp.einsum(
            "bxyc,bcz->xyz", home * weight_blocks[:, None, None, :], cos_blocks, precision=precise
        )
        press_x, press_y, press_z = gradients(faces(pressure[None]), 1.0)
        current = interim - jnp.concatenate([press_x, press_y, press_z], axis=0)
        tendency_old = tendency
    return (current, tendency)


def cas_table(first, second, length):
    angle = 2.0 * np.pi / length * (np.outer(first, second) % length)
    return np.cos(angle) + np.sin(angle)


def halves(table):
    high = table.astype(np.float32).astype(jnp.bfloat16)
    low = (table - high.astype(np.float64)).astype(np.float32).astype(jnp.bfloat16)
    stacked = np.concatenate([high, low], axis=0)
    return np.concatenate(np.split(stacked, stacked.shape[1] // LANES, axis=1), axis=0)


def whole(table, columns):
    count = table.shape[0] * LANES // columns
    parts = [table[i * count : (i + 1) * count] for i in range(columns // LANES)]
    return jnp.concatenate(parts, axis=1)


def tables(sec_count, tile_count, slab_x, tile_y, depth_z):
    full_x, full_y = slab_x * sec_count, tile_y * tile_count
    wide_x = -(-full_x // LANES) * LANES
    planes, block = tile_y + 2, slab_x + ROWS
    z_at = np.arange(depth_z)
    cos_z = np.cos(np.pi / depth_z * np.outer(z_at, z_at + 0.5))
    x_cas = np.zeros((LANES, wide_x))
    x_back = np.zeros((LANES, wide_x))
    for sec in range(sec_count):
        start = sec * slab_x
        cells = np.concatenate([start + np.arange(slab_x), [start - 1, start + slab_x]]) % full_x
        x_cas[sec * block : sec * block + slab_x + 2, :full_x] = cas_table(
            cells, np.arange(full_x), full_x
        )
        cells = np.arange(start - EDGE, start + slab_x + EDGE) % full_x
        x_back[sec * block : sec * block + slab_x + 2 * EDGE, :full_x] = cas_table(
            cells, np.arange(full_x), full_x
        )
    y_blocks = []
    for plane in range(1 - EDGE, planes + EDGE - 1):
        y_at = (np.arange(tile_count) * tile_y + plane - 1) % full_y
        y_blocks.append(np.kron(cas_table(np.arange(full_y), y_at, full_y), np.eye(ROWS)))
    y_cas = np.concatenate(y_blocks[EDGE - 1 : EDGE - 1 + planes], axis=1)
    y_back = np.concatenate(y_blocks, axis=1).T
    k_x, k_y = np.arange(full_x), np.arange(full_y)
    sin_x = np.where(k_x % (full_x // 2) == 0, 0.0, np.sin(2.0 * np.pi * k_x / full_x) ** 2)
    sin_y = np.where(k_y % (full_y // 2) == 0, 0.0, np.sin(2.0 * np.pi * k_y / full_y) ** 2)
    sin_xy = np.ones((full_y * ROWS, wide_x), np.float32)
    sin_xy[:, :full_x] = np.repeat(sin_y, ROWS)[:, None] + sin_x[None, :]
    sin_z = np.sin(np.pi * z_at / depth_z) ** 2
    weight_z = -np.where(z_at == 0, 1.0, 2.0) / (depth_z * full_x * full_y)
    mode_z = np.stack([sin_z, weight_z]).astype(np.float32)
    mode_z = np.ascontiguousarray(np.broadcast_to(mode_z[:, :, None], (2, depth_z, wide_x)))
    lam = fringe_rate * np.sin(np.pi * (np.arange(slab_x) + 0.5) / slab_x) ** 2
    lam = np.ascontiguousarray(np.broadcast_to(lam.astype(np.float32)[:, None], (slab_x, depth_z)))
    return (
        halves(cos_z),
        halves(x_cas),
        halves(x_back.T),
        halves(y_cas),
        halves(y_back),
        sin_xy,
        mode_z,
        lam,
    )


def split(value):
    high = value.astype(jnp.bfloat16)
    return high, (value - high.astype(jnp.float32)).astype(jnp.bfloat16)


def dot(first, second, dims):
    return lax.dot_general(first, second, (dims, ((), ())), preferred_element_type=jnp.float32)


def table_first(table, second, dims):
    count = table.shape[0] // 2
    high, low = split(second)
    both = dot(table, high, dims)
    return both[:count] + (both[count:] + dot(table[:count], low, dims))


def table_second(first, table):
    count, depth = first.shape[0], table.shape[0] // 2
    high, low = split(first)
    both = dot(jnp.concatenate([high, low], axis=0), table[:depth], NN)
    return both[:count] + (both[count:] + dot(high, table[depth:], NN))


NN = ((1,), (0,))
NT = ((1,), (1,))


def slope_z(value, z_sign):
    depth = value.shape[1]
    lane = lax.broadcasted_iota(jnp.int32, value.shape, 1)
    edge = value * z_sign
    above = jnp.where(lane == depth - 1, edge, pltpu.roll(value, depth - 1, 1))
    below = jnp.where(lane == 0, edge, pltpu.roll(value, 1, 1))
    return 0.5 * (above - below)


def slope_x(value, low=None, high=None):
    count = value.shape[0]
    after = pltpu.roll(value, count - 1, 0)
    before = pltpu.roll(value, 1, 0)
    if low is not None:
        row = lax.broadcasted_iota(jnp.int32, value.shape, 0)
        after = jnp.where(row == count - 1, high, after)
        before = jnp.where(row == 0, low, before)
    return 0.5 * (after - before)


def step_kernel(
    sec_count,
    tile_count,
    slab_x,
    tile_y,
    depth_z,
    vel_hbm,
    old_hbm,
    cells_hbm,
    kinds_hbm,
    weights_ref,
    cos_hbm,
    x_hbm,
    xt_hbm,
    y_hbm,
    yt_hbm,
    sin_xy_hbm,
    mode_z_hbm,
    lam_hbm,
    vel_result,
    tend_result,
    wide,
    target,
    share,
    coeffs,
    plane_in,
    wide_out,
    last_out,
    wide_returned,
    last_returned,
    press,
    thrust,
    recip,
    vel_ref,
    old_ref,
    cells_ref,
    kinds_ref,
    cos_ref,
    x_ref,
    xt_ref,
    y_ref,
    yt_ref,
    sin_xy_ref,
    mode_z_ref,
    lam_ref,
    vel_out,
    tend_out,
    load_sem,
    result_sem,
    corner_out,
    corner_in,
    halo_send,
    halo_recv,
    target_send,
    target_recv,
    mode_send,
    mode_recv,
    back_send,
    back_recv,
):
    sec = lax.axis_index("sec")
    tile = lax.axis_index("tile")
    devices = sec_count * tile_count
    me = tile * sec_count + sec
    owners = depth_z // ROWS
    planes = tile_y + 2
    deep = tile_y + 4
    group = tile_count * ROWS
    block = slab_x + ROWS
    root = sec_count // 2 - 1
    fringes = sorted({0, sec_count // 2, 3 * sec_count // 4, sec_count - 1} - {root})
    first_tile = (tile_count - owners // sec_count) // 2
    is_owner = (tile >= first_tile) & (tile < first_tile + owners // sec_count)
    owner_at = (tile - first_tile) * sec_count + sec
    in_fringe = functools.reduce(jnp.logical_or, [sec == which for which in fringes])
    low_sec, high_sec = lax.rem(sec + sec_count - 1, sec_count), lax.rem(sec + 1, sec_count)
    low_tile, high_tile = lax.rem(tile + tile_count - 1, tile_count), lax.rem(tile + 1, tile_count)
    end_x = ROWS + slab_x
    own_x, own_y = slice(ROWS, end_x), slice(2, 2 + tile_y)

    loads = [
        pltpu.make_async_copy(source, held, load_sem.at[place])
        for place, (source, held) in enumerate(
            (
                (vel_hbm, vel_ref),
                (cells_hbm, cells_ref),
                (kinds_hbm, kinds_ref),
                (sin_xy_hbm, sin_xy_ref),
                (mode_z_hbm, mode_z_ref),
                (old_hbm, old_ref),
                (lam_hbm, lam_ref),
                (cos_hbm, cos_ref),
                (y_hbm, y_ref),
                (x_hbm, x_ref),
                (xt_hbm, xt_ref),
                (yt_hbm, yt_ref),
            )
        )
    ]
    for load in loads:
        load.start()

    results = [
        pltpu.make_async_copy(vel_out, vel_result, result_sem.at[0]),
        pltpu.make_async_copy(tend_out, tend_result, result_sem.at[1]),
    ]

    barrier = pltpu.get_barrier_semaphore()

    def greet(ahead, carry):
        other = lax.rem(me + ahead, devices)
        pl.semaphore_signal(
            barrier,
            inc=1,
            device_id=(lax.rem(other, sec_count), lax.div(other, sec_count)),
            device_id_type=MESH,
        )
        return carry

    lax.fori_loop(1, devices, greet, 0)

    share[...] = jnp.zeros_like(share)
    corner_out[...] = jnp.zeros_like(corner_out)
    loads[0].wait()
    for part in range(3):
        for row in range(tile_y):
            wide[0, part, 2 + row, own_x, :] = vel_ref[part, pl.ds(row, slab_x, stride=tile_y), :]

    pl.semaphore_wait(barrier, devices - 1)

    def start_halo(step):
        xs = {
            -1: (low_sec, slice(ROWS, 2 * ROWS), slice(end_x, end_x + ROWS)),
            0: (sec, own_x, own_x),
            1: (high_sec, slice(end_x - ROWS, end_x), slice(0, ROWS)),
        }
        ys = {
            -1: (low_tile, slice(2, 4), slice(2 + tile_y, deep)),
            0: (tile, own_y, own_y),
            1: (high_tile, slice(tile_y, 2 + tile_y), slice(0, 2)),
        }
        copies = []
        for x_way in (-1, 0, 1):
            for y_way in (-1, 0, 1):
                if x_way == 0 and y_way == 0:
                    continue
                slot = len(copies)
                to_sec, x_from, x_to = xs[x_way]
                to_tile, y_from, y_to = ys[y_way]
                source = wide.at[step, :, y_from, x_from, :]
                end = wide.at[step, :, y_to, x_to, :]
                if x_way != 0 and y_way != 0:
                    corner = x_way + 1 + (y_way + 1) // 2
                    plane = 2 if y_way < 0 else 1 + tile_y
                    row = ROWS if x_way < 0 else end_x - 1
                    for part in range(3):
                        corner_out[step, corner, part : part + 1, :] = wide[
                            step, part, plane, row : row + 1, :
                        ]
                    source, end = corner_out.at[step, corner], corner_in.at[step, corner]
                copy = pltpu.make_async_remote_copy(
                    src_ref=source,
                    dst_ref=end,
                    send_sem=halo_send.at[step, slot],
                    recv_sem=halo_recv.at[step, slot],
                    device_id=(to_sec, to_tile),
                    device_id_type=MESH,
                )
                copies.append(copy)
        for copy in copies:
            copy.start()
        return copies

    def unpack_corners(step):
        for x_way in (-1, 1):
            for y_way in (-1, 1):
                corner = x_way + 1 + (y_way + 1) // 2
                plane = 2 + tile_y if y_way < 0 else 1
                row = end_x if x_way < 0 else ROWS - 1
                for part in range(3):
                    wide[step, part, plane, row : row + 1, :] = corner_in[
                        step, corner, part : part + 1, :
                    ]

    def start_target(step):
        sends = [
            pltpu.make_async_remote_copy(
                src_ref=wide.at[step, :, own_y, own_x, :],
                dst_ref=target.at[step],
                send_sem=target_send.at[step, place],
                recv_sem=target_recv.at[step],
                device_id=(which, tile),
                device_id_type=MESH,
            )
            for place, which in enumerate(fringes)
        ]

        @pl.when(sec == root)
        def _():
            for send in sends:
                send.start()

        return sends

    halos = {0: start_halo(0)}
    targets = {0: start_target(0)}

    for load in loads[1:5]:
        load.wait()
    cells = cells_ref[...]
    kinds = kinds_ref[...]
    weight = jnp.zeros(cells.shape, jnp.float32)
    for kind in range(KINDS):
        weight = jnp.where(kinds == kind, weights_ref[kind], weight)
    weight = jnp.where(cells < slab_x * tile_y * depth_z, weight, 0.0)
    column = lax.div(cells, depth_z)
    row_of = lax.rem(column, tile_y) * slab_x + lax.div(column, tile_y)
    slots = cells.shape[1]
    hit_row = lax.broadcasted_iota(jnp.int32, (tile_y * slab_x, slots), 0) == row_of
    hit_z = lax.broadcasted_iota(jnp.int32, (depth_z, slots), 0) == lax.rem(cells, depth_z)
    hit_z = hit_z.astype(jnp.float32).astype(jnp.bfloat16)
    rest = jnp.where(hit_row, weight, 0.0)
    summed = jnp.zeros((tile_y * slab_x, depth_z), jnp.float32)
    for _ in range(3):
        piece, rest_next = rest.astype(jnp.bfloat16), None
        rest_next = rest - piece.astype(jnp.float32)
        summed = summed + lax.dot_general(
            piece, hit_z, (NT, ((), ())), preferred_element_type=jnp.float32
        )
        rest = rest_next
    thrust[...] = summed

    @pl.when(is_owner)
    def _():
        rows = pl.ds(pl.multiple_of(owner_at * ROWS, ROWS), ROWS)
        full_y = tile_y * tile_count
        sum_sin = sin_xy_ref[...] + jnp.concatenate([mode_z_ref[0, rows, :]] * full_y, axis=0)
        scale = jnp.concatenate([mode_z_ref[1, rows, :]] * full_y, axis=0)
        zero_mode = sum_sin == 0.0
        recip[...] = jnp.where(zero_mode, 0.0, scale / jnp.where(zero_mode, 1.0, sum_sin))

    for load in loads[5:]:
        load.wait()
    old = [
        [old_ref[part, pl.ds(row, slab_x, stride=tile_y), :] for row in range(tile_y)]
        for part in range(3)
    ]

    for step in range(STEPS):
        if step == 0:
            for copy in halos[0]:
                copy.wait_recv()
            unpack_corners(0)

        centre, stress, advect = {}, {}, {}
        for plane in range(1, deep - 1):
            here = [wide[step, part, plane] for part in range(3)]
            d_x = [slope_x(value) for value in here]
            d_y = [
                0.5 * (wide[step, part, plane + 1] - wide[step, part, plane - 1])
                for part in range(3)
            ]
            d_z = [slope_z(value, -1.0) for value in here]
            s_xx, s_yy, s_zz = d_x[0], d_y[1], d_z[2]
            s_xy = 0.5 * (d_x[1] + d_y[0])
            s_xz = 0.5 * (d_x[2] + d_z[0])
            s_yz = 0.5 * (d_y[2] + d_z[1])
            squared = s_xx * s_xx + s_yy * s_yy + s_zz * s_zz
            squared = squared + 2.0 * (s_xy * s_xy + s_xz * s_xz + s_yz * s_yz)
            double = (2.0 * smag_coef) * jnp.sqrt(2.0 * squared + 0.01)
            stress[plane] = [double * s for s in (s_xx, s_yy, s_zz, s_xy, s_xz, s_yz)]
            centre[plane] = here
            advect[plane] = [
                here[0] * d_x[part] + here[1] * d_y[part] + here[2] * d_z[part]
                for part in range(3)
            ]

        @pl.when(in_fringe)
        def _(step=step):
            pltpu.make_async_copy(target.at[step], target.at[step], target_recv.at[step]).wait()

        @pl.when(jnp.logical_not(in_fringe))
        def _(step=step):
            target[step] = wide[step, :, own_y, own_x, :]

        interim, tendency = [], []
        for row in range(tile_y):
            plane = 2 + row
            xx, yy, zz, xy, xz, yz = stress[plane]
            before, after = stress[plane - 1], stress[plane + 1]
            push = [
                slope_x(xx) + 0.5 * (after[3] - before[3]) + slope_z(xz, 0.0),
                slope_x(xy) + 0.5 * (after[1] - before[1]) + slope_z(yz, 0.0),
                slope_x(xz) + 0.5 * (after[5] - before[5]) + slope_z(zz, 0.0),
            ]
            lam = lam_ref[...]
            tend, mid = [], []
            for part in range(3):
                here = centre[plane][part][own_x]
                total = (push[part] - advect[plane][part])[own_x]
                if part == 0:
                    force = thrust[row * slab_x : (row + 1) * slab_x, :]
                    total = total - force * here * jnp.abs(here)
                total = total + lam * (target[step, part, row] - here)
                tend.append(total)
                mid.append(here + time_step * (1.5 * total - 0.5 * old[part][row]))
                if step == STEPS - 1:
                    tend_out[part, pl.ds(row, slab_x, stride=tile_y), :] = total
            tendency.append(tend)
            interim.append(mid)
        if step == STEPS - 1:
            results[1].start()
        old = [[tendency[row][part] for row in range(tile_y)] for part in range(3)]

        share[0:slab_x, :] = 0.5 * interim[0][1]
        last = (planes - 1) * block
        share[last : last + slab_x, :] = -0.5 * interim[tile_y - 1][1]
        for row in range(tile_y):
            along_x, _, along_z = interim[row]
            total = slope_x(along_x, 0.0, 0.0) + slope_z(along_z, -1.0)
            if row + 1 < tile_y:
                total = total + 0.5 * interim[row + 1][1]
            if row > 0:
                total = total - 0.5 * interim[row - 1][1]
            start = (row + 1) * block
            edge = start + slab_x
            share[start:edge, :] = total
            share[edge : edge + 1, :] = 0.5 * along_x[0:1]
            share[edge + 1 : edge + 2, :] = -0.5 * along_x[slab_x - 1 : slab_x]
        coeffs[step] = table_first(cos_ref[...], share[...], NT)

        my_rows = pl.ds(pl.multiple_of(tile * ROWS, ROWS), ROWS)

        first_owner = jnp.where(is_owner, owner_at, lax.rem(me, owners))

        def modes_to(owner, step=step):
            flat = owner + first_tile * sec_count
            return pltpu.make_async_remote_copy(
                src_ref=coeffs.at[step, pl.ds(pl.multiple_of(owner * ROWS, ROWS), ROWS), :],
                dst_ref=plane_in.at[step, sec, my_rows, :],
                send_sem=mode_send.at[step],
                recv_sem=mode_recv.at[step],
                device_id=(lax.rem(flat, sec_count), lax.div(flat, sec_count)),
                device_id_type=MESH,
            )

        def send_modes(ahead, carry):
            modes_to(lax.rem(first_owner + ahead, owners)).start()
            return carry

        lax.fori_loop(1, owners, send_modes, 0, unroll=True)

        @pl.when(is_owner)
        def _(step=step):
            rows = pl.ds(pl.multiple_of(owner_at * ROWS, ROWS), ROWS)
            pltpu.make_async_copy(
                coeffs.at[step, rows, :], plane_in.at[step, sec, my_rows, :], mode_recv.at[step]
            ).start()

        @pl.when(jnp.logical_not(is_owner))
        def _(first_owner=first_owner):
            modes_to(first_owner).start()

        final = step == STEPS - 1
        if not final:
            for part in range(3):
                for row in range(tile_y):
                    wide[step + 1, part, 2 + row, own_x, :] = interim[row][part]
            halos[step + 1] = start_halo(step + 1)
        reach = 1 if final else EDGE
        plane_out, returned = (last_out, last_returned) if final else (wide_out, wide_returned)
        per_tile = LANES // block
        back_planes = tile_y + 2 * reach

        @pl.when(is_owner)
        def _(step=step):
            pltpu.make_async_copy(
                plane_in.at[step], plane_in.at[step], mode_recv.at[step]
            ).wait()
            lane_block = lax.broadcasted_iota(jnp.int32, (group, LANES), 1) // block
            arrived = [plane_in[step, part] for part in range(sec_count)]
            blocks = []
            for plane in range(planes):
                piece = pltpu.roll(arrived[0], -plane * block % LANES, 1)
                for part in range(1, sec_count):
                    other = pltpu.roll(arrived[part], (part - plane) * block % LANES, 1)
                    piece = jnp.where(lane_block == part, other, piece)
                blocks.append(piece)
            stacked = jnp.concatenate(blocks, axis=0)
            modes = table_second(table_first(whole(y_ref[...], planes * group), stacked, NN), whole(x_ref[...], recip.shape[1])) * recip[...]
            skip = (EDGE - reach) * group
            kept = back_planes * group
            back_table = yt_ref[...]
            half = back_table.shape[0] // 2
            back_table = jnp.concatenate(
                [back_table[skip : skip + kept], back_table[half + skip : half + skip + kept]], axis=0
            )
            back_x = table_second(modes, whole(xt_ref[...], LANES))
            spread = table_first(back_table, back_x, NN)
            for part in range(sec_count):
                for first in range(0, back_planes, per_tile):
                    piece = None
                    for place in range(min(per_tile, back_planes - first)):
                        start = (first + place) * group
                        other = spread[start : start + group]
                        other = pltpu.roll(other, (place - part) * block % LANES, 1)
                        piece = other if piece is None else jnp.where(lane_block == place, other, piece)
                    lanes = slice(first // per_tile * LANES, (first // per_tile + 1) * LANES)
                    plane_out[part, :, lanes] = piece
            rows = pl.ds(pl.multiple_of(owner_at * ROWS, ROWS), ROWS)

            pltpu.make_async_copy(
                plane_out.at[sec, my_rows, :], returned.at[rows, :], back_recv.at[step]
            ).start()

            def send_back(ahead, carry):
                other = lax.rem(me + ahead, devices)
                to_sec, to_tile = lax.rem(other, sec_count), lax.div(other, sec_count)
                pltpu.make_async_remote_copy(
                    src_ref=plane_out.at[
                        to_sec, pl.ds(pl.multiple_of(to_tile * ROWS, ROWS), ROWS), :
                    ],
                    dst_ref=returned.at[rows, :],
                    send_sem=back_send.at[step],
                    recv_sem=back_recv.at[step],
                    device_id=(to_sec, to_tile),
                    device_id_type=MESH,
                ).start()
                return carry

            lax.fori_loop(1, devices, send_back, 0, unroll=True)

        pltpu.make_async_copy(returned, returned, back_recv.at[step]).wait()
        columns = returned[...]
        columns = jnp.concatenate(
            [columns[:, i : i + LANES].T for i in range(0, columns.shape[1], LANES)], axis=0
        )
        press[0 : columns.shape[0], :] = table_second(columns, cos_ref[...])

        def press_slopes(start, count):
            here = press[start : start + count, :]
            above = press[start + block : start + block + count, :]
            below = press[start - block : start - block + count, :]
            return here, 0.5 * (above - below), slope_z(here, 1.0)

        if final:
            for row in range(tile_y):
                start = (row + 1) * block + EDGE
                here, along_y, along_z = press_slopes(start, slab_x)
                low = press[start - 1 : start, :]
                high = press[start + slab_x : start + slab_x + 1, :]
                slopes = [slope_x(here, low, high), along_y, along_z]
                for part in range(3):
                    vel_out[part, pl.ds(row, slab_x, stride=tile_y), :] = (
                        interim[row][part] - slopes[part]
                    )
        else:
            for copy in halos[step + 1]:
                copy.wait()
            unpack_corners(step + 1)
            span = slice(ROWS - EDGE, ROWS - EDGE + block)
            for plane in sorted(range(deep), key=lambda at: not 2 <= at < 2 + tile_y):
                if plane == 0:
                    targets[step + 1] = start_target(step + 1)
                here, along_y, along_z = press_slopes((plane + 1) * block, block)
                slopes = [slope_x(here), along_y, along_z]
                for part in range(3):
                    wide[step + 1, part, plane, span, :] = (
                        wide[step + 1, part, plane, span, :] - slopes[part]
                    )

    results[0].start()
    for copy in halos[0]:
        copy.wait_send()
    for step, sends in targets.items():
        plane_out = last_out if step == STEPS - 1 else wide_out

        @pl.when(sec == root)
        def _(sends=sends):
            for send in sends:
                send.wait_send()

        @pl.when(is_owner)
        def _(step=step, plane_out=plane_out):
            most = coeffs.at[step, pl.ds(0, (owners - 1) * ROWS), :]
            pltpu.make_async_copy(most, most, mode_send.at[step]).wait()
            some = plane_out.at[pl.ds(0, sec_count - 1)]
            pltpu.make_async_copy(some, some, back_send.at[step]).wait()
            last = plane_out.at[sec_count - 1, pl.ds(0, group - ROWS), :]
            pltpu.make_async_copy(last, last, back_send.at[step]).wait()

        @pl.when(jnp.logical_not(is_owner))
        def _(step=step):
            pltpu.make_async_copy(coeffs.at[step], coeffs.at[step], mode_send.at[step]).wait()

    for result in results:
        result.wait()


def hand_over(vel_from, tend_from, vel_to, tend_to, held, in_sems, out_sems):
    pieces = []
    for place, (source, end) in enumerate(((vel_from, vel_to), (tend_from, tend_to))):
        for part in range(3):
            slot = 3 * place + part
            pieces.append(
                (
                    pltpu.make_async_copy(source.at[part], held.at[slot], in_sems.at[slot]),
                    pltpu.make_async_copy(held.at[slot], end.at[part], out_sems.at[slot]),
                )
            )
    for arrive, _ in pieces:
        arrive.start()
    for arrive, leave in pieces:
        arrive.wait()
        leave.start()
    for _, leave in pieces:
        leave.wait()


def direct(sec_count, tile_count, velocity, prev_tendency, disk_cells, disk_kind, rotor_weights):
    _, slab_x, tile_y, depth_z = velocity.shape
    constants = [
        jnp.asarray(table) for table in tables(sec_count, tile_count, slab_x, tile_y, depth_z)
    ]
    wide_x = constants[5].shape[1]
    full_y = tile_y * tile_count
    group = tile_count * ROWS
    wide_lanes = (tile_y + 2 * EDGE) * (slab_x + ROWS)
    wide_lanes = -(-wide_lanes // LANES) * LANES
    flat = (3, slab_x * tile_y, depth_z)
    hbm = pl.BlockSpec(memory_space=pltpu.HBM)
    operands = [
        velocity.reshape(flat),
        prev_tendency.reshape(flat),
        disk_cells.reshape(1, -1),
        disk_kind.reshape(1, -1),
        *constants,
    ]
    smem = pl.BlockSpec(memory_space=pltpu.SMEM)
    dma = pltpu.SemaphoreType.DMA
    outs = pl.pallas_call(
        functools.partial(step_kernel, sec_count, tile_count, slab_x, tile_y, depth_z),
        out_shape=[jax.ShapeDtypeStruct(flat, jnp.float32)] * 2,
        in_specs=[hbm] * 4 + [smem] + [hbm] * len(constants),
        out_specs=[hbm] * 2,
        scratch_shapes=[
            pltpu.VMEM((STEPS, 3, tile_y + 4, slab_x + 2 * ROWS, depth_z), jnp.float32),
            pltpu.VMEM((STEPS, 3, tile_y, slab_x, depth_z), jnp.float32),
            pltpu.VMEM((LANES, depth_z), jnp.float32),
            pltpu.VMEM((STEPS, depth_z, LANES), jnp.float32),
            pltpu.VMEM((STEPS, sec_count, group, LANES), jnp.float32),
            pltpu.VMEM((sec_count, group, wide_lanes), jnp.float32),
            pltpu.VMEM((sec_count, group, LANES), jnp.float32),
            pltpu.VMEM((depth_z, wide_lanes), jnp.float32),
            pltpu.VMEM((depth_z, LANES), jnp.float32),
            pltpu.VMEM((wide_lanes, depth_z), jnp.float32),
            pltpu.VMEM((tile_y * slab_x, depth_z), jnp.float32),
            pltpu.VMEM((full_y * ROWS, wide_x), jnp.float32),
            *[pltpu.VMEM(operand.shape, operand.dtype) for operand in operands],
            pltpu.VMEM(flat, jnp.float32),
            pltpu.VMEM(flat, jnp.float32),
            dma((len(operands),)),
            dma((2,)),
            pltpu.VMEM((STEPS, 4, ROWS, depth_z), jnp.float32),
            pltpu.VMEM((STEPS, 4, ROWS, depth_z), jnp.float32),
            dma((STEPS, 8)),
            dma((STEPS, 8)),
            dma((STEPS, 4)),
            dma((STEPS,)),
            dma((STEPS,)),
            dma((STEPS,)),
            dma((STEPS,)),
            dma((STEPS,)),
        ],
        compiler_params=pltpu.CompilerParams(
            collective_id=0, has_side_effects=True, vmem_limit_bytes=60 * 1024 * 1024
        ),
        name="les_steps",
    )(*operands[:4], rotor_weights, *operands[4:])
    outs = pl.pallas_call(
        hand_over,
        out_shape=[jax.ShapeDtypeStruct(flat, jnp.float32)] * 2,
        in_specs=[hbm] * 2,
        out_specs=[hbm] * 2,
        scratch_shapes=[pltpu.VMEM((6, *flat[1:]), jnp.float32), dma((6,)), dma((6,))],
        compiler_params=pltpu.CompilerParams(vmem_limit_bytes=60 * 1024 * 1024),
        name="hand_over",
    )(*outs)
    return tuple(out.reshape(velocity.shape) for out in outs)


def solution(mesh):
    sec_count, tile_count = mesh.shape["sec"], mesh.shape["tile"]
    in_specs = (
        P(None, "sec", "tile", None),
        P(None, "sec", "tile", None),
        P("sec", "tile", None),
        P("sec", "tile", None),
        P(),
    )
    out_specs = (P(None, "sec", "tile", None), P(None, "sec", "tile", None))

    def pick(velocity, *others):
        _, slab_x, tile_y, depth_z = velocity.shape
        owners = depth_z // ROWS
        fits = (
            owners <= sec_count * tile_count
            and owners % sec_count == 0
            and sec_count * (slab_x + ROWS) <= LANES
            and LANES % (slab_x + ROWS) == 0
            and depth_z % LANES == 0
            and slab_x % ROWS == 0
            and tile_y >= 2
            and (tile_y + 2) * (slab_x + ROWS) <= LANES
            and tile_y * tile_count * ROWS <= 512
            and sec_count >= 3
            and tile_count >= 3
        )
        if fits:
            return direct(sec_count, tile_count, velocity, *others)
        return local(velocity, *others)

    return jax.shard_map(pick, mesh=mesh, in_specs=in_specs, out_specs=out_specs, check_vma=False)
```

```python
import functools
import math

import jax
import jax.numpy as jnp
import numpy as np
from jax import lax
from jax.experimental import pallas as pl
from jax.experimental.pallas import tpu as pltpu
from jax.sharding import PartitionSpec as P

STEPS = 2
KINDS = 16
ROWS = 8
LANES = 128
EDGE = 3
MESH = pl.DeviceIdType.MESH

precise = lax.Precision.HIGHEST
time_step = 0.1
fringe_rate = 2.0
smag_coef = 0.04


def extended_2(block, sides, width):
    for axis, dim in sides:
        count = lax.axis_size(axis)
        forward = [(i, i + 1) for i in range(count - 1)]
        forward.append((count - 1, 0))
        backward = [(target, source) for source, target in forward]
        low = lax.ppermute(
            lax.slice_in_dim(block, block.shape[dim] - width, None, axis=dim), axis, forward
        )
        high = lax.ppermute(lax.slice_in_dim(block, 0, width, axis=dim), axis, backward)
        block = jnp.concatenate([low, block, high], axis=dim)
    return block


def from_root(block, axis, owner):
    block = jnp.where(lax.axis_index(axis) == owner, block, jnp.zeros_like(block))
    return lax.psum(block, axis)


def gradients(padded, z_sign):
    centre = padded[:, 1:-1, 1:-1, :]
    grad_x = 0.5 * (padded[:, 2:, 1:-1, :] - padded[:, :-2, 1:-1, :])
    grad_y = 0.5 * (padded[:, 1:-1, 2:, :] - padded[:, 1:-1, :-2, :])
    extended = jnp.concatenate(
        [z_sign * centre[..., :1], centre, z_sign * centre[..., -1:]], axis=-1
    )
    grad_z = 0.5 * (extended[..., 2:] - extended[..., :-2])
    return (grad_x, grad_y, grad_z)


def strain_stress(slopes):

    def strain(first, second):
        return 0.5 * (slopes[second][first] + slopes[first][second])

    strain_xx = strain(0, 0)
    strain_yy = strain(1, 1)
    strain_zz = strain(2, 2)
    strain_xy = strain(0, 1)
    strain_xz = strain(0, 2)
    strain_yz = strain(1, 2)
    squared = strain_xx * strain_xx + strain_yy * strain_yy + strain_zz * strain_zz
    squared = squared + 2.0 * (
        strain_xy * strain_xy + strain_xz * strain_xz + strain_yz * strain_yz
    )
    double = 2.0 * (smag_coef * jnp.sqrt(2.0 * squared + 0.01))
    return jnp.stack(
        [
            double * strain_xx,
            double * strain_yy,
            double * strain_zz,
            double * strain_xy,
            double * strain_xz,
            double * strain_yz,
        ]
    )


def advection(slopes, centre):
    return centre[0:1] * slopes[0] + centre[1:2] * slopes[1] + centre[2:3] * slopes[2]


def stress_force(padded):
    grad_x, grad_y, grad_z = gradients(padded, 0.0)
    return jnp.stack(
        [
            grad_x[0] + grad_y[3] + grad_z[4],
            grad_x[3] + grad_y[1] + grad_z[5],
            grad_x[4] + grad_y[5] + grad_z[2],
        ]
    )


def faces(source):
    return extended_2(source, (("sec", 1), ("tile", 2)), 1)


def sec_turn(blocks):
    return lax.all_to_all(blocks, "sec", split_axis=0, concat_axis=0, tiled=True)


def tile_turn(blocks):
    return lax.all_to_all(blocks, "tile", split_axis=0, concat_axis=0, tiled=True)


def hartley_table(length):
    index_row = jnp.arange(length)
    product = index_row[:, None] * index_row[None, :] % length
    angle = 2.0 * math.pi / length * product.astype(jnp.float32)
    return jnp.cos(angle) + jnp.sin(angle)


def local(velocity, prev_tendency, disk_cells, disk_kind, rotor_weights):
    sec_count = lax.axis_size("sec")
    tile_count = lax.axis_size("tile")
    sec_at = lax.axis_index("sec")
    tile_at = lax.axis_index("tile")
    slab_x = velocity.shape[1]
    tile_y = velocity.shape[2]
    depth_z = velocity.shape[3]
    full_x = slab_x * sec_count
    full_y = tile_y * tile_count
    part_z = depth_z // sec_count
    modes_each = slab_x * depth_z // tile_count
    cell_count = slab_x * tile_y * depth_z
    modes = jnp.arange(depth_z).astype(jnp.float32)[:, None]
    points = jnp.arange(depth_z).astype(jnp.float32)[None, :] + 0.5
    cos_blocks = jnp.cos(math.pi * modes * points / depth_z).reshape(sec_count, part_z, depth_z)
    weight_blocks = jnp.where(jnp.arange(depth_z) == 0, 1.0 / depth_z, 2.0 / depth_z).astype(
        jnp.float32
    )
    weight_blocks = weight_blocks.reshape(sec_count, part_z)
    x_table = hartley_table(full_x)
    y_table = hartley_table(full_y).reshape(full_y, tile_count, tile_y)
    flat_ids = tile_at * modes_each + jnp.arange(modes_each)
    mode_x = flat_ids // part_z
    mode_z = sec_at * part_z + flat_ids % part_z
    mode_y = jnp.arange(full_y)
    sin_x = jnp.sin(2.0 * math.pi * mode_x.astype(jnp.float32) / full_x)
    sin_y = jnp.sin(2.0 * math.pi * mode_y.astype(jnp.float32) / full_y)
    sin_z = jnp.sin(math.pi * mode_z.astype(jnp.float32) / depth_z)
    eigen = -((sin_x * sin_x)[:, None] + (sin_y * sin_y)[None, :] + (sin_z * sin_z)[:, None])
    zero_mode = (
        (mode_x % (full_x // 2) == 0)[:, None]
        & (mode_y % (full_y // 2) == 0)[None, :]
        & (mode_z == 0)[:, None]
    )
    recip = jnp.where(zero_mode, 0.0, 1.0 / jnp.where(zero_mode, 1.0, eigen))
    slab_pos = jnp.sin(math.pi * (jnp.arange(slab_x).astype(jnp.float32) + 0.5) / slab_x)
    lam_x = fringe_rate * (slab_pos * slab_pos)
    flag = (
        (sec_at == 0)
        | (sec_at == sec_count // 2)
        | (sec_at == 3 * sec_count // 4)
        | (sec_at == sec_count - 1)
    ).astype(jnp.float32)
    picked = disk_cells.reshape(-1)
    kinds = disk_kind.reshape(-1)
    live = picked < cell_count
    safe = jnp.minimum(picked, cell_count - 1)
    weight = jnp.sum(
        jnp.where(kinds[:, None] == jnp.arange(KINDS)[None, :], rotor_weights[None, :], 0.0), axis=1
    )
    current = velocity
    tendency_old = prev_tendency
    tendency = prev_tendency
    for step_no in range(STEPS):
        wide = extended_2(current, (("sec", 1), ("tile", 2)), 2)
        wide_slopes = gradients(wide, -1.0)
        push_field = stress_force(strain_stress(wide_slopes))
        slopes = tuple((piece[:, 1:-1, 1:-1, :] for piece in wide_slopes))
        advect = advection(slopes, current)
        target = from_root(current, "sec", sec_count // 2 - 1)
        fringe = flag * lam_x[None, :, None, None] * (target - current)
        sampled = current[0].reshape(-1)[safe]
        push = jnp.where(live, -(weight * sampled * jnp.abs(sampled)), 0.0)
        turbine = (
            jnp.zeros((cell_count,), jnp.float32)
            .at[safe]
            .add(push)
            .reshape(slab_x, tile_y, depth_z)
        )
        empty = jnp.zeros_like(turbine)
        tendency = push_field - advect + jnp.stack([turbine, empty, empty]) + fringe
        interim = current + time_step * (1.5 * tendency - 0.5 * tendency_old)
        grad_x, grad_y, grad_z = gradients(faces(interim), -1.0)
        rhs = grad_x[0] + grad_y[1] + grad_z[2]
        coeffs = jnp.einsum("xyz,bcz->bxyc", rhs, cos_blocks, precision=precise)
        gathered = sec_turn(coeffs).reshape(full_x, tile_y, part_z)
        along_x = jnp.einsum("xyc,kx->kcy", gathered, x_table, precision=precise)
        spread = tile_turn(along_x.reshape(tile_count, modes_each, tile_y))
        along_y = jnp.einsum("sqt,lst->ql", spread, y_table, precision=precise)
        scaled = along_y * recip
        back_y = jnp.einsum("ql,lst->sqt", scaled, y_table, precision=precise) / (full_x * full_y)
        returned = tile_turn(back_y).reshape(full_x, part_z, tile_y)
        back_x = jnp.einsum("kcy,kx->xyc", returned, x_table, precision=precise)
        home = sec_turn(back_x.reshape(sec_count, slab_x, tile_y, part_z))
        pressure = jnp.einsum(
            "bxyc,bcz->xyz", home * weight_blocks[:, None, None, :], cos_blocks, precision=precise
        )
        press_x, press_y, press_z = gradients(faces(pressure[None]), 1.0)
        current = interim - jnp.concatenate([press_x, press_y, press_z], axis=0)
        tendency_old = tendency
    return (current, tendency)


def cas_table(first, second, length):
    angle = 2.0 * np.pi / length * (np.outer(first, second) % length)
    return np.cos(angle) + np.sin(angle)


def halves(table):
    high = table.astype(np.float32).astype(jnp.bfloat16)
    low = (table - high.astype(np.float64)).astype(np.float32).astype(jnp.bfloat16)
    stacked = np.concatenate([high, low], axis=0)
    return np.concatenate(np.split(stacked, stacked.shape[1] // LANES, axis=1), axis=0)


def whole(table, columns):
    count = table.shape[0] * LANES // columns
    parts = [table[i * count : (i + 1) * count] for i in range(columns // LANES)]
    return jnp.concatenate(parts, axis=1)


def tables(sec_count, tile_count, slab_x, tile_y, depth_z):
    full_x, full_y = slab_x * sec_count, tile_y * tile_count
    wide_x = -(-full_x // LANES) * LANES
    planes, block = tile_y + 2, slab_x + ROWS
    z_at = np.arange(depth_z)
    cos_z = np.cos(np.pi / depth_z * np.outer(z_at, z_at + 0.5))
    x_cas = np.zeros((LANES, wide_x))
    x_back = np.zeros((LANES, wide_x))
    for sec in range(sec_count):
        start = sec * slab_x
        cells = np.concatenate([start + np.arange(slab_x), [start - 1, start + slab_x]]) % full_x
        x_cas[sec * block : sec * block + slab_x + 2, :full_x] = cas_table(
            cells, np.arange(full_x), full_x
        )
        cells = np.arange(start - EDGE, start + slab_x + EDGE) % full_x
        x_back[sec * block : sec * block + slab_x + 2 * EDGE, :full_x] = cas_table(
            cells, np.arange(full_x), full_x
        )
    y_blocks = []
    for plane in range(1 - EDGE, planes + EDGE - 1):
        y_at = (np.arange(tile_count) * tile_y + plane - 1) % full_y
        y_blocks.append(np.kron(cas_table(np.arange(full_y), y_at, full_y), np.eye(ROWS)))
    y_cas = np.concatenate(y_blocks[EDGE - 1 : EDGE - 1 + planes], axis=1)
    y_back = np.concatenate(y_blocks, axis=1).T
    k_x, k_y = np.arange(full_x), np.arange(full_y)
    sin_x = np.where(k_x % (full_x // 2) == 0, 0.0, np.sin(2.0 * np.pi * k_x / full_x) ** 2)
    sin_y = np.where(k_y % (full_y // 2) == 0, 0.0, np.sin(2.0 * np.pi * k_y / full_y) ** 2)
    sin_xy = np.ones((full_y * ROWS, wide_x), np.float32)
    sin_xy[:, :full_x] = np.repeat(sin_y, ROWS)[:, None] + sin_x[None, :]
    sin_z = np.sin(np.pi * z_at / depth_z) ** 2
    weight_z = -np.where(z_at == 0, 1.0, 2.0) / (depth_z * full_x * full_y)
    mode_z = np.stack([sin_z, weight_z]).astype(np.float32)
    mode_z = np.ascontiguousarray(np.broadcast_to(mode_z[:, :, None], (2, depth_z, wide_x)))
    lam = fringe_rate * np.sin(np.pi * (np.arange(slab_x) + 0.5) / slab_x) ** 2
    lam = np.ascontiguousarray(np.broadcast_to(lam.astype(np.float32)[:, None], (slab_x, depth_z)))
    return (
        halves(cos_z),
        halves(x_cas),
        halves(x_back.T),
        halves(y_cas),
        halves(y_back),
        sin_xy,
        mode_z,
        lam,
    )


def split(value):
    high = value.astype(jnp.bfloat16)
    return high, (value - high.astype(jnp.float32)).astype(jnp.bfloat16)


def dot(first, second, dims):
    return lax.dot_general(first, second, (dims, ((), ())), preferred_element_type=jnp.float32)


def table_first(table, second, dims):
    count = table.shape[0] // 2
    high, low = split(second)
    both = dot(table, high, dims)
    return both[:count] + (both[count:] + dot(table[:count], low, dims))


def table_second(first, table):
    count, depth = first.shape[0], table.shape[0] // 2
    high, low = split(first)
    both = dot(jnp.concatenate([high, low], axis=0), table[:depth], NN)
    return both[:count] + (both[count:] + dot(high, table[depth:], NN))


NN = ((1,), (0,))
NT = ((1,), (1,))


def slope_z(value, z_sign):
    depth = value.shape[1]
    lane = lax.broadcasted_iota(jnp.int32, value.shape, 1)
    edge = value * z_sign
    above = jnp.where(lane == depth - 1, edge, pltpu.roll(value, depth - 1, 1))
    below = jnp.where(lane == 0, edge, pltpu.roll(value, 1, 1))
    return 0.5 * (above - below)


def slope_x(value, low=None, high=None):
    count = value.shape[0]
    after = pltpu.roll(value, count - 1, 0)
    before = pltpu.roll(value, 1, 0)
    if low is not None:
        row = lax.broadcasted_iota(jnp.int32, value.shape, 0)
        after = jnp.where(row == count - 1, high, after)
        before = jnp.where(row == 0, low, before)
    return 0.5 * (after - before)


def step_kernel(
    sec_count,
    tile_count,
    slab_x,
    tile_y,
    depth_z,
    vel_hbm,
    old_hbm,
    cells_hbm,
    kinds_hbm,
    weights_ref,
    cos_hbm,
    x_hbm,
    xt_hbm,
    y_hbm,
    yt_hbm,
    sin_xy_hbm,
    mode_z_hbm,
    lam_hbm,
    vel_result,
    tend_result,
    wide,
    target,
    share,
    coeffs,
    plane_in,
    wide_out,
    last_out,
    wide_returned,
    last_returned,
    press,
    thrust,
    recip,
    vel_ref,
    old_ref,
    cells_ref,
    kinds_ref,
    cos_ref,
    x_ref,
    xt_ref,
    y_ref,
    yt_ref,
    sin_xy_ref,
    mode_z_ref,
    lam_ref,
    vel_out,
    tend_out,
    load_sem,
    result_sem,
    corner_out,
    corner_in,
    halo_send,
    halo_recv,
    target_send,
    target_recv,
    mode_send,
    mode_recv,
    back_send,
    back_recv,
):
    sec = lax.axis_index("sec")
    tile = lax.axis_index("tile")
    devices = sec_count * tile_count
    me = tile * sec_count + sec
    owners = depth_z // ROWS
    planes = tile_y + 2
    deep = tile_y + 4
    group = tile_count * ROWS
    block = slab_x + ROWS
    root = sec_count // 2 - 1
    fringes = sorted({0, sec_count // 2, 3 * sec_count // 4, sec_count - 1} - {root})
    first_tile = (tile_count - owners // sec_count) // 2
    is_owner = (tile >= first_tile) & (tile < first_tile + owners // sec_count)
    owner_at = (tile - first_tile) * sec_count + sec
    in_fringe = functools.reduce(jnp.logical_or, [sec == which for which in fringes])
    low_sec, high_sec = lax.rem(sec + sec_count - 1, sec_count), lax.rem(sec + 1, sec_count)
    low_tile, high_tile = lax.rem(tile + tile_count - 1, tile_count), lax.rem(tile + 1, tile_count)
    end_x = ROWS + slab_x
    own_x, own_y = slice(ROWS, end_x), slice(2, 2 + tile_y)

    loads = [
        pltpu.make_async_copy(source, held, load_sem.at[place])
        for place, (source, held) in enumerate(
            (
                (vel_hbm, vel_ref),
                (cells_hbm, cells_ref),
                (kinds_hbm, kinds_ref),
                (sin_xy_hbm, sin_xy_ref),
                (mode_z_hbm, mode_z_ref),
                (old_hbm, old_ref),
                (lam_hbm, lam_ref),
                (cos_hbm, cos_ref),
                (y_hbm, y_ref),
                (x_hbm, x_ref),
                (xt_hbm, xt_ref),
                (yt_hbm, yt_ref),
            )
        )
    ]
    for load in loads:
        load.start()

    results = [
        pltpu.make_async_copy(vel_out, vel_result, result_sem.at[0]),
        pltpu.make_async_copy(tend_out, tend_result, result_sem.at[1]),
    ]

    barrier = pltpu.get_barrier_semaphore()

    def greet(ahead, carry):
        other = lax.rem(me + ahead, devices)
        pl.semaphore_signal(
            barrier,
            inc=1,
            device_id=(lax.rem(other, sec_count), lax.div(other, sec_count)),
            device_id_type=MESH,
        )
        return carry

    lax.fori_loop(1, devices, greet, 0)

    share[...] = jnp.zeros_like(share)
    corner_out[...] = jnp.zeros_like(corner_out)
    loads[0].wait()
    for part in range(3):
        for row in range(tile_y):
            wide[0, part, 2 + row, own_x, :] = vel_ref[part, pl.ds(row, slab_x, stride=tile_y), :]

    pl.semaphore_wait(barrier, devices - 1)

    def start_halo(step):
        xs = {
            -1: (low_sec, slice(ROWS, 2 * ROWS), slice(end_x, end_x + ROWS)),
            0: (sec, own_x, own_x),
            1: (high_sec, slice(end_x - ROWS, end_x), slice(0, ROWS)),
        }
        ys = {
            -1: (low_tile, slice(2, 4), slice(2 + tile_y, deep)),
            0: (tile, own_y, own_y),
            1: (high_tile, slice(tile_y, 2 + tile_y), slice(0, 2)),
        }
        copies = []
        for x_way in (0, -1, 1):
            for y_way in (-1, 0, 1):
                if x_way == 0 and y_way == 0:
                    continue
                slot = len(copies)
                to_sec, x_from, x_to = xs[x_way]
                to_tile, y_from, y_to = ys[y_way]
                source = wide.at[step, :, y_from, x_from, :]
                end = wide.at[step, :, y_to, x_to, :]
                if x_way != 0 and y_way != 0:
                    corner = x_way + 1 + (y_way + 1) // 2
                    plane = 2 if y_way < 0 else 1 + tile_y
                    row = ROWS if x_way < 0 else end_x - 1
                    for part in range(3):
                        corner_out[step, corner, part : part + 1, :] = wide[
                            step, part, plane, row : row + 1, :
                        ]
                    source, end = corner_out.at[step, corner], corner_in.at[step, corner]
                copy = pltpu.make_async_remote_copy(
                    src_ref=source,
                    dst_ref=end,
                    send_sem=halo_send.at[step, slot],
                    recv_sem=halo_recv.at[step, slot],
                    device_id=(to_sec, to_tile),
                    device_id_type=MESH,
                )
                copies.append(copy)
        for copy in copies:
            copy.start()
        return copies

    def unpack_corners(step):
        for x_way in (-1, 1):
            for y_way in (-1, 1):
                corner = x_way + 1 + (y_way + 1) // 2
                plane = 2 + tile_y if y_way < 0 else 1
                row = end_x if x_way < 0 else ROWS - 1
                for part in range(3):
                    wide[step, part, plane, row : row + 1, :] = corner_in[
                        step, corner, part : part + 1, :
                    ]

    def start_target(step):
        sends = [
            pltpu.make_async_remote_copy(
                src_ref=wide.at[step, :, own_y, own_x, :],
                dst_ref=target.at[step],
                send_sem=target_send.at[step, place],
                recv_sem=target_recv.at[step],
                device_id=(which, tile),
                device_id_type=MESH,
            )
            for place, which in enumerate(fringes)
        ]

        @pl.when(sec == root)
        def _():
            for send in sends:
                send.start()

        return sends

    halos = {0: start_halo(0)}
    targets = {0: start_target(0)}

    for load in loads[1:5]:
        load.wait()
    cells = cells_ref[...]
    kinds = kinds_ref[...]
    weight = jnp.zeros(cells.shape, jnp.float32)
    for kind in range(KINDS):
        weight = jnp.where(kinds == kind, weights_ref[kind], weight)
    weight = jnp.where(cells < slab_x * tile_y * depth_z, weight, 0.0)
    column = lax.div(cells, depth_z)
    row_of = lax.rem(column, tile_y) * slab_x + lax.div(column, tile_y)
    slots = cells.shape[1]
    hit_row = lax.broadcasted_iota(jnp.int32, (tile_y * slab_x, slots), 0) == row_of
    hit_z = lax.broadcasted_iota(jnp.int32, (depth_z, slots), 0) == lax.rem(cells, depth_z)
    hit_z = hit_z.astype(jnp.float32).astype(jnp.bfloat16)
    rest = jnp.where(hit_row, weight, 0.0)
    summed = jnp.zeros((tile_y * slab_x, depth_z), jnp.float32)
    for _ in range(3):
        piece, rest_next = rest.astype(jnp.bfloat16), None
        rest_next = rest - piece.astype(jnp.float32)
        summed = summed + lax.dot_general(
            piece, hit_z, (NT, ((), ())), preferred_element_type=jnp.float32
        )
        rest = rest_next
    thrust[...] = summed

    @pl.when(is_owner)
    def _():
        rows = pl.ds(pl.multiple_of(owner_at * ROWS, ROWS), ROWS)
        full_y = tile_y * tile_count
        sum_sin = sin_xy_ref[...] + jnp.concatenate([mode_z_ref[0, rows, :]] * full_y, axis=0)
        scale = jnp.concatenate([mode_z_ref[1, rows, :]] * full_y, axis=0)
        zero_mode = sum_sin == 0.0
        recip[...] = jnp.where(zero_mode, 0.0, scale / jnp.where(zero_mode, 1.0, sum_sin))

    for load in loads[5:]:
        load.wait()
    old = [
        [old_ref[part, pl.ds(row, slab_x, stride=tile_y), :] for row in range(tile_y)]
        for part in range(3)
    ]

    for step in range(STEPS):
        if step == 0:
            for copy in halos[0]:
                copy.wait_recv()
            unpack_corners(0)

        centre, stress, advect = {}, {}, {}
        for plane in range(1, deep - 1):
            here = [wide[step, part, plane] for part in range(3)]
            d_x = [slope_x(value) for value in here]
            d_y = [
                0.5 * (wide[step, part, plane + 1] - wide[step, part, plane - 1])
                for part in range(3)
            ]
            d_z = [slope_z(value, -1.0) for value in here]
            s_xx, s_yy, s_zz = d_x[0], d_y[1], d_z[2]
            s_xy = 0.5 * (d_x[1] + d_y[0])
            s_xz = 0.5 * (d_x[2] + d_z[0])
            s_yz = 0.5 * (d_y[2] + d_z[1])
            squared = s_xx * s_xx + s_yy * s_yy + s_zz * s_zz
            squared = squared + 2.0 * (s_xy * s_xy + s_xz * s_xz + s_yz * s_yz)
            double = (2.0 * smag_coef) * jnp.sqrt(2.0 * squared + 0.01)
            stress[plane] = [double * s for s in (s_xx, s_yy, s_zz, s_xy, s_xz, s_yz)]
            centre[plane] = here
            advect[plane] = [
                here[0] * d_x[part] + here[1] * d_y[part] + here[2] * d_z[part]
                for part in range(3)
            ]

        @pl.when(in_fringe)
        def _(step=step):
            pltpu.make_async_copy(target.at[step], target.at[step], target_recv.at[step]).wait()

        @pl.when(jnp.logical_not(in_fringe))
        def _(step=step):
            target[step] = wide[step, :, own_y, own_x, :]

        interim, tendency = [], []
        for row in range(tile_y):
            plane = 2 + row
            xx, yy, zz, xy, xz, yz = stress[plane]
            before, after = stress[plane - 1], stress[plane + 1]
            push = [
                slope_x(xx) + 0.5 * (after[3] - before[3]) + slope_z(xz, 0.0),
                slope_x(xy) + 0.5 * (after[1] - before[1]) + slope_z(yz, 0.0),
                slope_x(xz) + 0.5 * (after[5] - before[5]) + slope_z(zz, 0.0),
            ]
            lam = lam_ref[...]
            tend, mid = [], []
            for part in range(3):
                here = centre[plane][part][own_x]
                total = (push[part] - advect[plane][part])[own_x]
                if part == 0:
                    force = thrust[row * slab_x : (row + 1) * slab_x, :]
                    total = total - force * here * jnp.abs(here)
                total = total + lam * (target[step, part, row] - here)
                tend.append(total)
                mid.append(here + time_step * (1.5 * total - 0.5 * old[part][row]))
                if step == STEPS - 1:
                    tend_out[part, pl.ds(row, slab_x, stride=tile_y), :] = total
            tendency.append(tend)
            interim.append(mid)
        if step == STEPS - 1:
            results[1].start()
        old = [[tendency[row][part] for row in range(tile_y)] for part in range(3)]

        share[0:slab_x, :] = 0.5 * interim[0][1]
        last = (planes - 1) * block
        share[last : last + slab_x, :] = -0.5 * interim[tile_y - 1][1]
        for row in range(tile_y):
            along_x, _, along_z = interim[row]
            total = slope_x(along_x, 0.0, 0.0) + slope_z(along_z, -1.0)
            if row + 1 < tile_y:
                total = total + 0.5 * interim[row + 1][1]
            if row > 0:
                total = total - 0.5 * interim[row - 1][1]
            start = (row + 1) * block
            edge = start + slab_x
            share[start:edge, :] = total
            share[edge : edge + 1, :] = 0.5 * along_x[0:1]
            share[edge + 1 : edge + 2, :] = -0.5 * along_x[slab_x - 1 : slab_x]
        coeffs[step] = table_first(cos_ref[...], share[...], NT)

        my_rows = pl.ds(pl.multiple_of(tile * ROWS, ROWS), ROWS)

        far_half = jnp.where(tile < tile_count // 2, 0, owners // 2)
        first_owner = jnp.where(is_owner, owner_at, lax.rem(me, owners // 2) + far_half)

        def modes_to(owner, step=step):
            flat = owner + first_tile * sec_count
            return pltpu.make_async_remote_copy(
                src_ref=coeffs.at[step, pl.ds(pl.multiple_of(owner * ROWS, ROWS), ROWS), :],
                dst_ref=plane_in.at[step, sec, my_rows, :],
                send_sem=mode_send.at[step],
                recv_sem=mode_recv.at[step],
                device_id=(lax.rem(flat, sec_count), lax.div(flat, sec_count)),
                device_id_type=MESH,
            )

        for ahead in (*range(owners // 2, owners), *range(1, owners // 2)):
            modes_to(lax.rem(first_owner + ahead, owners)).start()

        @pl.when(is_owner)
        def _(step=step):
            rows = pl.ds(pl.multiple_of(owner_at * ROWS, ROWS), ROWS)
            pltpu.make_async_copy(
                coeffs.at[step, rows, :], plane_in.at[step, sec, my_rows, :], mode_recv.at[step]
            ).start()

        @pl.when(jnp.logical_not(is_owner))
        def _(first_owner=first_owner):
            modes_to(first_owner).start()

        final = step == STEPS - 1
        if not final:
            for part in range(3):
                for row in range(tile_y):
                    wide[step + 1, part, 2 + row, own_x, :] = interim[row][part]
            halos[step + 1] = start_halo(step + 1)
        reach = 1 if final else EDGE
        plane_out, returned = (last_out, last_returned) if final else (wide_out, wide_returned)
        per_tile = LANES // block
        back_planes = tile_y + 2 * reach

        @pl.when(is_owner)
        def _(step=step):
            pltpu.make_async_copy(
                plane_in.at[step], plane_in.at[step], mode_recv.at[step]
            ).wait()
            lane_block = lax.broadcasted_iota(jnp.int32, (group, LANES), 1) // block
            arrived = [plane_in[step, part] for part in range(sec_count)]
            blocks = []
            for plane in range(planes):
                piece = pltpu.roll(arrived[0], -plane * block % LANES, 1)
                for part in range(1, sec_count):
                    other = pltpu.roll(arrived[part], (part - plane) * block % LANES, 1)
                    piece = jnp.where(lane_block == part, other, piece)
                blocks.append(piece)
            stacked = jnp.concatenate(blocks, axis=0)
            modes = table_second(table_first(whole(y_ref[...], planes * group), stacked, NN), whole(x_ref[...], recip.shape[1])) * recip[...]
            skip = (EDGE - reach) * group
            kept = back_planes * group
            back_table = yt_ref[...]
            half = back_table.shape[0] // 2
            back_table = jnp.concatenate(
                [back_table[skip : skip + kept], back_table[half + skip : half + skip + kept]], axis=0
            )
            back_x = table_second(modes, whole(xt_ref[...], LANES))
            spread = table_first(back_table, back_x, NN)
            for part in range(sec_count):
                for first in range(0, back_planes, per_tile):
                    piece = None
                    for place in range(min(per_tile, back_planes - first)):
                        start = (first + place) * group
                        other = spread[start : start + group]
                        other = pltpu.roll(other, (place - part) * block % LANES, 1)
                        piece = other if piece is None else jnp.where(lane_block == place, other, piece)
                    lanes = slice(first // per_tile * LANES, (first // per_tile + 1) * LANES)
                    plane_out[part, :, lanes] = piece
            rows = pl.ds(pl.multiple_of(owner_at * ROWS, ROWS), ROWS)

            pltpu.make_async_copy(
                plane_out.at[sec, my_rows, :], returned.at[rows, :], back_recv.at[step]
            ).start()

            def send_back(count, carry):
                away = lax.div(count + 1, 2) * (1 - 2 * lax.rem(count, 2))
                other = lax.rem(me + devices // 2 + away + devices, devices)
                to_sec, to_tile = lax.rem(other, sec_count), lax.div(other, sec_count)
                pltpu.make_async_remote_copy(
                    src_ref=plane_out.at[
                        to_sec, pl.ds(pl.multiple_of(to_tile * ROWS, ROWS), ROWS), :
                    ],
                    dst_ref=returned.at[rows, :],
                    send_sem=back_send.at[step],
                    recv_sem=back_recv.at[step],
                    device_id=(to_sec, to_tile),
                    device_id_type=MESH,
                ).start()
                return carry

            lax.fori_loop(0, devices - 1, send_back, 0, unroll=True)

        pltpu.make_async_copy(returned, returned, back_recv.at[step]).wait()
        columns = returned[...]
        columns = jnp.concatenate(
            [columns[:, i : i + LANES].T for i in range(0, columns.shape[1], LANES)], axis=0
        )
        press[0 : columns.shape[0], :] = table_second(columns, cos_ref[...])

        def press_slopes(start, count):
            here = press[start : start + count, :]
            above = press[start + block : start + block + count, :]
            below = press[start - block : start - block + count, :]
            return here, 0.5 * (above - below), slope_z(here, 1.0)

        if final:
            for row in range(tile_y):
                start = (row + 1) * block + EDGE
                here, along_y, along_z = press_slopes(start, slab_x)
                low = press[start - 1 : start, :]
                high = press[start + slab_x : start + slab_x + 1, :]
                slopes = [slope_x(here, low, high), along_y, along_z]
                for part in range(3):
                    vel_out[part, pl.ds(row, slab_x, stride=tile_y), :] = (
                        interim[row][part] - slopes[part]
                    )
        else:
            for copy in halos[step + 1]:
                copy.wait()
            unpack_corners(step + 1)
            span = slice(ROWS - EDGE, ROWS - EDGE + block)
            for plane in sorted(range(deep), key=lambda at: not 2 <= at < 2 + tile_y):
                if plane == 0:
                    targets[step + 1] = start_target(step + 1)
                here, along_y, along_z = press_slopes((plane + 1) * block, block)
                slopes = [slope_x(here), along_y, along_z]
                for part in range(3):
                    wide[step + 1, part, plane, span, :] = (
                        wide[step + 1, part, plane, span, :] - slopes[part]
                    )

    results[0].start()
    for copy in halos[0]:
        copy.wait_send()
    for step, sends in targets.items():
        plane_out = last_out if step == STEPS - 1 else wide_out

        @pl.when(sec == root)
        def _(sends=sends):
            for send in sends:
                send.wait_send()

        @pl.when(is_owner)
        def _(step=step, plane_out=plane_out):
            most = coeffs.at[step, pl.ds(0, (owners - 1) * ROWS), :]
            pltpu.make_async_copy(most, most, mode_send.at[step]).wait()
            some = plane_out.at[pl.ds(0, sec_count - 1)]
            pltpu.make_async_copy(some, some, back_send.at[step]).wait()
            last = plane_out.at[sec_count - 1, pl.ds(0, group - ROWS), :]
            pltpu.make_async_copy(last, last, back_send.at[step]).wait()

        @pl.when(jnp.logical_not(is_owner))
        def _(step=step):
            pltpu.make_async_copy(coeffs.at[step], coeffs.at[step], mode_send.at[step]).wait()

    for result in results:
        result.wait()


def hand_over(vel_from, tend_from, vel_to, tend_to, held, in_sems, out_sems):
    pieces = []
    for place, (source, end) in enumerate(((vel_from, vel_to), (tend_from, tend_to))):
        for part in range(3):
            slot = 3 * place + part
            pieces.append(
                (
                    pltpu.make_async_copy(source.at[part], held.at[slot], in_sems.at[slot]),
                    pltpu.make_async_copy(held.at[slot], end.at[part], out_sems.at[slot]),
                )
            )
    for arrive, _ in pieces:
        arrive.start()
    for arrive, leave in pieces:
        arrive.wait()
        leave.start()
    for _, leave in pieces:
        leave.wait()


def direct(sec_count, tile_count, velocity, prev_tendency, disk_cells, disk_kind, rotor_weights):
    _, slab_x, tile_y, depth_z = velocity.shape
    constants = [
        jnp.asarray(table) for table in tables(sec_count, tile_count, slab_x, tile_y, depth_z)
    ]
    wide_x = constants[5].shape[1]
    full_y = tile_y * tile_count
    group = tile_count * ROWS
    wide_lanes = (tile_y + 2 * EDGE) * (slab_x + ROWS)
    wide_lanes = -(-wide_lanes // LANES) * LANES
    flat = (3, slab_x * tile_y, depth_z)
    hbm = pl.BlockSpec(memory_space=pltpu.HBM)
    operands = [
        velocity.reshape(flat),
        prev_tendency.reshape(flat),
        disk_cells.reshape(1, -1),
        disk_kind.reshape(1, -1),
        *constants,
    ]
    smem = pl.BlockSpec(memory_space=pltpu.SMEM)
    dma = pltpu.SemaphoreType.DMA
    outs = pl.pallas_call(
        functools.partial(step_kernel, sec_count, tile_count, slab_x, tile_y, depth_z),
        out_shape=[jax.ShapeDtypeStruct(flat, jnp.float32)] * 2,
        in_specs=[hbm] * 4 + [smem] + [hbm] * len(constants),
        out_specs=[hbm] * 2,
        scratch_shapes=[
            pltpu.VMEM((STEPS, 3, tile_y + 4, slab_x + 2 * ROWS, depth_z), jnp.float32),
            pltpu.VMEM((STEPS, 3, tile_y, slab_x, depth_z), jnp.float32),
            pltpu.VMEM((LANES, depth_z), jnp.float32),
            pltpu.VMEM((STEPS, depth_z, LANES), jnp.float32),
            pltpu.VMEM((STEPS, sec_count, group, LANES), jnp.float32),
            pltpu.VMEM((sec_count, group, wide_lanes), jnp.float32),
            pltpu.VMEM((sec_count, group, LANES), jnp.float32),
            pltpu.VMEM((depth_z, wide_lanes), jnp.float32),
            pltpu.VMEM((depth_z, LANES), jnp.float32),
            pltpu.VMEM((wide_lanes, depth_z), jnp.float32),
            pltpu.VMEM((tile_y * slab_x, depth_z), jnp.float32),
            pltpu.VMEM((full_y * ROWS, wide_x), jnp.float32),
            *[pltpu.VMEM(operand.shape, operand.dtype) for operand in operands],
            pltpu.VMEM(flat, jnp.float32),
            pltpu.VMEM(flat, jnp.float32),
            dma((len(operands),)),
            dma((2,)),
            pltpu.VMEM((STEPS, 4, ROWS, depth_z), jnp.float32),
            pltpu.VMEM((STEPS, 4, ROWS, depth_z), jnp.float32),
            dma((STEPS, 8)),
            dma((STEPS, 8)),
            dma((STEPS, 4)),
            dma((STEPS,)),
            dma((STEPS,)),
            dma((STEPS,)),
            dma((STEPS,)),
            dma((STEPS,)),
        ],
        compiler_params=pltpu.CompilerParams(
            collective_id=0, has_side_effects=True, vmem_limit_bytes=60 * 1024 * 1024
        ),
        name="les_steps",
    )(*operands[:4], rotor_weights, *operands[4:])
    outs = pl.pallas_call(
        hand_over,
        out_shape=[jax.ShapeDtypeStruct(flat, jnp.float32)] * 2,
        in_specs=[hbm] * 2,
        out_specs=[hbm] * 2,
        scratch_shapes=[pltpu.VMEM((6, *flat[1:]), jnp.float32), dma((6,)), dma((6,))],
        compiler_params=pltpu.CompilerParams(vmem_limit_bytes=60 * 1024 * 1024),
        name="hand_over",
    )(*outs)
    return tuple(out.reshape(velocity.shape) for out in outs)


def solution(mesh):
    sec_count, tile_count = mesh.shape["sec"], mesh.shape["tile"]
    in_specs = (
        P(None, "sec", "tile", None),
        P(None, "sec", "tile", None),
        P("sec", "tile", None),
        P("sec", "tile", None),
        P(),
    )
    out_specs = (P(None, "sec", "tile", None), P(None, "sec", "tile", None))

    def pick(velocity, *others):
        _, slab_x, tile_y, depth_z = velocity.shape
        owners = depth_z // ROWS
        fits = (
            owners <= sec_count * tile_count
            and owners % sec_count == 0
            and sec_count * (slab_x + ROWS) <= LANES
            and LANES % (slab_x + ROWS) == 0
            and depth_z % LANES == 0
            and slab_x % ROWS == 0
            and tile_y >= 2
            and (tile_y + 2) * (slab_x + ROWS) <= LANES
            and tile_y * tile_count * ROWS <= 512
            and sec_count >= 3
            and tile_count >= 3
        )
        if fits:
            return direct(sec_count, tile_count, velocity, *others)
        return local(velocity, *others)

    return jax.shard_map(pick, mesh=mesh, in_specs=in_specs, out_specs=out_specs, check_vma=False)
```

```python
import functools
import math

import jax
import jax.numpy as jnp
import numpy as np
from jax import lax
from jax.experimental import pallas as pl
from jax.experimental.pallas import tpu as pltpu
from jax.sharding import PartitionSpec as P

STEPS = 2
KINDS = 16
ROWS = 8
LANES = 128
EDGE = 3
MESH = pl.DeviceIdType.MESH

precise = lax.Precision.HIGHEST
time_step = 0.1
fringe_rate = 2.0
smag_coef = 0.04


def extended_2(block, sides, width):
    for axis, dim in sides:
        count = lax.axis_size(axis)
        forward = [(i, i + 1) for i in range(count - 1)]
        forward.append((count - 1, 0))
        backward = [(target, source) for source, target in forward]
        low = lax.ppermute(
            lax.slice_in_dim(block, block.shape[dim] - width, None, axis=dim), axis, forward
        )
        high = lax.ppermute(lax.slice_in_dim(block, 0, width, axis=dim), axis, backward)
        block = jnp.concatenate([low, block, high], axis=dim)
    return block


def from_root(block, axis, owner):
    block = jnp.where(lax.axis_index(axis) == owner, block, jnp.zeros_like(block))
    return lax.psum(block, axis)


def gradients(padded, z_sign):
    centre = padded[:, 1:-1, 1:-1, :]
    grad_x = 0.5 * (padded[:, 2:, 1:-1, :] - padded[:, :-2, 1:-1, :])
    grad_y = 0.5 * (padded[:, 1:-1, 2:, :] - padded[:, 1:-1, :-2, :])
    extended = jnp.concatenate(
        [z_sign * centre[..., :1], centre, z_sign * centre[..., -1:]], axis=-1
    )
    grad_z = 0.5 * (extended[..., 2:] - extended[..., :-2])
    return (grad_x, grad_y, grad_z)


def strain_stress(slopes):

    def strain(first, second):
        return 0.5 * (slopes[second][first] + slopes[first][second])

    strain_xx = strain(0, 0)
    strain_yy = strain(1, 1)
    strain_zz = strain(2, 2)
    strain_xy = strain(0, 1)
    strain_xz = strain(0, 2)
    strain_yz = strain(1, 2)
    squared = strain_xx * strain_xx + strain_yy * strain_yy + strain_zz * strain_zz
    squared = squared + 2.0 * (
        strain_xy * strain_xy + strain_xz * strain_xz + strain_yz * strain_yz
    )
    double = 2.0 * (smag_coef * jnp.sqrt(2.0 * squared + 0.01))
    return jnp.stack(
        [
            double * strain_xx,
            double * strain_yy,
            double * strain_zz,
            double * strain_xy,
            double * strain_xz,
            double * strain_yz,
        ]
    )


def advection(slopes, centre):
    return centre[0:1] * slopes[0] + centre[1:2] * slopes[1] + centre[2:3] * slopes[2]


def stress_force(padded):
    grad_x, grad_y, grad_z = gradients(padded, 0.0)
    return jnp.stack(
        [
            grad_x[0] + grad_y[3] + grad_z[4],
            grad_x[3] + grad_y[1] + grad_z[5],
            grad_x[4] + grad_y[5] + grad_z[2],
        ]
    )


def faces(source):
    return extended_2(source, (("sec", 1), ("tile", 2)), 1)


def sec_turn(blocks):
    return lax.all_to_all(blocks, "sec", split_axis=0, concat_axis=0, tiled=True)


def tile_turn(blocks):
    return lax.all_to_all(blocks, "tile", split_axis=0, concat_axis=0, tiled=True)


def hartley_table(length):
    index_row = jnp.arange(length)
    product = index_row[:, None] * index_row[None, :] % length
    angle = 2.0 * math.pi / length * product.astype(jnp.float32)
    return jnp.cos(angle) + jnp.sin(angle)


def local(velocity, prev_tendency, disk_cells, disk_kind, rotor_weights):
    sec_count = lax.axis_size("sec")
    tile_count = lax.axis_size("tile")
    sec_at = lax.axis_index("sec")
    tile_at = lax.axis_index("tile")
    slab_x = velocity.shape[1]
    tile_y = velocity.shape[2]
    depth_z = velocity.shape[3]
    full_x = slab_x * sec_count
    full_y = tile_y * tile_count
    part_z = depth_z // sec_count
    modes_each = slab_x * depth_z // tile_count
    cell_count = slab_x * tile_y * depth_z
    modes = jnp.arange(depth_z).astype(jnp.float32)[:, None]
    points = jnp.arange(depth_z).astype(jnp.float32)[None, :] + 0.5
    cos_blocks = jnp.cos(math.pi * modes * points / depth_z).reshape(sec_count, part_z, depth_z)
    weight_blocks = jnp.where(jnp.arange(depth_z) == 0, 1.0 / depth_z, 2.0 / depth_z).astype(
        jnp.float32
    )
    weight_blocks = weight_blocks.reshape(sec_count, part_z)
    x_table = hartley_table(full_x)
    y_table = hartley_table(full_y).reshape(full_y, tile_count, tile_y)
    flat_ids = tile_at * modes_each + jnp.arange(modes_each)
    mode_x = flat_ids // part_z
    mode_z = sec_at * part_z + flat_ids % part_z
    mode_y = jnp.arange(full_y)
    sin_x = jnp.sin(2.0 * math.pi * mode_x.astype(jnp.float32) / full_x)
    sin_y = jnp.sin(2.0 * math.pi * mode_y.astype(jnp.float32) / full_y)
    sin_z = jnp.sin(math.pi * mode_z.astype(jnp.float32) / depth_z)
    eigen = -((sin_x * sin_x)[:, None] + (sin_y * sin_y)[None, :] + (sin_z * sin_z)[:, None])
    zero_mode = (
        (mode_x % (full_x // 2) == 0)[:, None]
        & (mode_y % (full_y // 2) == 0)[None, :]
        & (mode_z == 0)[:, None]
    )
    recip = jnp.where(zero_mode, 0.0, 1.0 / jnp.where(zero_mode, 1.0, eigen))
    slab_pos = jnp.sin(math.pi * (jnp.arange(slab_x).astype(jnp.float32) + 0.5) / slab_x)
    lam_x = fringe_rate * (slab_pos * slab_pos)
    flag = (
        (sec_at == 0)
        | (sec_at == sec_count // 2)
        | (sec_at == 3 * sec_count // 4)
        | (sec_at == sec_count - 1)
    ).astype(jnp.float32)
    picked = disk_cells.reshape(-1)
    kinds = disk_kind.reshape(-1)
    live = picked < cell_count
    safe = jnp.minimum(picked, cell_count - 1)
    weight = jnp.sum(
        jnp.where(kinds[:, None] == jnp.arange(KINDS)[None, :], rotor_weights[None, :], 0.0), axis=1
    )
    current = velocity
    tendency_old = prev_tendency
    tendency = prev_tendency
    for step_no in range(STEPS):
        wide = extended_2(current, (("sec", 1), ("tile", 2)), 2)
        wide_slopes = gradients(wide, -1.0)
        push_field = stress_force(strain_stress(wide_slopes))
        slopes = tuple((piece[:, 1:-1, 1:-1, :] for piece in wide_slopes))
        advect = advection(slopes, current)
        target = from_root(current, "sec", sec_count // 2 - 1)
        fringe = flag * lam_x[None, :, None, None] * (target - current)
        sampled = current[0].reshape(-1)[safe]
        push = jnp.where(live, -(weight * sampled * jnp.abs(sampled)), 0.0)
        turbine = (
            jnp.zeros((cell_count,), jnp.float32)
            .at[safe]
            .add(push)
            .reshape(slab_x, tile_y, depth_z)
        )
        empty = jnp.zeros_like(turbine)
        tendency = push_field - advect + jnp.stack([turbine, empty, empty]) + fringe
        interim = current + time_step * (1.5 * tendency - 0.5 * tendency_old)
        grad_x, grad_y, grad_z = gradients(faces(interim), -1.0)
        rhs = grad_x[0] + grad_y[1] + grad_z[2]
        coeffs = jnp.einsum("xyz,bcz->bxyc", rhs, cos_blocks, precision=precise)
        gathered = sec_turn(coeffs).reshape(full_x, tile_y, part_z)
        along_x = jnp.einsum("xyc,kx->kcy", gathered, x_table, precision=precise)
        spread = tile_turn(along_x.reshape(tile_count, modes_each, tile_y))
        along_y = jnp.einsum("sqt,lst->ql", spread, y_table, precision=precise)
        scaled = along_y * recip
        back_y = jnp.einsum("ql,lst->sqt", scaled, y_table, precision=precise) / (full_x * full_y)
        returned = tile_turn(back_y).reshape(full_x, part_z, tile_y)
        back_x = jnp.einsum("kcy,kx->xyc", returned, x_table, precision=precise)
        home = sec_turn(back_x.reshape(sec_count, slab_x, tile_y, part_z))
        pressure = jnp.einsum(
            "bxyc,bcz->xyz", home * weight_blocks[:, None, None, :], cos_blocks, precision=precise
        )
        press_x, press_y, press_z = gradients(faces(pressure[None]), 1.0)
        current = interim - jnp.concatenate([press_x, press_y, press_z], axis=0)
        tendency_old = tendency
    return (current, tendency)


def cas_table(first, second, length):
    angle = 2.0 * np.pi / length * (np.outer(first, second) % length)
    return np.cos(angle) + np.sin(angle)


def halves(table):
    high = table.astype(np.float32).astype(jnp.bfloat16)
    low = (table - high.astype(np.float64)).astype(np.float32).astype(jnp.bfloat16)
    stacked = np.concatenate([high, low], axis=0)
    return np.concatenate(np.split(stacked, stacked.shape[1] // LANES, axis=1), axis=0)


def whole(table, columns):
    count = table.shape[0] * LANES // columns
    parts = [table[i * count : (i + 1) * count] for i in range(columns // LANES)]
    return jnp.concatenate(parts, axis=1)


def tables(sec_count, tile_count, slab_x, tile_y, depth_z):
    full_x, full_y = slab_x * sec_count, tile_y * tile_count
    wide_x = -(-full_x // LANES) * LANES
    planes, block = tile_y + 2, slab_x + ROWS
    z_at = np.arange(depth_z)
    cos_z = np.cos(np.pi / depth_z * np.outer(z_at, z_at + 0.5))
    x_cas = np.zeros((LANES, wide_x))
    x_back = np.zeros((LANES, wide_x))
    for sec in range(sec_count):
        start = sec * slab_x
        cells = np.concatenate([start + np.arange(slab_x), [start - 1, start + slab_x]]) % full_x
        x_cas[sec * block : sec * block + slab_x + 2, :full_x] = cas_table(
            cells, np.arange(full_x), full_x
        )
        cells = np.arange(start - EDGE, start + slab_x + EDGE) % full_x
        x_back[sec * block : sec * block + slab_x + 2 * EDGE, :full_x] = cas_table(
            cells, np.arange(full_x), full_x
        )
    y_blocks = []
    for plane in range(1 - EDGE, planes + EDGE - 1):
        y_at = (np.arange(tile_count) * tile_y + plane - 1) % full_y
        y_blocks.append(np.kron(cas_table(np.arange(full_y), y_at, full_y), np.eye(ROWS)))
    y_cas = np.concatenate(y_blocks[EDGE - 1 : EDGE - 1 + planes], axis=1)
    y_back = np.concatenate(y_blocks, axis=1).T
    k_x, k_y = np.arange(full_x), np.arange(full_y)
    sin_x = np.where(k_x % (full_x // 2) == 0, 0.0, np.sin(2.0 * np.pi * k_x / full_x) ** 2)
    sin_y = np.where(k_y % (full_y // 2) == 0, 0.0, np.sin(2.0 * np.pi * k_y / full_y) ** 2)
    sin_xy = np.ones((full_y * ROWS, wide_x), np.float32)
    sin_xy[:, :full_x] = np.repeat(sin_y, ROWS)[:, None] + sin_x[None, :]
    sin_z = np.sin(np.pi * z_at / depth_z) ** 2
    weight_z = -np.where(z_at == 0, 1.0, 2.0) / (depth_z * full_x * full_y)
    mode_z = np.stack([sin_z, weight_z]).astype(np.float32)
    mode_z = np.ascontiguousarray(np.broadcast_to(mode_z[:, :, None], (2, depth_z, wide_x)))
    lam = fringe_rate * np.sin(np.pi * (np.arange(slab_x) + 0.5) / slab_x) ** 2
    lam = np.ascontiguousarray(np.broadcast_to(lam.astype(np.float32)[:, None], (slab_x, depth_z)))
    return (
        halves(cos_z),
        halves(x_cas),
        halves(x_back.T),
        halves(y_cas),
        halves(y_back),
        sin_xy,
        mode_z,
        lam,
    )


def split(value):
    high = value.astype(jnp.bfloat16)
    return high, (value - high.astype(jnp.float32)).astype(jnp.bfloat16)


def dot(first, second, dims):
    return lax.dot_general(first, second, (dims, ((), ())), preferred_element_type=jnp.float32)


def table_first(table, second, dims):
    count = table.shape[0] // 2
    high, low = split(second)
    both = dot(table, high, dims)
    return both[:count] + (both[count:] + dot(table[:count], low, dims))


def table_second(first, table):
    count, depth = first.shape[0], table.shape[0] // 2
    high, low = split(first)
    both = dot(jnp.concatenate([high, low], axis=0), table[:depth], NN)
    return both[:count] + (both[count:] + dot(high, table[depth:], NN))


NN = ((1,), (0,))
NT = ((1,), (1,))


def slope_z(value, z_sign):
    depth = value.shape[1]
    lane = lax.broadcasted_iota(jnp.int32, value.shape, 1)
    edge = value * z_sign
    above = jnp.where(lane == depth - 1, edge, pltpu.roll(value, depth - 1, 1))
    below = jnp.where(lane == 0, edge, pltpu.roll(value, 1, 1))
    return 0.5 * (above - below)


def slope_x(value, low=None, high=None):
    count = value.shape[0]
    after = pltpu.roll(value, count - 1, 0)
    before = pltpu.roll(value, 1, 0)
    if low is not None:
        row = lax.broadcasted_iota(jnp.int32, value.shape, 0)
        after = jnp.where(row == count - 1, high, after)
        before = jnp.where(row == 0, low, before)
    return 0.5 * (after - before)


def step_kernel(
    sec_count,
    tile_count,
    slab_x,
    tile_y,
    depth_z,
    vel_hbm,
    old_hbm,
    cells_hbm,
    kinds_hbm,
    weights_ref,
    cos_hbm,
    x_hbm,
    xt_hbm,
    y_hbm,
    yt_hbm,
    sin_xy_hbm,
    mode_z_hbm,
    lam_hbm,
    vel_result,
    tend_result,
    wide,
    target,
    share,
    coeffs,
    plane_in,
    wide_out,
    last_out,
    wide_returned,
    last_returned,
    press,
    thrust,
    recip,
    vel_ref,
    old_ref,
    cells_ref,
    kinds_ref,
    cos_ref,
    x_ref,
    xt_ref,
    y_ref,
    yt_ref,
    sin_xy_ref,
    mode_z_ref,
    lam_ref,
    vel_out,
    tend_out,
    load_sem,
    result_sem,
    corner_out,
    corner_in,
    halo_send,
    halo_recv,
    target_send,
    target_recv,
    mode_send,
    mode_recv,
    back_send,
    back_recv,
):
    sec = lax.axis_index("sec")
    tile = lax.axis_index("tile")
    devices = sec_count * tile_count
    me = tile * sec_count + sec
    owners = depth_z // ROWS
    planes = tile_y + 2
    deep = tile_y + 4
    group = tile_count * ROWS
    block = slab_x + ROWS
    root = sec_count // 2 - 1
    fringes = sorted({0, sec_count // 2, 3 * sec_count // 4, sec_count - 1} - {root})
    first_tile = (tile_count - owners // sec_count) // 2
    is_owner = (tile >= first_tile) & (tile < first_tile + owners // sec_count)
    owner_at = (tile - first_tile) * sec_count + sec
    in_fringe = functools.reduce(jnp.logical_or, [sec == which for which in fringes])
    low_sec, high_sec = lax.rem(sec + sec_count - 1, sec_count), lax.rem(sec + 1, sec_count)
    low_tile, high_tile = lax.rem(tile + tile_count - 1, tile_count), lax.rem(tile + 1, tile_count)
    end_x = ROWS + slab_x
    own_x, own_y = slice(ROWS, end_x), slice(2, 2 + tile_y)

    loads = [
        pltpu.make_async_copy(source, held, load_sem.at[place])
        for place, (source, held) in enumerate(
            (
                (vel_hbm, vel_ref),
                (cells_hbm, cells_ref),
                (kinds_hbm, kinds_ref),
                (sin_xy_hbm, sin_xy_ref),
                (mode_z_hbm, mode_z_ref),
                (old_hbm, old_ref),
                (lam_hbm, lam_ref),
                (cos_hbm, cos_ref),
                (y_hbm, y_ref),
                (x_hbm, x_ref),
                (xt_hbm, xt_ref),
                (yt_hbm, yt_ref),
            )
        )
    ]
    for load in loads:
        load.start()

    results = [
        pltpu.make_async_copy(vel_out, vel_result, result_sem.at[0]),
        pltpu.make_async_copy(tend_out, tend_result, result_sem.at[1]),
    ]

    barrier = pltpu.get_barrier_semaphore()

    def greet(ahead, carry):
        other = lax.rem(me + ahead, devices)
        pl.semaphore_signal(
            barrier,
            inc=1,
            device_id=(lax.rem(other, sec_count), lax.div(other, sec_count)),
            device_id_type=MESH,
        )
        return carry

    lax.fori_loop(1, devices, greet, 0)

    share[...] = jnp.zeros_like(share)
    corner_out[...] = jnp.zeros_like(corner_out)
    loads[0].wait()
    for part in range(3):
        for row in range(tile_y):
            wide[0, part, 2 + row, own_x, :] = vel_ref[part, pl.ds(row, slab_x, stride=tile_y), :]

    pl.semaphore_wait(barrier, devices - 1)

    def start_halo(step):
        xs = {
            -1: (low_sec, slice(ROWS, 2 * ROWS), slice(end_x, end_x + ROWS)),
            0: (sec, own_x, own_x),
            1: (high_sec, slice(end_x - ROWS, end_x), slice(0, ROWS)),
        }
        ys = {
            -1: (low_tile, slice(2, 4), slice(2 + tile_y, deep)),
            0: (tile, own_y, own_y),
            1: (high_tile, slice(tile_y, 2 + tile_y), slice(0, 2)),
        }
        copies = []
        for x_way in (0, -1, 1):
            for y_way in (-1, 0, 1):
                if x_way == 0 and y_way == 0:
                    continue
                slot = len(copies)
                to_sec, x_from, x_to = xs[x_way]
                to_tile, y_from, y_to = ys[y_way]
                source = wide.at[step, :, y_from, x_from, :]
                end = wide.at[step, :, y_to, x_to, :]
                if x_way != 0 and y_way != 0:
                    corner = x_way + 1 + (y_way + 1) // 2
                    plane = 2 if y_way < 0 else 1 + tile_y
                    row = ROWS if x_way < 0 else end_x - 1
                    for part in range(3):
                        corner_out[step, corner, part : part + 1, :] = wide[
                            step, part, plane, row : row + 1, :
                        ]
                    source, end = corner_out.at[step, corner], corner_in.at[step, corner]
                copy = pltpu.make_async_remote_copy(
                    src_ref=source,
                    dst_ref=end,
                    send_sem=halo_send.at[step, slot],
                    recv_sem=halo_recv.at[step, slot],
                    device_id=(to_sec, to_tile),
                    device_id_type=MESH,
                )
                copies.append(copy)
        for copy in copies:
            copy.start()
        return copies

    def unpack_corners(step):
        for x_way in (-1, 1):
            for y_way in (-1, 1):
                corner = x_way + 1 + (y_way + 1) // 2
                plane = 2 + tile_y if y_way < 0 else 1
                row = end_x if x_way < 0 else ROWS - 1
                for part in range(3):
                    wide[step, part, plane, row : row + 1, :] = corner_in[
                        step, corner, part : part + 1, :
                    ]

    def start_target(step):
        sends = [
            pltpu.make_async_remote_copy(
                src_ref=wide.at[step, :, own_y, own_x, :],
                dst_ref=target.at[step],
                send_sem=target_send.at[step, place],
                recv_sem=target_recv.at[step],
                device_id=(which, tile),
                device_id_type=MESH,
            )
            for place, which in enumerate(fringes)
        ]

        @pl.when(sec == root)
        def _():
            for send in sends:
                send.start()

        return sends

    halos = {0: start_halo(0)}
    targets = {0: start_target(0)}

    for load in loads[1:5]:
        load.wait()
    cells = cells_ref[...]
    kinds = kinds_ref[...]
    weight = jnp.zeros(cells.shape, jnp.float32)
    for kind in range(KINDS):
        weight = jnp.where(kinds == kind, weights_ref[kind], weight)
    weight = jnp.where(cells < slab_x * tile_y * depth_z, weight, 0.0)
    column = lax.div(cells, depth_z)
    row_of = lax.rem(column, tile_y) * slab_x + lax.div(column, tile_y)
    slots = cells.shape[1]
    hit_row = lax.broadcasted_iota(jnp.int32, (tile_y * slab_x, slots), 0) == row_of
    hit_z = lax.broadcasted_iota(jnp.int32, (depth_z, slots), 0) == lax.rem(cells, depth_z)
    hit_z = hit_z.astype(jnp.float32).astype(jnp.bfloat16)
    rest = jnp.where(hit_row, weight, 0.0)
    summed = jnp.zeros((tile_y * slab_x, depth_z), jnp.float32)
    for _ in range(3):
        piece, rest_next = rest.astype(jnp.bfloat16), None
        rest_next = rest - piece.astype(jnp.float32)
        summed = summed + lax.dot_general(
            piece, hit_z, (NT, ((), ())), preferred_element_type=jnp.float32
        )
        rest = rest_next
    thrust[...] = summed

    @pl.when(is_owner)
    def _():
        rows = pl.ds(pl.multiple_of(owner_at * ROWS, ROWS), ROWS)
        full_y = tile_y * tile_count
        sum_sin = sin_xy_ref[...] + jnp.concatenate([mode_z_ref[0, rows, :]] * full_y, axis=0)
        scale = jnp.concatenate([mode_z_ref[1, rows, :]] * full_y, axis=0)
        zero_mode = sum_sin == 0.0
        recip[...] = jnp.where(zero_mode, 0.0, scale / jnp.where(zero_mode, 1.0, sum_sin))

    for load in loads[5:]:
        load.wait()
    old = [
        [old_ref[part, pl.ds(row, slab_x, stride=tile_y), :] for row in range(tile_y)]
        for part in range(3)
    ]

    for step in range(STEPS):
        if step == 0:
            for copy in halos[0]:
                copy.wait_recv()
            unpack_corners(0)

        centre, stress, advect = {}, {}, {}
        for plane in range(1, deep - 1):
            here = [wide[step, part, plane] for part in range(3)]
            d_x = [slope_x(value) for value in here]
            d_y = [
                0.5 * (wide[step, part, plane + 1] - wide[step, part, plane - 1])
                for part in range(3)
            ]
            d_z = [slope_z(value, -1.0) for value in here]
            s_xx, s_yy, s_zz = d_x[0], d_y[1], d_z[2]
            s_xy = 0.5 * (d_x[1] + d_y[0])
            s_xz = 0.5 * (d_x[2] + d_z[0])
            s_yz = 0.5 * (d_y[2] + d_z[1])
            squared = s_xx * s_xx + s_yy * s_yy + s_zz * s_zz
            squared = squared + 2.0 * (s_xy * s_xy + s_xz * s_xz + s_yz * s_yz)
            double = (2.0 * smag_coef) * jnp.sqrt(2.0 * squared + 0.01)
            stress[plane] = [double * s for s in (s_xx, s_yy, s_zz, s_xy, s_xz, s_yz)]
            centre[plane] = here
            advect[plane] = [
                here[0] * d_x[part] + here[1] * d_y[part] + here[2] * d_z[part]
                for part in range(3)
            ]

        @pl.when(in_fringe)
        def _(step=step):
            pltpu.make_async_copy(target.at[step], target.at[step], target_recv.at[step]).wait()

        @pl.when(jnp.logical_not(in_fringe))
        def _(step=step):
            target[step] = wide[step, :, own_y, own_x, :]

        interim, tendency = [], []
        for row in range(tile_y):
            plane = 2 + row
            xx, yy, zz, xy, xz, yz = stress[plane]
            before, after = stress[plane - 1], stress[plane + 1]
            push = [
                slope_x(xx) + 0.5 * (after[3] - before[3]) + slope_z(xz, 0.0),
                slope_x(xy) + 0.5 * (after[1] - before[1]) + slope_z(yz, 0.0),
                slope_x(xz) + 0.5 * (after[5] - before[5]) + slope_z(zz, 0.0),
            ]
            lam = lam_ref[...]
            tend, mid = [], []
            for part in range(3):
                here = centre[plane][part][own_x]
                total = (push[part] - advect[plane][part])[own_x]
                if part == 0:
                    force = thrust[row * slab_x : (row + 1) * slab_x, :]
                    total = total - force * here * jnp.abs(here)
                total = total + lam * (target[step, part, row] - here)
                tend.append(total)
                mid.append(here + time_step * (1.5 * total - 0.5 * old[part][row]))
                if step == STEPS - 1:
                    tend_out[part, pl.ds(row, slab_x, stride=tile_y), :] = total
            tendency.append(tend)
            interim.append(mid)
        if step == STEPS - 1:
            results[1].start()
        old = [[tendency[row][part] for row in range(tile_y)] for part in range(3)]

        share[0:slab_x, :] = 0.5 * interim[0][1]
        last = (planes - 1) * block
        share[last : last + slab_x, :] = -0.5 * interim[tile_y - 1][1]
        for row in range(tile_y):
            along_x, _, along_z = interim[row]
            total = slope_x(along_x, 0.0, 0.0) + slope_z(along_z, -1.0)
            if row + 1 < tile_y:
                total = total + 0.5 * interim[row + 1][1]
            if row > 0:
                total = total - 0.5 * interim[row - 1][1]
            start = (row + 1) * block
            edge = start + slab_x
            share[start:edge, :] = total
            share[edge : edge + 1, :] = 0.5 * along_x[0:1]
            share[edge + 1 : edge + 2, :] = -0.5 * along_x[slab_x - 1 : slab_x]
        coeffs[step] = table_first(cos_ref[...], share[...], NT)

        my_rows = pl.ds(pl.multiple_of(tile * ROWS, ROWS), ROWS)

        first_owner = jnp.where(is_owner, owner_at, lax.rem(me, owners))

        def modes_to(owner, step=step):
            flat = owner + first_tile * sec_count
            return pltpu.make_async_remote_copy(
                src_ref=coeffs.at[step, pl.ds(pl.multiple_of(owner * ROWS, ROWS), ROWS), :],
                dst_ref=plane_in.at[step, sec, my_rows, :],
                send_sem=mode_send.at[step],
                recv_sem=mode_recv.at[step],
                device_id=(lax.rem(flat, sec_count), lax.div(flat, sec_count)),
                device_id_type=MESH,
            )

        def send_modes(ahead, carry):
            modes_to(lax.rem(first_owner + ahead, owners)).start()
            return carry

        lax.fori_loop(1, owners, send_modes, 0, unroll=True)

        @pl.when(is_owner)
        def _(step=step):
            rows = pl.ds(pl.multiple_of(owner_at * ROWS, ROWS), ROWS)
            pltpu.make_async_copy(
                coeffs.at[step, rows, :], plane_in.at[step, sec, my_rows, :], mode_recv.at[step]
            ).start()

        @pl.when(jnp.logical_not(is_owner))
        def _(first_owner=first_owner):
            modes_to(first_owner).start()

        final = step == STEPS - 1
        if not final:
            for part in range(3):
                for row in range(tile_y):
                    wide[step + 1, part, 2 + row, own_x, :] = interim[row][part]
            halos[step + 1] = start_halo(step + 1)
        reach = 1 if final else EDGE
        plane_out, returned = (last_out, last_returned) if final else (wide_out, wide_returned)
        per_tile = LANES // block
        back_planes = tile_y + 2 * reach

        @pl.when(is_owner)
        def _(step=step):
            pltpu.make_async_copy(
                plane_in.at[step], plane_in.at[step], mode_recv.at[step]
            ).wait()
            lane_block = lax.broadcasted_iota(jnp.int32, (group, LANES), 1) // block
            arrived = [plane_in[step, part] for part in range(sec_count)]
            blocks = []
            for plane in range(planes):
                piece = pltpu.roll(arrived[0], -plane * block % LANES, 1)
                for part in range(1, sec_count):
                    other = pltpu.roll(arrived[part], (part - plane) * block % LANES, 1)
                    piece = jnp.where(lane_block == part, other, piece)
                blocks.append(piece)
            stacked = jnp.concatenate(blocks, axis=0)
            modes = table_second(table_first(whole(y_ref[...], planes * group), stacked, NN), whole(x_ref[...], recip.shape[1])) * recip[...]
            skip = (EDGE - reach) * group
            kept = back_planes * group
            back_table = yt_ref[...]
            half = back_table.shape[0] // 2
            back_table = jnp.concatenate(
                [back_table[skip : skip + kept], back_table[half + skip : half + skip + kept]], axis=0
            )
            back_x = table_second(modes, whole(xt_ref[...], LANES))
            spread = table_first(back_table, back_x, NN)
            for part in range(sec_count):
                for first in range(0, back_planes, per_tile):
                    piece = None
                    for place in range(min(per_tile, back_planes - first)):
                        start = (first + place) * group
                        other = spread[start : start + group]
                        other = pltpu.roll(other, (place - part) * block % LANES, 1)
                        piece = other if piece is None else jnp.where(lane_block == place, other, piece)
                    lanes = slice(first // per_tile * LANES, (first // per_tile + 1) * LANES)
                    plane_out[part, :, lanes] = piece
            rows = pl.ds(pl.multiple_of(owner_at * ROWS, ROWS), ROWS)

            pltpu.make_async_copy(
                plane_out.at[sec, my_rows, :], returned.at[rows, :], back_recv.at[step]
            ).start()

            def send_back(ahead, carry):
                other = lax.rem(me + ahead, devices)
                to_sec, to_tile = lax.rem(other, sec_count), lax.div(other, sec_count)
                pltpu.make_async_remote_copy(
                    src_ref=plane_out.at[
                        to_sec, pl.ds(pl.multiple_of(to_tile * ROWS, ROWS), ROWS), :
                    ],
                    dst_ref=returned.at[rows, :],
                    send_sem=back_send.at[step],
                    recv_sem=back_recv.at[step],
                    device_id=(to_sec, to_tile),
                    device_id_type=MESH,
                ).start()
                return carry

            lax.fori_loop(1, devices, send_back, 0, unroll=True)

        pltpu.make_async_copy(returned, returned, back_recv.at[step]).wait()
        columns = returned[...]
        columns = jnp.concatenate(
            [columns[:, i : i + LANES].T for i in range(0, columns.shape[1], LANES)], axis=0
        )
        press[0 : columns.shape[0], :] = table_second(columns, cos_ref[...])

        def press_slopes(start, count):
            here = press[start : start + count, :]
            above = press[start + block : start + block + count, :]
            below = press[start - block : start - block + count, :]
            return here, 0.5 * (above - below), slope_z(here, 1.0)

        if final:
            for row in range(tile_y):
                start = (row + 1) * block + EDGE
                here, along_y, along_z = press_slopes(start, slab_x)
                low = press[start - 1 : start, :]
                high = press[start + slab_x : start + slab_x + 1, :]
                slopes = [slope_x(here, low, high), along_y, along_z]
                for part in range(3):
                    vel_out[part, pl.ds(row, slab_x, stride=tile_y), :] = (
                        interim[row][part] - slopes[part]
                    )
        else:
            for copy in halos[step + 1]:
                copy.wait()
            unpack_corners(step + 1)
            span = slice(ROWS - EDGE, ROWS - EDGE + block)
            for plane in sorted(range(deep), key=lambda at: not 2 <= at < 2 + tile_y):
                if plane == 0:
                    targets[step + 1] = start_target(step + 1)
                here, along_y, along_z = press_slopes((plane + 1) * block, block)
                slopes = [slope_x(here), along_y, along_z]
                for part in range(3):
                    wide[step + 1, part, plane, span, :] = (
                        wide[step + 1, part, plane, span, :] - slopes[part]
                    )

    results[0].start()
    for copy in halos[0]:
        copy.wait_send()
    for step, sends in targets.items():
        plane_out = last_out if step == STEPS - 1 else wide_out

        @pl.when(sec == root)
        def _(sends=sends):
            for send in sends:
                send.wait_send()

        @pl.when(is_owner)
        def _(step=step, plane_out=plane_out):
            most = coeffs.at[step, pl.ds(0, (owners - 1) * ROWS), :]
            pltpu.make_async_copy(most, most, mode_send.at[step]).wait()
            some = plane_out.at[pl.ds(0, sec_count - 1)]
            pltpu.make_async_copy(some, some, back_send.at[step]).wait()
            last = plane_out.at[sec_count - 1, pl.ds(0, group - ROWS), :]
            pltpu.make_async_copy(last, last, back_send.at[step]).wait()

        @pl.when(jnp.logical_not(is_owner))
        def _(step=step):
            pltpu.make_async_copy(coeffs.at[step], coeffs.at[step], mode_send.at[step]).wait()

    for result in results:
        result.wait()


def hand_over(vel_from, tend_from, vel_to, tend_to, held, in_sems, out_sems):
    pieces = []
    for place, (source, end) in enumerate(((vel_from, vel_to), (tend_from, tend_to))):
        for part in range(3):
            slot = 3 * place + part
            pieces.append(
                (
                    pltpu.make_async_copy(source.at[part], held.at[slot], in_sems.at[slot]),
                    pltpu.make_async_copy(held.at[slot], end.at[part], out_sems.at[slot]),
                )
            )
    for arrive, _ in pieces:
        arrive.start()
    for arrive, leave in pieces:
        arrive.wait()
        leave.start()
    for _, leave in pieces:
        leave.wait()


def direct(sec_count, tile_count, velocity, prev_tendency, disk_cells, disk_kind, rotor_weights):
    _, slab_x, tile_y, depth_z = velocity.shape
    constants = [
        jnp.asarray(table) for table in tables(sec_count, tile_count, slab_x, tile_y, depth_z)
    ]
    wide_x = constants[5].shape[1]
    full_y = tile_y * tile_count
    group = tile_count * ROWS
    wide_lanes = (tile_y + 2 * EDGE) * (slab_x + ROWS)
    wide_lanes = -(-wide_lanes // LANES) * LANES
    flat = (3, slab_x * tile_y, depth_z)
    hbm = pl.BlockSpec(memory_space=pltpu.HBM)
    operands = [
        velocity.reshape(flat),
        prev_tendency.reshape(flat),
        disk_cells.reshape(1, -1),
        disk_kind.reshape(1, -1),
        *constants,
    ]
    smem = pl.BlockSpec(memory_space=pltpu.SMEM)
    dma = pltpu.SemaphoreType.DMA
    outs = pl.pallas_call(
        functools.partial(step_kernel, sec_count, tile_count, slab_x, tile_y, depth_z),
        out_shape=[jax.ShapeDtypeStruct(flat, jnp.float32)] * 2,
        in_specs=[hbm] * 4 + [smem] + [hbm] * len(constants),
        out_specs=[hbm] * 2,
        scratch_shapes=[
            pltpu.VMEM((STEPS, 3, tile_y + 4, slab_x + 2 * ROWS, depth_z), jnp.float32),
            pltpu.VMEM((STEPS, 3, tile_y, slab_x, depth_z), jnp.float32),
            pltpu.VMEM((LANES, depth_z), jnp.float32),
            pltpu.VMEM((STEPS, depth_z, LANES), jnp.float32),
            pltpu.VMEM((STEPS, sec_count, group, LANES), jnp.float32),
            pltpu.VMEM((sec_count, group, wide_lanes), jnp.float32),
            pltpu.VMEM((sec_count, group, LANES), jnp.float32),
            pltpu.VMEM((depth_z, wide_lanes), jnp.float32),
            pltpu.VMEM((depth_z, LANES), jnp.float32),
            pltpu.VMEM((wide_lanes, depth_z), jnp.float32),
            pltpu.VMEM((tile_y * slab_x, depth_z), jnp.float32),
            pltpu.VMEM((full_y * ROWS, wide_x), jnp.float32),
            *[pltpu.VMEM(operand.shape, operand.dtype) for operand in operands],
            pltpu.VMEM(flat, jnp.float32),
            pltpu.VMEM(flat, jnp.float32),
            dma((len(operands),)),
            dma((2,)),
            pltpu.VMEM((STEPS, 4, ROWS, depth_z), jnp.float32),
            pltpu.VMEM((STEPS, 4, ROWS, depth_z), jnp.float32),
            dma((STEPS, 8)),
            dma((STEPS, 8)),
            dma((STEPS, 4)),
            dma((STEPS,)),
            dma((STEPS,)),
            dma((STEPS,)),
            dma((STEPS,)),
            dma((STEPS,)),
        ],
        compiler_params=pltpu.CompilerParams(
            collective_id=0, has_side_effects=True, vmem_limit_bytes=60 * 1024 * 1024
        ),
        name="les_steps",
    )(*operands[:4], rotor_weights, *operands[4:])
    outs = pl.pallas_call(
        hand_over,
        out_shape=[jax.ShapeDtypeStruct(flat, jnp.float32)] * 2,
        in_specs=[hbm] * 2,
        out_specs=[hbm] * 2,
        scratch_shapes=[pltpu.VMEM((6, *flat[1:]), jnp.float32), dma((6,)), dma((6,))],
        compiler_params=pltpu.CompilerParams(vmem_limit_bytes=60 * 1024 * 1024),
        name="hand_over",
    )(*outs)
    return tuple(out.reshape(velocity.shape) for out in outs)


def solution(mesh):
    sec_count, tile_count = mesh.shape["sec"], mesh.shape["tile"]
    in_specs = (
        P(None, "sec", "tile", None),
        P(None, "sec", "tile", None),
        P("sec", "tile", None),
        P("sec", "tile", None),
        P(),
    )
    out_specs = (P(None, "sec", "tile", None), P(None, "sec", "tile", None))

    def pick(velocity, *others):
        _, slab_x, tile_y, depth_z = velocity.shape
        owners = depth_z // ROWS
        fits = (
            owners <= sec_count * tile_count
            and owners % sec_count == 0
            and sec_count * (slab_x + ROWS) <= LANES
            and LANES % (slab_x + ROWS) == 0
            and depth_z % LANES == 0
            and slab_x % ROWS == 0
            and tile_y >= 2
            and (tile_y + 2) * (slab_x + ROWS) <= LANES
            and tile_y * tile_count * ROWS <= 512
            and sec_count >= 3
            and tile_count >= 3
        )
        if fits:
            return direct(sec_count, tile_count, velocity, *others)
        return local(velocity, *others)

    return jax.shard_map(pick, mesh=mesh, in_specs=in_specs, out_specs=out_specs, check_vma=False)
```
